32 devices in a mesh: wide: 32 (over z, y, x, core), narrow: 1.
Axes of the slice: x: 2, y: 2, z: 4, core: 2. Of those that a mesh axis runs over, the one named last changes fastest.
Arguments:
- tokens: bfloat16 [768, 4096], P('wide', 'narrow'), may hold values from -6 to 6
- grad_out: bfloat16 [768, 4096], P('wide', 'narrow'), may hold values from -1.1953125 to 1.1953125
- expert_ids: int32 [768, 8], P('wide'), may hold values from 0 to 31, all different within a row; in each aligned block of 24 rows (0 to 23, 24 to 47, ...) at most 12 rows name the same one
- route_weights: bfloat16 [768, 8], P('wide'), may hold values from 0.049804688 to 1
- w_gate: bfloat16 [32, 4096, 1536], P('wide', None, 'narrow'), may hold values from -0.09375 to 0.09375
- w_up: bfloat16 [32, 4096, 1536], P('wide', None, 'narrow'), may hold values from -0.09375 to 0.09375
- w_down: bfloat16 [32, 1536, 4096], P('wide', 'narrow'), may hold values from -0.15625 to 0.15625
Outputs:
- grad_tokens: bfloat16 [768, 4096], P('wide', 'narrow')
- grad_route: bfloat16 [768, 8], P('wide')
- grad_down: bfloat16 [32, 1536, 4096], P('wide', 'narrow')
The draws below stay inside these ranges and needn't reach their ends.
Inputs may be any that keep to these rules, and one draw needn't show every extreme that they name: `expert_ids`: each row names 8 different experts. In each aligned block of 24 rows (the tokens of one index of wide) no expert is named by more than 12 rows, a bound that some block reaches.
All inputs are finite; a program needn't handle non-finite values.
Results may differ from the reference program's by a relative error of at most 0.019.
Values may be sent and summed in bfloat16 or wider, within the bound.
No kernel may reach another device: no remote copies, remote signals or barrier semaphores. Data moves between devices by JAX's collectives and lax.ppermute only.
A program may use at most 128 MiB of HBM per device.

```python
import math
import jax
import jax.numpy as jnp
import numpy as np
from jax import lax

D = 4096
FF = 1536
TOP = 8
TOK_COL = 24
EXPERTS = 32
CAP = 12
TOKENS = 768
N_WIDE = 32
N_NARROW = 1


def levels(rng, shape, pieces, smallest, largest):
    def one(dim, blocks):
        draws = jax.random.uniform(jax.random.fold_in(jax.random.fold_in(rng, 6), dim), (blocks,), jnp.float32, smallest / len(pieces), largest / len(pieces))
        return jnp.repeat(jnp.exp(draws), shape[dim] // blocks).reshape((-1,) + (1,) * (len(shape) - dim - 1))

    factor_of = one(*pieces[0])
    for cut in pieces[1:]:
        factor_of = factor_of * one(*cut)
    return factor_of


def routed_block(stream_key, own, number, rows, count, top, reach, lean):
    sequence = jax.random.permutation(stream_key, count)
    heavy_load, common = load_shares(count, rows * top, reach, lean, True), load_shares(count, rows * top, reach, lean, False)
    places = jnp.arange(count)

    def named(tallies, offset_by):
        used = int((tallies > 0).sum())
        fixed = max(1, used // 4)
        passed = fixed + (places - fixed + offset_by * (used - fixed)) % max(1, count - fixed)
        return jnp.zeros((count,), jnp.int32).at[sequence[jnp.where(places < fixed, places, passed)]].set(jnp.asarray(tallies, jnp.int32))

    tallies = jnp.where(number % 4 == 0, named(heavy_load, number // 4), named(common, number - number // 4 - 1))
    mixed = jax.random.permutation(jax.random.fold_in(own, 3), count)
    giver, receiver = mixed[0:count // 2 * 2:2], mixed[1:count // 2 * 2:2]
    room = jnp.minimum(tallies[giver] - 1, reach - tallies[receiver]) // 2
    room = jnp.where((giver == sequence[0]) | (receiver == sequence[0]) | (tallies[receiver] == 0), 0, jnp.maximum(room, 0))
    passed = jax.random.randint(jax.random.fold_in(own, 4), (count // 2,), 0, 1 << 20) % (room + 1)
    tallies = tallies.at[giver].add(-passed).at[receiver].add(passed)
    items = jnp.searchsorted(jnp.cumsum(tallies), jnp.arange(rows * top), side="right").astype(jnp.int32)
    table = items.reshape(top, rows).T
    table = table[jax.random.permutation(jax.random.fold_in(own, 1), rows)]
    offset_by = jax.random.randint(jax.random.fold_in(own, 2), (rows, 1), 0, top)
    return jnp.take_along_axis(table, (jnp.arange(top)[None, :] + offset_by) % top, axis=1)


def load_shares(amount, total, limit, lean, full):
    loads = [(1 << 20) // math.isqrt(rank ** lean) + 1 for rank in range(1, amount + 1)]
    largest = limit if full else min(limit, max(-(-total // amount), total * loads[0] // sum(loads)))
    least = 1 if total - largest >= amount - 1 else 0
    given, spare = [largest] + [least] * (amount - 1), total - largest - least * (amount - 1)
    while spare > 0:
        free = [i for i in range(1, amount) if given[i] < largest] or [i for i in range(1, amount) if given[i] < limit]
        pool, budget = sum([loads[i] for i in free]), spare
        for i in free:
            more = min(limit - given[i], max(1, budget * loads[i] // pool), spare)
            given[i] = given[i] + more
            spare = spare - more
    return np.array(given)


def noise(rng, dims, scale, most, pieces=(), kind=jnp.bfloat16):
    result = jax.random.normal(rng, dims, jnp.float32) * scale
    if len(pieces) > 0:
        result = levels(rng, dims, pieces, -0.22, 0.18) * result
    return jnp.clip(result, min=-most, max=most).astype(kind)


def setup_inputs(seed: int = 0) -> dict:
    keys = jax.random.split(jax.random.key(seed), 8)
    tokens = noise(keys[0], (TOKENS, D), 1.0, 6.0, ((0, 32),))
    grad_out = noise(keys[1], (TOKENS, D), 0.2, 1.1953125, ((0, 32),))
    expert_ids_keys = jax.random.split(jax.random.fold_in(keys[2], 1), TOKENS // TOK_COL)
    expert_ids_turns = jax.random.permutation(jax.random.fold_in(keys[2], 3), TOKENS // TOK_COL)
    expert_ids = jax.vmap(lambda own, number: routed_block(jax.random.fold_in(keys[2], 2), own, number, TOK_COL, EXPERTS, TOP, CAP, 2))(expert_ids_keys, expert_ids_turns).reshape((TOKENS, TOP))
    route_weights = jnp.clip(jnp.exp(math.log(1.0) - 2.9996462 * jax.random.uniform(keys[3], (TOKENS, TOP), jnp.float32) ** levels(keys[3], (TOKENS, TOP), ((0, 32),), -0.2, 0.2)), 0.049804688, 1.0).astype(jnp.bfloat16)
    w_gate = noise(keys[4], (EXPERTS, D, FF), D ** -0.5, 0.09375, ((0, 32),))
    w_up = noise(keys[5], (EXPERTS, D, FF), D ** -0.5, 0.09375, ((0, 32),))
    w_down = noise(keys[6], (EXPERTS, FF, D), FF ** -0.5, 0.15625, ((0, 32),))
    return dict(tokens=tokens, grad_out=grad_out, expert_ids=expert_ids, route_weights=route_weights, w_gate=w_gate, w_up=w_up, w_down=w_down)


def silu_parts(gate_pre):
    sigmoid_val = jax.nn.sigmoid(gate_pre)
    return gate_pre * sigmoid_val, sigmoid_val * (1.0 + gate_pre * (1.0 - sigmoid_val))


def reference(tokens, grad_out, expert_ids, route_weights, w_gate, w_up, w_down):
    slot_rows = N_WIDE * CAP
    copies = TOK_COL * TOP
    blocks = expert_ids.reshape(N_WIDE, copies)
    onehot = (blocks[:, :, None] == jnp.arange(EXPERTS, dtype=jnp.int32)[None, None, :]).astype(jnp.int32)
    before = jnp.cumsum(onehot, axis=1) - onehot
    rank_in = jnp.sum(before * onehot, axis=2)
    column = jnp.arange(N_WIDE, dtype=jnp.int32)[:, None]
    position = (blocks * slot_rows + column * CAP + rank_in).reshape(-1).astype(jnp.int32)
    copy_index = jnp.arange(N_WIDE * copies, dtype=jnp.int32)
    token_index = (copy_index // TOP).astype(jnp.int32)
    token_table = jnp.zeros((EXPERTS * slot_rows,), jnp.int32).at[position].set(token_index).reshape(EXPERTS, slot_rows)
    copy_table = jnp.zeros((EXPERTS * slot_rows,), jnp.int32).at[position].set(copy_index).reshape(EXPERTS, slot_rows)
    filled = jnp.zeros((EXPERTS * slot_rows,), jnp.float32).at[position].set(1.0).reshape(EXPERTS, slot_rows)
    weight_flat = route_weights.reshape(-1).astype(jnp.float32)
    width = FF // N_NARROW

    def expert(operands):
        gate_w, up_w, down_w, token_idx, copy_idx, filled_row = operands
        keep_row = filled_row[:, None] > 0
        token_rows = jnp.where(keep_row, tokens[token_idx], jnp.zeros((), tokens.dtype))
        grad_rows = jnp.where(keep_row, grad_out[token_idx], jnp.zeros((), grad_out.dtype))
        gain_rows = weight_flat[copy_idx] * filled_row
        gate_pre = jnp.dot(token_rows, gate_w, preferred_element_type=jnp.float32)
        up_pre = jnp.dot(token_rows, up_w, preferred_element_type=jnp.float32)
        active, gate_slope = silu_parts(gate_pre)
        hidden = (active * up_pre).astype(jnp.bfloat16)
        back_proj = jnp.dot(grad_rows, down_w.T, preferred_element_type=jnp.float32)
        d_hidden = gain_rows[:, None] * back_proj
        d_gate = (d_hidden * up_pre * gate_slope).astype(jnp.bfloat16)
        d_up = (d_hidden * active).astype(jnp.bfloat16)
        scaled = (gain_rows[:, None] * grad_rows.astype(jnp.float32)).astype(jnp.bfloat16)
        grad_down = jnp.dot(hidden.T, scaled, preferred_element_type=jnp.float32).astype(jnp.bfloat16)
        input_total = jnp.zeros((slot_rows, D), jnp.float32)
        route_total = jnp.zeros((slot_rows,), jnp.float32)
        for block_id in range(N_NARROW):
            low = block_id * width
            high = low + width
            part_in = jnp.dot(d_gate[:, low:high], gate_w[:, low:high].T, preferred_element_type=jnp.float32)
            part_in = part_in + jnp.dot(d_up[:, low:high], up_w[:, low:high].T, preferred_element_type=jnp.float32)
            input_total = input_total + lax.optimization_barrier(part_in.astype(jnp.bfloat16)).astype(jnp.float32)
            part_route = jnp.sum(hidden[:, low:high].astype(jnp.float32) * back_proj[:, low:high], axis=1)
            route_total = route_total + lax.optimization_barrier(part_route.astype(jnp.bfloat16)).astype(jnp.float32)
        return grad_down, input_total.astype(jnp.bfloat16), route_total.astype(jnp.bfloat16)

    grad_down, input_rows, route_rows = lax.map(
        expert, (w_gate, w_up, w_down, token_table, copy_table, filled))
    flat_filled = filled.reshape(-1)
    grad_tokens = jnp.zeros((TOKENS, D), jnp.float32).at[token_table.reshape(-1)].add(
        input_rows.reshape(-1, D).astype(jnp.float32) * flat_filled[:, None])
    grad_route = jnp.zeros((TOKENS * TOP,), jnp.float32).at[copy_table.reshape(-1)].add(
        route_rows.reshape(-1).astype(jnp.float32) * flat_filled)
    return (grad_tokens.astype(jnp.bfloat16), grad_route.reshape(TOKENS, TOP).astype(jnp.bfloat16),
            grad_down)
```

```python
import jax
import jax.numpy as jnp
from jax import lax
from jax.sharding import PartitionSpec as P


def silu_parts(gate_pre):
    sigmoid_val = jax.nn.sigmoid(gate_pre)
    return (gate_pre * sigmoid_val, sigmoid_val * (1.0 + gate_pre * (1.0 - sigmoid_val)))


def dot(a, b, dims):
    return lax.dot_general(a, b, ((dims[0], dims[1]), ((), ())), preferred_element_type=jnp.float32)


def body(tokens, grad_out, expert_ids, route_weights, w_gate, w_up, w_down):
    wide_count = lax.axis_size("wide")
    local_experts = w_gate.shape[0]
    experts_all = local_experts * wide_count
    tok_count, top_count = expert_ids.shape
    capacity = min(tok_count, 2 * tok_count * top_count // experts_all)
    rows = wide_count * capacity
    tok_all = wide_count * tok_count
    bf16, f32 = jnp.bfloat16, jnp.float32
    all_ids = lax.all_gather(expert_ids, "wide", axis=0, tiled=True)
    all_weights = lax.all_gather(route_weights, "wide", axis=0, tiled=True)
    all_tokens = lax.all_gather(tokens, "wide", axis=0, tiled=True)
    all_grads = lax.all_gather(grad_out, "wide", axis=0, tiled=True)
    first = lax.axis_index("wide") * local_experts
    dense = 0
    route_cols = []
    grad_downs = []
    for j in range(local_experts):
        match = all_ids == first + j
        chosen = jnp.any(match, axis=1)
        gain = jnp.sum(jnp.where(match, all_weights.astype(f32), 0.0), axis=1)
        rank = jnp.cumsum(chosen.astype(jnp.int32)) - 1
        slot = jnp.where(chosen, rank, -1)
        place = slot[None, :] == jnp.arange(rows, dtype=jnp.int32)[:, None]
        row_gain = jnp.sum(jnp.where(place, gain[None, :], 0.0), axis=1, keepdims=True)
        place = place.astype(bf16)
        x = dot(place, all_tokens, ((1,), (0,))).astype(bf16)
        g = dot(place, all_grads, ((1,), (0,))).astype(bf16)
        x = lax.all_gather(x, "narrow", axis=1, tiled=True)
        g = lax.all_gather(g, "narrow", axis=1, tiled=True)
        gate_pre = dot(x, w_gate[j], ((1,), (0,)))
        up_pre = dot(x, w_up[j], ((1,), (0,)))
        active, slope = silu_parts(gate_pre)
        hidden = (active * up_pre).astype(bf16)
        back = dot(g, w_down[j], ((1,), (1,)))
        d_hidden = row_gain * back
        d_gate = (d_hidden * up_pre * slope).astype(bf16)
        d_up = (d_hidden * active).astype(bf16)
        scaled = (row_gain * g).astype(bf16)
        grad_downs.append(dot(hidden, scaled, ((0,), (0,))).astype(bf16))
        part = dot(d_gate, w_gate[j], ((1,), (1,))) + dot(d_up, w_up[j], ((1,), (1,)))
        part = lax.psum_scatter(part.astype(bf16), "narrow", scatter_dimension=1, tiled=True)
        dense = dense + dot(place, part, ((0,), (0,)))
        route = jnp.sum(hidden.astype(f32) * back, axis=1).astype(bf16)
        route = lax.psum(route.astype(f32), "narrow")
        route_cols.append(dot(place, route.astype(bf16)[:, None], ((0,), (0,))))
    grad_tokens = lax.psum_scatter(dense.astype(bf16), "wide", scatter_dimension=0, tiled=True)
    cols = jnp.concatenate(route_cols, axis=1).astype(bf16).reshape(wide_count, tok_count, local_experts)
    cols = lax.all_to_all(cols, "wide", split_axis=0, concat_axis=0, tiled=True)
    by_expert = jnp.swapaxes(cols, 0, 1).reshape(tok_count, experts_all)
    pick = expert_ids[:, :, None] == jnp.arange(experts_all, dtype=jnp.int32)[None, None, :]
    grad_route = jnp.sum(jnp.where(pick, by_expert.astype(f32)[:, None, :], 0.0), axis=2)
    return (grad_tokens, grad_route.astype(bf16), jnp.stack(grad_downs))


def solution(mesh):
    in_specs = (
        P("wide", "narrow"),
        P("wide", "narrow"),
        P("wide", None),
        P("wide", None),
        P("wide", None, "narrow"),
        P("wide", None, "narrow"),
        P("wide", "narrow", None),
    )
    out_specs = (P("wide", "narrow"), P("wide", None), P("wide", "narrow", None))
    return jax.shard_map(body, mesh=mesh, in_specs=in_specs, out_specs=out_specs, check_vma=False)
```

```python
import jax
import jax.numpy as jnp
from jax import lax
from jax.sharding import PartitionSpec as P

LANES = 128


def silu_parts(gate_pre):
    sigmoid_val = jax.nn.sigmoid(gate_pre)
    return (gate_pre * sigmoid_val, sigmoid_val * (1.0 + gate_pre * (1.0 - sigmoid_val)))


def dot(a, b, dims):
    return lax.dot_general(a, b, ((dims[0], dims[1]), ((), ())), preferred_element_type=jnp.float32)


def add(*terms):
    total = terms[0].astype(jnp.float32)
    for term in terms[1:]:
        total = total + term.astype(jnp.float32)
    return total.astype(terms[0].dtype)


class Routes:
    def __init__(self):
        self.count = lax.axis_size("wide")
        self.depth = self.count // 8
        self.z = lax.axis_index("wide") // 8

    def flip(self, value, bit):
        return lax.ppermute(value, "wide", [(i, i ^ bit) for i in range(self.count)])

    def core(self, value):
        return self.flip(value, 1)

    def x(self, value):
        return self.flip(value, 2)

    def y(self, value):
        return self.flip(value, 4)

    def up(self, value):
        return lax.ppermute(value, "wide", [(i, i + 8) for i in range(self.count - 8)])

    def down(self, value):
        return lax.ppermute(value, "wide", [(i + 8, i) for i in range(self.count - 8)])

    def chain_gather(self, value):
        ups, downs = [value], [value]
        for _ in range(self.depth - 1):
            ups.append(self.up(ups[-1]))
            downs.append(self.down(downs[-1]))
        return [value] + [
            jnp.where(self.z >= k, ups[k], downs[self.depth - k]) for k in range(1, self.depth)
        ]

    def chain_scatter(self, blocks):
        n = self.depth
        rise = fall = None
        for t in range(1, n):
            mine_up = jnp.where(self.z < t, blocks[t], jnp.zeros_like(blocks[t]))
            mine_down = jnp.where(self.z >= n - t, blocks[n - t], jnp.zeros_like(blocks[t]))
            rise = self.up(mine_up if rise is None else add(mine_up, rise))
            fall = self.down(mine_down if fall is None else add(mine_down, fall))
        return add(blocks[0], rise, fall) if n > 1 else blocks[0]


def gather_rows(routes, shard):
    cut = 2 * (shard.shape[0] // 3)
    first = jnp.concatenate(routes.chain_gather(shard[:cut]), axis=0)
    half = first.shape[0] // 2
    by_x, by_y = routes.x(first), routes.y(first)
    pieces = [first, by_x, by_y, routes.x(by_y[:half]), routes.y(by_x[half:])]
    last = shard[cut:]
    last = jnp.concatenate([last, routes.x(last)], axis=0)
    last = jnp.concatenate([last, routes.y(last)], axis=0)
    pieces += routes.chain_gather(last)
    return pieces + [routes.core(piece) for piece in pieces]


def scatter_rows(routes, dense, tok_count):
    half_rows = dense.shape[0] // 2
    mine = add(dense[:half_rows], routes.core(dense[half_rows:]))
    cut = 2 * (tok_count // 3)
    n = routes.depth
    size = n * cut
    half = size // 2
    first, by_x, by_y = mine[:size], mine[size : 2 * size], mine[2 * size : 3 * size]
    far = mine[3 * size : 4 * size]
    got_y = routes.x(far[:half])
    got_x = routes.y(far[half:])
    by_y = jnp.concatenate([add(by_y[:half], got_y), by_y[half:]], axis=0)
    by_x = jnp.concatenate([by_x[:half], add(by_x[half:], got_x)], axis=0)
    first = add(first, routes.x(by_x), routes.y(by_y))
    head = routes.chain_scatter([first[k * cut : (k + 1) * cut] for k in range(n)])
    rest = mine[4 * size :]
    step = rest.shape[0] // n
    last = routes.chain_scatter([rest[k * step : (k + 1) * step] for k in range(n)])
    last = add(last[: step // 2], routes.y(last[step // 2 :]))
    last = add(last[: step // 4], routes.x(last[step // 4 :]))
    return jnp.concatenate([head, last], axis=0)


def body(tokens, grad_out, expert_ids, route_weights, w_gate, w_up, w_down):
    routes = Routes()
    wide_count = routes.count
    local_experts = w_gate.shape[0]
    experts_all = local_experts * wide_count
    tok_count, top_count = expert_ids.shape
    capacity = min(tok_count, 2 * tok_count * top_count // experts_all)
    rows = wide_count * capacity
    cols = tokens.shape[1]
    bf16, f32 = jnp.bfloat16, jnp.float32
    pad = -2 * top_count % LANES
    meta = jnp.concatenate(
        [expert_ids.astype(bf16), route_weights, jnp.zeros((tok_count, pad), bf16)], axis=1
    )
    pieces = gather_rows(routes, jnp.concatenate([tokens, meta], axis=1))
    all_tokens = jnp.concatenate([piece[:, :cols] for piece in pieces], axis=0)
    all_meta = jnp.concatenate([piece[:, cols:] for piece in pieces], axis=0)
    all_grads = jnp.concatenate(gather_rows(routes, grad_out), axis=0)
    all_ids = all_meta[:, :top_count].astype(jnp.int32)
    all_weights = all_meta[:, top_count : 2 * top_count].astype(f32)
    first = lax.axis_index("wide") * local_experts
    dense = 0
    route_cols = 0
    grad_downs = []
    expert_cols = experts_all + -experts_all % LANES
    for j in range(local_experts):
        match = all_ids == first + j
        chosen = jnp.any(match, axis=1)
        gain = jnp.sum(jnp.where(match, all_weights, 0.0), axis=1)
        rank = jnp.cumsum(chosen.astype(jnp.int32)) - 1
        slot = jnp.where(chosen, rank, -1)
        place = slot[None, :] == jnp.arange(rows, dtype=jnp.int32)[:, None]
        row_gain = jnp.sum(jnp.where(place, gain[None, :], 0.0), axis=1, keepdims=True)
        place = place.astype(bf16)
        x = dot(place, all_tokens, ((1,), (0,))).astype(bf16)
        g = dot(place, all_grads, ((1,), (0,))).astype(bf16)
        x = lax.all_gather(x, "narrow", axis=1, tiled=True)
        g = lax.all_gather(g, "narrow", axis=1, tiled=True)
        gate_pre = dot(x, w_gate[j], ((1,), (0,)))
        up_pre = dot(x, w_up[j], ((1,), (0,)))
        active, slope = silu_parts(gate_pre)
        hidden = (active * up_pre).astype(bf16)
        back = dot(g, w_down[j], ((1,), (1,)))
        d_hidden = row_gain * back
        d_gate = (d_hidden * up_pre * slope).astype(bf16)
        d_up = (d_hidden * active).astype(bf16)
        scaled = (row_gain * g).astype(bf16)
        grad_downs.append(dot(hidden, scaled, ((0,), (0,))).astype(bf16))
        part = dot(d_gate, w_gate[j], ((1,), (1,))) + dot(d_up, w_up[j], ((1,), (1,)))
        part = lax.psum_scatter(part.astype(bf16), "narrow", scatter_dimension=1, tiled=True)
        route = jnp.sum(hidden.astype(f32) * back, axis=1).astype(bf16)
        route = lax.psum(route.astype(f32), "narrow").astype(bf16)
        at = (jnp.arange(expert_cols, dtype=jnp.int32) == first + j)[None, :]
        route = jnp.where(at, route[:, None], jnp.zeros((), bf16))
        dense = dense + dot(place, jnp.concatenate([part, route], axis=1), ((0,), (0,)))
    mine = scatter_rows(routes, dense.astype(bf16), tok_count)
    pick = expert_ids[:, :, None] == jnp.arange(experts_all, dtype=jnp.int32)[None, None, :]
    by_expert = mine[:, cols : cols + experts_all].astype(f32)
    grad_route = jnp.sum(jnp.where(pick, by_expert[:, None, :], 0.0), axis=2)
    return (mine[:, :cols], grad_route.astype(bf16), jnp.stack(grad_downs))


def solution(mesh):
    in_specs = (
        P("wide", "narrow"),
        P("wide", "narrow"),
        P("wide", None),
        P("wide", None),
        P("wide", None, "narrow"),
        P("wide", None, "narrow"),
        P("wide", "narrow", None),
    )
    out_specs = (P("wide", "narrow"), P("wide", None), P("wide", "narrow", None))
    return jax.shard_map(body, mesh=mesh, in_specs=in_specs, out_specs=out_specs, check_vma=False)
```

```python
import jax
import jax.numpy as jnp
from jax import lax
from jax.sharding import PartitionSpec as P

LANES = 128


def silu_parts(gate_pre):
    sigmoid_val = jax.nn.sigmoid(gate_pre)
    return (gate_pre * sigmoid_val, sigmoid_val * (1.0 + gate_pre * (1.0 - sigmoid_val)))


def dot(a, b, dims):
    return lax.dot_general(a, b, ((dims[0], dims[1]), ((), ())), preferred_element_type=jnp.float32)


def groups(count):
    along = [[i + 8 * k for k in range(count // 8)] for i in range(8)]
    square = [[8 * k + 2 * q + c for q in range(4)] for k in range(count // 8) for c in range(2)]
    pair = [[2 * i, 2 * i + 1] for i in range(count // 2)]
    return [along, square, pair]


def gather_rows(shard):
    for group in groups(lax.axis_size("wide")):
        shard = lax.all_gather(shard, "wide", axis=0, tiled=True, axis_index_groups=group)
    return shard


def scatter_rows(dense):
    for group in reversed(groups(lax.axis_size("wide"))):
        dense = lax.psum_scatter(
            dense, "wide", scatter_dimension=0, tiled=True, axis_index_groups=group
        )
    return dense


def body(tokens, grad_out, expert_ids, route_weights, w_gate, w_up, w_down):
    wide_count = lax.axis_size("wide")
    local_experts = w_gate.shape[0]
    experts_all = local_experts * wide_count
    tok_count, top_count = expert_ids.shape
    capacity = min(tok_count, 2 * tok_count * top_count // experts_all)
    rows = wide_count * capacity
    cols = tokens.shape[1]
    bf16, f32 = jnp.bfloat16, jnp.float32
    pad = -2 * top_count % LANES
    meta = jnp.concatenate(
        [expert_ids.astype(bf16), route_weights, jnp.zeros((tok_count, pad), bf16)], axis=1
    )
    arrived = gather_rows(jnp.concatenate([tokens, meta], axis=1))
    all_tokens, all_meta = arrived[:, :cols], arrived[:, cols:]
    all_grads = gather_rows(grad_out)
    all_ids = all_meta[:, :top_count].astype(jnp.int32)
    all_weights = all_meta[:, top_count : 2 * top_count].astype(f32)
    first = lax.axis_index("wide") * local_experts
    dense = 0
    route_cols = 0
    grad_downs = []
    expert_cols = experts_all + -experts_all % LANES
    for j in range(local_experts):
        match = all_ids == first + j
        chosen = jnp.any(match, axis=1)
        gain = jnp.sum(jnp.where(match, all_weights, 0.0), axis=1)
        rank = jnp.cumsum(chosen.astype(jnp.int32)) - 1
        slot = jnp.where(chosen, rank, -1)
        place = slot[None, :] == jnp.arange(rows, dtype=jnp.int32)[:, None]
        row_gain = jnp.sum(jnp.where(place, gain[None, :], 0.0), axis=1, keepdims=True)
        place = place.astype(bf16)
        x = dot(place, all_tokens, ((1,), (0,))).astype(bf16)
        g = dot(place, all_grads, ((1,), (0,))).astype(bf16)
        x = lax.all_gather(x, "narrow", axis=1, tiled=True)
        g = lax.all_gather(g, "narrow", axis=1, tiled=True)
        gate_pre = dot(x, w_gate[j], ((1,), (0,)))
        up_pre = dot(x, w_up[j], ((1,), (0,)))
        active, slope = silu_parts(gate_pre)
        hidden = (active * up_pre).astype(bf16)
        back = dot(g, w_down[j], ((1,), (1,)))
        d_hidden = row_gain * back
        d_gate = (d_hidden * up_pre * slope).astype(bf16)
        d_up = (d_hidden * active).astype(bf16)
        scaled = (row_gain * g).astype(bf16)
        grad_downs.append(dot(hidden, scaled, ((0,), (0,))).astype(bf16))
        part = dot(d_gate, w_gate[j], ((1,), (1,))) + dot(d_up, w_up[j], ((1,), (1,)))
        part = lax.psum_scatter(part.astype(bf16), "narrow", scatter_dimension=1, tiled=True)
        route = jnp.sum(hidden.astype(f32) * back, axis=1).astype(bf16)
        route = lax.psum(route.astype(f32), "narrow").astype(bf16)
        at = (jnp.arange(expert_cols, dtype=jnp.int32) == first + j)[None, :]
        route = jnp.where(at, route[:, None], jnp.zeros((), bf16))
        dense = dense + dot(place, jnp.concatenate([part, route], axis=1), ((0,), (0,)))
    mine = scatter_rows(dense.astype(bf16))
    pick = expert_ids[:, :, None] == jnp.arange(experts_all, dtype=jnp.int32)[None, None, :]
    by_expert = mine[:, cols : cols + experts_all].astype(f32)
    grad_route = jnp.sum(jnp.where(pick, by_expert[:, None, :], 0.0), axis=2)
    return (mine[:, :cols], grad_route.astype(bf16), jnp.stack(grad_downs))


def solution(mesh):
    in_specs = (
        P("wide", "narrow"),
        P("wide", "narrow"),
        P("wide", None),
        P("wide", None),
        P("wide", None, "narrow"),
        P("wide", None, "narrow"),
        P("wide", "narrow", None),
    )
    out_specs = (P("wide", "narrow"), P("wide", None), P("wide", "narrow", None))
    return jax.shard_map(body, mesh=mesh, in_specs=in_specs, out_specs=out_specs, check_vma=False)
```

```python
import functools

import jax
import jax.numpy as jnp
from jax import lax
from jax.experimental import pallas as pl
from jax.experimental.pallas import tpu as pltpu
from jax.sharding import PartitionSpec as P

LANES = 128
CHUNKS = 2
bf16, f32 = jnp.bfloat16, jnp.float32


def dot(a, b, dims):
    return lax.dot_general(a, b, ((dims[0], dims[1]), ((), ())), preferred_element_type=f32)


def add(*terms):
    total = terms[0].astype(f32)
    for term in terms[1:]:
        total = total + term.astype(f32)
    return total.astype(terms[0].dtype)


def tile(size, most):
    fits = [t for t in range(LANES, min(size, most) + 1, LANES) if size % t == 0]
    return fits[-1] if fits else size


def call(kernel, flops, moved, **kwargs):
    return pl.pallas_call(
        kernel,
        compiler_params=pltpu.CompilerParams(vmem_limit_bytes=52 * 1024 * 1024),
        cost_estimate=pl.CostEstimate(flops=flops, bytes_accessed=moved, transcendentals=0),
        **kwargs,
    )


def whole(*shape):
    return pl.BlockSpec(shape, lambda i: (0,) * len(shape))


CORE, X, Y, Z = 1, 2, 4, 8


def flip(value, mask):
    count = lax.axis_size("wide")
    return lax.ppermute(value, "wide", [(i, i ^ mask) for i in range(count)])


def depth():
    return lax.axis_size("wide") // Z


def gather_z(shard):
    return jnp.concatenate([shard] + [flip(shard, Z * k) for k in range(1, depth())], axis=0)


def gather_square(first):
    by_x, by_y = flip(first, X), flip(first, Y)
    half = first.shape[0] // 2
    return [first, by_x, by_y, flip(by_y[:half], X), flip(by_x[half:], Y)]


def gather_core(pieces):
    return pieces + [flip(piece, CORE) for piece in pieces]


def offsets():
    return [Z * k + m + c for c in (0, CORE) for m in (0, X, Y, X | Y) for k in range(depth())]


def scatter_rows(own, other):
    mine = add(own, flip(other, CORE))
    size = mine.shape[0] // 4
    parts = [mine[k * size : (k + 1) * size] for k in range(4)]
    first = add(parts[0], flip(parts[1], X), flip(parts[2], Y), flip(parts[3], X | Y))
    step = size // depth()
    blocks = [first[k * step : (k + 1) * step] for k in range(depth())]
    return add(blocks[0], *[flip(blocks[k], Z * k) for k in range(1, depth())])


def pick_kernel(sizes, block, slot_ref, *refs):
    pieces, (out_ref, held, place, sems) = refs[: len(sizes)], refs[len(sizes) :]
    step = pl.program_id(0)
    starts = [sum(sizes[:k]) for k in range(len(sizes))]

    def copy(at, k):
        return pltpu.make_async_copy(
            pieces[k].at[:, pl.ds(pl.multiple_of(at * block, LANES), block)],
            held.at[at, pl.ds(starts[k], sizes[k]), :],
            sems.at[at, k],
        )

    @pl.when(step == 0)
    def _():
        @pl.loop(0, pl.num_programs(0))
        def _(at):
            for k in range(len(sizes)):
                copy(at, k).start()

        rows = lax.broadcasted_iota(jnp.int32, place.shape, 0)
        place[...] = jnp.where(rows == slot_ref[...], 1.0, 0.0).astype(bf16)

    for k in range(len(sizes)):
        copy(step, k).wait()
    out_ref[...] = dot(place[...], held[step], ((1,), (0,))).astype(bf16)


def pick_rows(slot, pieces, rows, cols):
    sizes = [piece.shape[0] for piece in pieces]
    total = sum(sizes)
    block = tile(cols, 512)
    steps = cols // block
    return call(
        functools.partial(pick_kernel, sizes, block),
        2 * rows * total * cols,
        2 * (rows + total) * cols,
        grid=(steps,),
        in_specs=[whole(1, total)] + [pl.BlockSpec(memory_space=pl.ANY)] * len(pieces),
        out_specs=pl.BlockSpec((rows, block), lambda i: (0, i)),
        out_shape=jax.ShapeDtypeStruct((rows, cols), bf16),
        scratch_shapes=[
            pltpu.VMEM((steps, total, block), bf16),
            pltpu.VMEM((rows, total), bf16),
            pltpu.SemaphoreType.DMA((steps, len(sizes))),
        ],
    )(slot.reshape(1, total), *pieces)


def forward_kernel(x_ref, gate_ref, up_ref, hidden_ref, active_ref, pull_ref):
    gate_pre = dot(x_ref[...], gate_ref[...], ((1,), (0,)))
    up_pre = dot(x_ref[...], up_ref[...], ((1,), (0,)))
    sig = jax.nn.sigmoid(gate_pre)
    active = gate_pre * sig
    hidden_ref[...] = (active * up_pre).astype(bf16)
    active_ref[...] = active.astype(bf16)
    pull_ref[...] = (up_pre * (sig * (1.0 + gate_pre * (1.0 - sig)))).astype(bf16)


def forward(x, w_gate, w_up):
    rows, width = x.shape
    units = w_gate.shape[1]
    block = tile(units, 256)
    weight = pl.BlockSpec((width, block), lambda i: (0, i))
    unit = pl.BlockSpec((rows, block), lambda i: (0, i))
    shape = jax.ShapeDtypeStruct((rows, units), bf16)
    return call(
        forward_kernel,
        4 * rows * width * units,
        4 * width * units,
        grid=(units // block,),
        in_specs=[whole(rows, width), weight, weight],
        out_specs=[unit] * 3,
        out_shape=[shape] * 3,
    )(x, w_gate, w_up)


def back_kernel(g_ref, gain_ref, down_ref, hidden_ref, active_ref, pull_ref, d_gate_ref, d_up_ref, route_ref):
    back = dot(g_ref[...], down_ref[...], ((1,), (1,)))
    d_hidden = gain_ref[...] * back
    d_gate_ref[...] = (d_hidden * pull_ref[...].astype(f32)).astype(bf16)
    d_up_ref[...] = (d_hidden * active_ref[...].astype(f32)).astype(bf16)

    @pl.when(pl.program_id(0) == 0)
    def _():
        route_ref[...] = jnp.zeros_like(route_ref)

    route_ref[...] += jnp.sum(hidden_ref[...].astype(f32) * back, axis=1, keepdims=True)


def back_project(g, gain, w_down, hidden, active, pull):
    rows, width = g.shape
    units = w_down.shape[0]
    block = tile(units, 256)
    unit = pl.BlockSpec((rows, block), lambda i: (0, i))
    shape = jax.ShapeDtypeStruct((rows, units), bf16)
    return call(
        back_kernel,
        2 * rows * width * units,
        2 * width * units,
        grid=(units // block,),
        in_specs=[
            whole(rows, width),
            whole(rows, 1),
            pl.BlockSpec((block, width), lambda i: (i, 0)),
            unit,
            unit,
            unit,
        ],
        out_specs=[unit, unit, whole(rows, 1)],
        out_shape=[shape, shape, jax.ShapeDtypeStruct((rows, 1), f32)],
    )(g, gain, w_down, hidden, active, pull)


def token_kernel(spread, d_gate_ref, d_up_ref, slot_ref, gate_ref, up_ref, *outs):
    part = dot(d_gate_ref[...], gate_ref[...], ((1,), (1,)))
    part = (part + dot(d_up_ref[...], up_ref[...], ((1,), (1,)))).astype(bf16)
    if not spread:
        outs[0][...] = part
        return
    half = slot_ref.shape[0] // 2
    rows = part.shape[0]
    for k in range(2):
        slot = slot_ref[k * half : (k + 1) * half, :]
        lanes = lax.broadcasted_iota(jnp.int32, (half, rows), 1)
        place = jnp.where(lanes == slot, 1.0, 0.0).astype(bf16)
        outs[k][...] = dot(place, part, ((1,), (0,))).astype(bf16)


def token_grad(d_gate, d_up, slot, w_gate, w_up, chunk, chunks, spread):
    rows, units = d_gate.shape
    width = w_gate.shape[0] // chunks
    total = slot.shape[0]
    block = tile(width, 512)
    first = chunk * (width // block)
    weight = pl.BlockSpec((block, units), lambda i: (first + i, 0))
    out_rows = [total // 2] * 2 if spread else [rows]
    return call(
        functools.partial(token_kernel, spread),
        4 * rows * width * units + 2 * rows * width * total * spread,
        4 * width * units + 2 * total * width,
        grid=(width // block,),
        in_specs=[whole(rows, units), whole(rows, units), whole(total, 1), weight, weight],
        out_specs=[pl.BlockSpec((n, block), lambda i: (0, i)) for n in out_rows],
        out_shape=[jax.ShapeDtypeStruct((n, width), bf16) for n in out_rows],
    )(d_gate, d_up, slot.reshape(total, 1), w_gate, w_up)


def down_kernel(g_ref, gain_ref, hidden_ref, out_ref, scaled):
    @pl.when(pl.program_id(0) == 0)
    def _():
        scaled[...] = (gain_ref[...] * g_ref[...].astype(f32)).astype(bf16)

    out_ref[...] = dot(hidden_ref[...], scaled[...], ((0,), (0,))).astype(bf16)


def down_grad(g, gain, hidden):
    rows, width = g.shape
    units = hidden.shape[1]
    block = tile(units, 256)
    return call(
        down_kernel,
        2 * rows * width * units,
        2 * width * units,
        grid=(units // block,),
        in_specs=[whole(rows, width), whole(rows, 1), pl.BlockSpec((rows, block), lambda i: (0, i))],
        out_specs=pl.BlockSpec((block, width), lambda i: (i, 0)),
        out_shape=jax.ShapeDtypeStruct((units, width), bf16),
        scratch_shapes=[pltpu.VMEM((rows, width), bf16)],
    )(g, gain, hidden)


def body(tokens, grad_out, expert_ids, route_weights, w_gate, w_up, w_down):
    wide_count = lax.axis_size("wide")
    narrow_count = lax.axis_size("narrow")
    local_experts = w_gate.shape[0]
    experts_all = local_experts * wide_count
    tok_count, top_count = expert_ids.shape
    capacity = min(tok_count, 2 * tok_count * top_count // experts_all)
    rows = wide_count * capacity
    total = wide_count * tok_count
    cols = tokens.shape[1]
    me = lax.axis_index("wide")
    pad = -2 * top_count % LANES
    meta = jnp.concatenate(
        [expert_ids.astype(bf16), route_weights, jnp.zeros((tok_count, pad), bf16)], axis=1
    )
    first_t = gather_z(jnp.concatenate([tokens, meta], axis=1))
    first_t, grad_out = lax.optimization_barrier((first_t, grad_out))
    square_t = gather_square(first_t)
    first_g = gather_z(grad_out)
    pieces_t = gather_core(square_t)
    pieces_g = gather_core(gather_square(first_g))
    all_meta = jnp.concatenate([piece[:, cols : cols + 2 * top_count] for piece in pieces_t], axis=0)
    all_ids = all_meta[:, :top_count].astype(jnp.int32)
    all_weights = all_meta[:, top_count:].astype(f32)
    first = me * local_experts
    fused = narrow_count == 1 and local_experts == 1
    chunks = CHUNKS if fused else 1
    dense = [[0, 0] for _ in range(chunks)]
    route_cols = []
    grad_downs = []
    for j in range(local_experts):
        match = all_ids == first + j
        chosen = jnp.any(match, axis=1)
        gain = jnp.sum(jnp.where(match, all_weights, 0.0), axis=1)
        rank = jnp.cumsum(chosen.astype(jnp.int32)) - 1
        slot = jnp.where(chosen, rank, -1)
        place = slot[None, :] == jnp.arange(rows, dtype=jnp.int32)[:, None]
        row_gain = jnp.sum(jnp.where(place, gain[None, :], 0.0), axis=1, keepdims=True)
        x = pick_rows(slot, pieces_t, rows, cols)
        x = lax.all_gather(x, "narrow", axis=1, tiled=True)
        hidden, active, pull = forward(x, w_gate[j], w_up[j])
        g = pick_rows(slot, pieces_g, rows, cols)
        g = lax.all_gather(g, "narrow", axis=1, tiled=True)
        d_gate, d_up, route = back_project(g, row_gain, w_down[j], hidden, active, pull)
        for c in range(chunks):
            part = token_grad(d_gate, d_up, slot, w_gate[j], w_up[j], c, chunks, fused)
            if fused:
                dense[c] = part
            else:
                part = lax.psum_scatter(part[0], "narrow", scatter_dimension=1, tiled=True)
                part = dot(place.astype(bf16), part, ((0,), (0,)))
                dense[c] = [dense[c][0] + part[: total // 2], dense[c][1] + part[total // 2 :]]
        route = lax.psum(route.astype(bf16).astype(f32), "narrow")
        route_cols.append(jnp.sum(jnp.where(place, route, 0.0), axis=0))
        grad_downs.append(down_grad(g, row_gain, hidden))
    shares = [scatter_rows(own.astype(bf16), other.astype(bf16)) for own, other in dense]
    grad_tokens = jnp.concatenate(shares, axis=1)
    came_from = me ^ jnp.array(offsets(), jnp.int32)
    order = (jnp.arange(wide_count, dtype=jnp.int32)[:, None] == came_from[None, :]).astype(bf16)
    route = jnp.stack(route_cols, axis=1).astype(bf16).reshape(wide_count, tok_count * local_experts)
    route = dot(order, route, ((1,), (0,))).astype(bf16)
    route = lax.all_to_all(
        route.reshape(wide_count, tok_count, local_experts), "wide", split_axis=0, concat_axis=0, tiled=True
    )
    by_expert = jnp.swapaxes(route, 0, 1).reshape(tok_count, experts_all)
    pick = expert_ids[:, :, None] == jnp.arange(experts_all, dtype=jnp.int32)[None, None, :]
    grad_route = jnp.sum(jnp.where(pick, by_expert.astype(f32)[:, None, :], 0.0), axis=2)
    return (grad_tokens, grad_route.astype(bf16), jnp.stack(grad_downs))


def solution(mesh):
    in_specs = (
        P("wide", "narrow"),
        P("wide", "narrow"),
        P("wide", None),
        P("wide", None),
        P("wide", None, "narrow"),
        P("wide", None, "narrow"),
        P("wide", "narrow", None),
    )
    out_specs = (P("wide", "narrow"), P("wide", None), P("wide", "narrow", None))
    return jax.shard_map(body, mesh=mesh, in_specs=in_specs, out_specs=out_specs, check_vma=False)
```

```python
import functools

import jax
import jax.numpy as jnp
from jax import lax
from jax.experimental import pallas as pl
from jax.experimental.pallas import tpu as pltpu
from jax.sharding import PartitionSpec as P

LANES = 128
CHUNKS = 2
bf16, f32 = jnp.bfloat16, jnp.float32


def dot(a, b, dims):
    return lax.dot_general(a, b, ((dims[0], dims[1]), ((), ())), preferred_element_type=f32)


def add(*terms):
    total = terms[0].astype(f32)
    for term in terms[1:]:
        total = total + term.astype(f32)
    return total.astype(terms[0].dtype)


def tile(size, most):
    fits = [t for t in range(LANES, min(size, most) + 1, LANES) if size % t == 0]
    return fits[-1] if fits else size


def call(kernel, flops, moved, **kwargs):
    return pl.pallas_call(
        kernel,
        compiler_params=pltpu.CompilerParams(vmem_limit_bytes=52 * 1024 * 1024),
        cost_estimate=pl.CostEstimate(flops=flops, bytes_accessed=moved, transcendentals=0),
        **kwargs,
    )


def whole(*shape):
    return pl.BlockSpec(shape, lambda i: (0,) * len(shape))


CORE, X, Y, Z = 1, 2, 4, 8


def flip(value, mask):
    count = lax.axis_size("wide")
    return lax.ppermute(value, "wide", [(i, i ^ mask) for i in range(count)])


def after(value, *deps):
    return lax.optimization_barrier((value, *deps))[0]


def depth():
    return lax.axis_size("wide") // Z


def gather_z(shard):
    return jnp.concatenate([shard] + [flip(shard, Z * k) for k in range(1, depth())], axis=0)


def gather_sides(first):
    return flip(first, X), flip(first, Y)


def gather_far(by_x, by_y):
    half = by_x.shape[0] // 2
    return [flip(by_y[:half], X), flip(by_x[half:], Y)]


def gather_core(pieces):
    return pieces + [flip(piece, CORE) for piece in pieces]


def offsets():
    return [Z * k + m + c for c in (0, CORE) for m in (0, X, Y, X | Y) for k in range(depth())]


def quarters(mine):
    size = mine.shape[0] // 4
    return [mine[k * size : (k + 1) * size] for k in range(4)]


def scatter_far(mine):
    first, by_x, by_y, far = quarters(mine)
    half = far.shape[0] // 2
    to_y, to_x = flip(far[:half], X), flip(far[half:], Y)
    by_y = jnp.concatenate([add(by_y[:half], to_y), by_y[half:]], axis=0)
    by_x = jnp.concatenate([by_x[:half], add(by_x[half:], to_x)], axis=0)
    return first, by_x, by_y


def scatter_sides(first, by_x, by_y):
    return add(first, flip(by_x, X), flip(by_y, Y))


def scatter_z(first):
    step = first.shape[0] // depth()
    blocks = [first[k * step : (k + 1) * step] for k in range(depth())]
    return add(blocks[0], *[flip(blocks[k], Z * k) for k in range(1, depth())])


def meta_kernel(sizes, cols, *refs):
    pieces, (out_ref, sems) = refs[: len(sizes)], refs[len(sizes) :]
    starts = [sum(sizes[:k]) for k in range(len(sizes))]
    copies = [
        pltpu.make_async_copy(
            pieces[k].at[:, pl.ds(cols, LANES)], out_ref.at[pl.ds(starts[k], sizes[k]), :], sems.at[k]
        )
        for k in range(len(sizes))
    ]
    for copy in copies:
        copy.start()
    for copy in copies:
        copy.wait()


def gather_meta(pieces, cols):
    sizes = [piece.shape[0] for piece in pieces]
    return call(
        functools.partial(meta_kernel, sizes, cols),
        0,
        4 * sum(sizes) * LANES,
        grid=(1,),
        in_specs=[pl.BlockSpec(memory_space=pl.ANY)] * len(pieces),
        out_specs=whole(sum(sizes), LANES),
        out_shape=jax.ShapeDtypeStruct((sum(sizes), LANES), bf16),
        scratch_shapes=[pltpu.SemaphoreType.DMA((len(sizes),))],
    )(*pieces)


def pick_kernel(sizes, block, slot_ref, *refs):
    pieces, (out_ref, held, place, sems) = refs[: len(sizes)], refs[len(sizes) :]
    step = pl.program_id(0)
    starts = [sum(sizes[:k]) for k in range(len(sizes))]

    def copy(at, k):
        return pltpu.make_async_copy(
            pieces[k].at[:, pl.ds(pl.multiple_of(at * block, LANES), block)],
            held.at[at, pl.ds(starts[k], sizes[k]), :],
            sems.at[at, k],
        )

    @pl.when(step == 0)
    def _():
        @pl.loop(0, pl.num_programs(0))
        def _(at):
            for k in range(len(sizes)):
                copy(at, k).start()

        rows = lax.broadcasted_iota(jnp.int32, place.shape, 0)
        place[...] = jnp.where(rows == slot_ref[...], 1.0, 0.0).astype(bf16)

    for k in range(len(sizes)):
        copy(step, k).wait()
    out_ref[...] = dot(place[...], held[step], ((1,), (0,))).astype(bf16)


def pick_rows(slot, pieces, rows, cols):
    sizes = [piece.shape[0] for piece in pieces]
    total = sum(sizes)
    block = tile(cols, 512)
    steps = cols // block
    return call(
        functools.partial(pick_kernel, sizes, block),
        2 * rows * total * cols,
        2 * (rows + total) * cols,
        grid=(steps,),
        in_specs=[whole(1, total)] + [pl.BlockSpec(memory_space=pl.ANY)] * len(pieces),
        out_specs=pl.BlockSpec((rows, block), lambda i: (0, i)),
        out_shape=jax.ShapeDtypeStruct((rows, cols), bf16),
        scratch_shapes=[
            pltpu.VMEM((steps, total, block), bf16),
            pltpu.VMEM((rows, total), bf16),
            pltpu.SemaphoreType.DMA((steps, len(sizes))),
        ],
    )(slot.reshape(1, total), *pieces)


def forward_kernel(x_ref, gate_ref, up_ref, hidden_ref, active_ref, pull_ref):
    gate_pre = dot(x_ref[...], gate_ref[...], ((1,), (0,)))
    up_pre = dot(x_ref[...], up_ref[...], ((1,), (0,)))
    sig = jax.nn.sigmoid(gate_pre)
    active = gate_pre * sig
    hidden_ref[...] = (active * up_pre).astype(bf16)
    active_ref[...] = active.astype(bf16)
    pull_ref[...] = (up_pre * (sig * (1.0 + gate_pre * (1.0 - sig)))).astype(bf16)


def forward(x, w_gate, w_up, part, parts):
    rows, width = x.shape
    units = w_gate.shape[1] // parts
    block = tile(units, 256)
    first = part * (units // block)
    weight = pl.BlockSpec((width, block), lambda i: (0, first + i))
    unit = pl.BlockSpec((rows, block), lambda i: (0, i))
    shape = jax.ShapeDtypeStruct((rows, units), bf16)
    return call(
        forward_kernel,
        4 * rows * width * units,
        4 * width * units,
        grid=(units // block,),
        in_specs=[whole(rows, width), weight, weight],
        out_specs=[unit] * 3,
        out_shape=[shape] * 3,
    )(x, w_gate, w_up)


def back_kernel(steps, g_ref, gain_ref, down_ref, *refs):
    parts, (d_gate_ref, d_up_ref, route_ref) = refs[:-3], refs[-3:]
    step = pl.program_id(0)
    back = dot(g_ref[...], down_ref[...], ((1,), (1,)))
    d_hidden = gain_ref[...] * back

    @pl.when(step == 0)
    def _():
        route_ref[...] = jnp.zeros_like(route_ref)

    for k in range(len(parts) // 3):
        hidden_ref, active_ref, pull_ref = parts[3 * k : 3 * k + 3]

        @pl.when((step >= k * steps) & (step < (k + 1) * steps))
        def _(hidden_ref=hidden_ref, active_ref=active_ref, pull_ref=pull_ref):
            d_gate_ref[...] = (d_hidden * pull_ref[...].astype(f32)).astype(bf16)
            d_up_ref[...] = (d_hidden * active_ref[...].astype(f32)).astype(bf16)
            route_ref[...] += jnp.sum(hidden_ref[...].astype(f32) * back, axis=1, keepdims=True)


def back_project(g, gain, w_down, parts):
    rows, width = g.shape
    units = w_down.shape[0]
    block = tile(parts[0][0].shape[1], 256)
    steps = units // block // len(parts)
    unit = pl.BlockSpec((rows, block), lambda i: (0, i))

    def unit_of(part):
        return pl.BlockSpec((rows, block), lambda i: (0, jnp.clip(i - part * steps, 0, steps - 1)))

    shape = jax.ShapeDtypeStruct((rows, units), bf16)
    return call(
        functools.partial(back_kernel, steps),
        2 * rows * width * units,
        2 * width * units,
        grid=(units // block,),
        in_specs=[
            whole(rows, width),
            whole(rows, 1),
            pl.BlockSpec((block, width), lambda i: (i, 0)),
        ]
        + [unit_of(k) for k in range(len(parts)) for _ in range(3)],
        out_specs=[unit, unit, whole(rows, 1)],
        out_shape=[shape, shape, jax.ShapeDtypeStruct((rows, 1), f32)],
    )(g, gain, w_down, *[array for part in parts for array in part])


def token_kernel(steps, spread, d_gate_ref, d_up_ref, slot_ref, route_ref, gate_ref, up_ref, *outs):
    step = pl.program_id(0)

    def store(part):
        if not spread:
            outs[0][...] = part
            return
        half = slot_ref.shape[0] // 2
        width = part.shape[1]
        for k in range(2):
            slot = slot_ref[k * half : (k + 1) * half, :]
            lanes = lax.broadcasted_iota(jnp.int32, (half, part.shape[0]), 1)
            place = jnp.where(lanes == slot, 1.0, 0.0).astype(bf16)
            outs[k][:, :width] = dot(place, part, ((1,), (0,))).astype(bf16)

    @pl.when(step < steps)
    def _():
        part = dot(d_gate_ref[...], gate_ref[...], ((1,), (1,)))
        store((part + dot(d_up_ref[...], up_ref[...], ((1,), (1,)))).astype(bf16))

    if spread:

        @pl.when(step >= steps)
        def _():
            store(route_ref[...])


def token_grad(d_gate, d_up, slot, route, w_gate, w_up, chunk, chunks, spread):
    rows, units = d_gate.shape
    width = w_gate.shape[0] // chunks
    total = slot.shape[0]
    block = tile(width, 512)
    steps = width // block
    first = chunk * steps
    extra = route.shape[1] if spread and chunk == chunks - 1 else 0
    weight = pl.BlockSpec((block, units), lambda i: (first + jnp.minimum(i, steps - 1), 0))
    out_rows = [total // 2] * 2 if spread else [rows]
    return call(
        functools.partial(token_kernel, steps, spread),
        4 * rows * width * units + 2 * rows * width * total * spread,
        4 * width * units + 2 * total * width,
        grid=(steps + (extra > 0),),
        in_specs=[whole(rows, units), whole(rows, units), whole(total, 1), whole(*route.shape), weight, weight],
        out_specs=[pl.BlockSpec((n, block), lambda i: (0, i)) for n in out_rows],
        out_shape=[jax.ShapeDtypeStruct((n, width + extra), bf16) for n in out_rows],
    )(d_gate, d_up, slot.reshape(total, 1), route, w_gate, w_up)


def down_kernel(g_ref, gain_ref, hidden_ref, *refs):
    out_ref, scaled = refs[-2:]

    @pl.when(pl.program_id(0) == 0)
    def _():
        scaled[...] = (gain_ref[...] * g_ref[...].astype(f32)).astype(bf16)

    out_ref[...] = dot(hidden_ref[...], scaled[...], ((0,), (0,))).astype(bf16)


def down_grad(g, gain, hidden, low, mine, first, units, into):
    rows, width = g.shape
    block = tile(mine, 256)
    start, source = first // block, low // block
    kept = [] if into is None else [into]
    return call(
        down_kernel,
        2 * rows * width * mine,
        2 * width * mine,
        grid=(mine // block,),
        in_specs=[whole(rows, width), whole(rows, 1), pl.BlockSpec((rows, block), lambda i: (0, source + i))]
        + [pl.BlockSpec(memory_space=pl.ANY)] * len(kept),
        out_specs=pl.BlockSpec((block, width), lambda i: (start + i, 0)),
        out_shape=jax.ShapeDtypeStruct((units, width), bf16),
        scratch_shapes=[pltpu.VMEM((rows, width), bf16)],
        input_output_aliases={3: 0} if kept else {},
    )(g, gain, hidden, *kept)


def body(tokens, grad_out, expert_ids, route_weights, w_gate, w_up, w_down):
    wide_count = lax.axis_size("wide")
    narrow_count = lax.axis_size("narrow")
    local_experts = w_gate.shape[0]
    experts_all = local_experts * wide_count
    tok_count, top_count = expert_ids.shape
    capacity = min(tok_count, 2 * tok_count * top_count // experts_all)
    rows = wide_count * capacity
    total = wide_count * tok_count
    cols = tokens.shape[1]
    me = lax.axis_index("wide")
    pad = -2 * top_count % LANES
    meta = jnp.concatenate(
        [expert_ids.astype(bf16), route_weights, jnp.zeros((tok_count, pad), bf16)], axis=1
    )
    first_t = gather_z(jnp.concatenate([tokens, meta], axis=1))
    x_t, y_t = gather_sides(first_t)
    first_g = gather_z(after(grad_out, first_t))
    far_t = gather_far(x_t, y_t)
    x_g, y_g = gather_sides(after(first_g, *far_t))
    pieces_t = gather_core([first_t, x_t, y_t] + far_t)
    all_meta = gather_meta(pieces_t, cols)
    all_ids = all_meta[:, :top_count].astype(jnp.int32)
    all_weights = all_meta[:, top_count : 2 * top_count].astype(f32)
    first = me * local_experts
    fused = narrow_count == 1 and local_experts == 1
    chunks = CHUNKS if fused else 1
    units = w_gate.shape[2]
    parts = 2 if units % (2 * LANES) == 0 else 1
    picked = []
    for j in range(local_experts):
        match = all_ids == first + j
        chosen = jnp.any(match, axis=1)
        gain = jnp.sum(jnp.where(match, all_weights, 0.0), axis=1)
        rank = jnp.cumsum(chosen.astype(jnp.int32)) - 1
        slot = jnp.where(chosen, rank, -1)
        place = slot[None, :] == jnp.arange(rows, dtype=jnp.int32)[:, None]
        row_gain = jnp.sum(jnp.where(place, gain[None, :], 0.0), axis=1, keepdims=True)
        x = pick_rows(slot, pieces_t, rows, cols)
        x = lax.all_gather(x, "narrow", axis=1, tiled=True)
        ahead = [forward(x, w_gate[j], w_up[j], 0, parts)]
        picked.append((slot, place, row_gain, x, ahead))
    x_g, y_g, *_ = lax.optimization_barrier((x_g, y_g, *[ahead[0][0] for *_, ahead in picked]))
    far_g = gather_far(x_g, y_g)
    for j in range(local_experts):
        slot, place, row_gain, x, ahead = picked[j]
        if parts == 2:
            ahead.append(forward(after(x, x_g, y_g), w_gate[j], w_up[j], 1, parts))
    far_g = lax.optimization_barrier((*far_g, *[ahead[-1][0] for *_, ahead in picked]))[: len(far_g)]
    pieces_g = gather_core([first_g, x_g, y_g, *far_g])
    expert_cols = experts_all + -experts_all % LANES
    dense = [0, 0]
    route_all = 0
    ends = []
    for j in range(local_experts):
        slot, place, row_gain, x, ahead = picked[j]
        g = pick_rows(slot, pieces_g, rows, cols)
        g = lax.all_gather(g, "narrow", axis=1, tiled=True)
        d_gate, d_up, route = back_project(g, row_gain, w_down[j], ahead)
        route = lax.psum(route.astype(bf16).astype(f32), "narrow")
        at = jnp.arange(expert_cols, dtype=jnp.int32) == first + j
        route = jnp.where(at[None, :], route, 0.0).astype(bf16)
        ends.append((g, row_gain, [part[0] for part in ahead]))
        if fused:
            own, other = token_grad(d_gate, d_up, slot, route, w_gate[j], w_up[j], 0, chunks, True)
            dense = [own, other]
            continue
        (part,) = token_grad(d_gate, d_up, slot, route, w_gate[j], w_up[j], 0, 1, False)
        part = lax.psum_scatter(part, "narrow", scatter_dimension=1, tiled=True)
        part = jnp.concatenate([part, route], axis=1)
        part = dot(place.astype(bf16), part, ((0,), (0,)))
        dense = [dense[0] + part[: total // 2], dense[1] + part[total // 2 :]]
    mine = [add(dense[0].astype(bf16), flip(dense[1].astype(bf16), CORE))]
    if fused and chunks == 2:
        own, other = token_grad(after(d_gate, dense[0]), d_up, slot, route, w_gate[0], w_up[0], 1, chunks, True)
        mine[0] = add(after(dense[0], own), flip(dense[1], CORE))
        mine.append(add(own, flip(other, CORE)))
    sides = [scatter_far(rows_) for rows_ in mine]
    firsts = [scatter_sides(*side) for side in sides]
    shares = [scatter_z(first_) for first_ in firsts]
    gates = iter([mine[0], sides[0][1], firsts[0], firsts[-1]])
    grad_downs = []
    for g, row_gain, hidden in ends:
        out, first_unit = None, 0
        for piece in hidden:
            count = piece.shape[1]
            cut = 2 * LANES * (count // (4 * LANES)) if len(hidden) > 1 and count % (2 * LANES) == 0 else 0
            for low, high in ((0, cut), (cut, count)):
                if high > low:
                    ready = after(piece, next(gates)) if local_experts == 1 else piece
                    out = down_grad(g, row_gain, ready, low, high - low, first_unit + low, units, out)
            first_unit += count
        grad_downs.append(out)
    joined = jnp.concatenate(shares, axis=1)
    width = tokens.shape[1]
    by_expert = joined[:, width : width + experts_all].astype(f32)
    pick = expert_ids[:, :, None] == jnp.arange(experts_all, dtype=jnp.int32)[None, None, :]
    grad_route = jnp.sum(jnp.where(pick, by_expert[:, None, :], 0.0), axis=2)
    return (joined[:, :width], grad_route.astype(bf16), jnp.stack(grad_downs))


def solution(mesh):
    in_specs = (
        P("wide", "narrow"),
        P("wide", "narrow"),
        P("wide", None),
        P("wide", None),
        P("wide", None, "narrow"),
        P("wide", None, "narrow"),
        P("wide", "narrow", None),
    )
    out_specs = (P("wide", "narrow"), P("wide", None), P("wide", "narrow", None))
    return jax.shard_map(body, mesh=mesh, in_specs=in_specs, out_specs=out_specs, check_vma=False)
```

```python
import functools

import jax
import jax.numpy as jnp
from jax import lax
from jax.experimental import pallas as pl
from jax.experimental.pallas import tpu as pltpu
from jax.sharding import PartitionSpec as P

LANES = 128
CHUNKS = 2
bf16, f32 = jnp.bfloat16, jnp.float32


def dot(a, b, dims):
    return lax.dot_general(a, b, ((dims[0], dims[1]), ((), ())), preferred_element_type=f32)


def add(*terms):
    total = terms[0].astype(f32)
    for term in terms[1:]:
        total = total + term.astype(f32)
    return total.astype(terms[0].dtype)


def tile(size, most):
    fits = [t for t in range(LANES, min(size, most) + 1, LANES) if size % t == 0]
    return fits[-1] if fits else size


def call(kernel, flops, moved, **kwargs):
    return pl.pallas_call(
        kernel,
        compiler_params=pltpu.CompilerParams(vmem_limit_bytes=52 * 1024 * 1024),
        cost_estimate=pl.CostEstimate(flops=flops, bytes_accessed=moved, transcendentals=0),
        **kwargs,
    )


def whole(*shape):
    return pl.BlockSpec(shape, lambda i: (0,) * len(shape))


CORE, X, Y, Z = 1, 2, 4, 8


def flip(value, mask):
    count = lax.axis_size("wide")
    return lax.ppermute(value, "wide", [(i, i ^ mask) for i in range(count)])


def after(value, *deps):
    return lax.optimization_barrier((value, *deps))[0]


def depth():
    return lax.axis_size("wide") // Z


def gather_z(shard):
    return jnp.concatenate([shard] + [flip(shard, Z * k) for k in range(1, depth())], axis=0)


def gather_sides(first):
    return flip(first, X), flip(first, Y)


def gather_far(by_x, by_y):
    half = by_x.shape[0] // 2
    return [flip(by_y[:half], X), flip(by_x[half:], Y)]


def gather_core(pieces):
    return pieces + [flip(piece, CORE) for piece in pieces]


def offsets():
    return [Z * k + m + c for c in (0, CORE) for m in (0, X, Y, X | Y) for k in range(depth())]


def quarters(mine):
    size = mine.shape[0] // 4
    return [mine[k * size : (k + 1) * size] for k in range(4)]


def scatter_far(mine):
    first, by_x, by_y, far = quarters(mine)
    half = far.shape[0] // 2
    to_y, to_x = flip(far[:half], X), flip(far[half:], Y)
    by_y = jnp.concatenate([add(by_y[:half], to_y), by_y[half:]], axis=0)
    by_x = jnp.concatenate([by_x[:half], add(by_x[half:], to_x)], axis=0)
    return first, by_x, by_y


def scatter_sides(first, by_x, by_y):
    return add(first, flip(by_x, X), flip(by_y, Y))


def scatter_z(first):
    step = first.shape[0] // depth()
    blocks = [first[k * step : (k + 1) * step] for k in range(depth())]
    return add(blocks[0], *[flip(blocks[k], Z * k) for k in range(1, depth())])


def meta_kernel(sizes, cols, *refs):
    pieces, (out_ref, sems) = refs[: len(sizes)], refs[len(sizes) :]
    starts = [sum(sizes[:k]) for k in range(len(sizes))]
    copies = [
        pltpu.make_async_copy(
            pieces[k].at[:, pl.ds(cols, LANES)], out_ref.at[pl.ds(starts[k], sizes[k]), :], sems.at[k]
        )
        for k in range(len(sizes))
    ]
    for copy in copies:
        copy.start()
    for copy in copies:
        copy.wait()


def gather_meta(pieces, cols):
    sizes = [piece.shape[0] for piece in pieces]
    return call(
        functools.partial(meta_kernel, sizes, cols),
        0,
        4 * sum(sizes) * LANES,
        grid=(1,),
        in_specs=[pl.BlockSpec(memory_space=pl.ANY)] * len(pieces),
        out_specs=whole(sum(sizes), LANES),
        out_shape=jax.ShapeDtypeStruct((sum(sizes), LANES), bf16),
        scratch_shapes=[pltpu.SemaphoreType.DMA((len(sizes),))],
    )(*pieces)


class Rows:
    def __init__(self, slot, pieces, rows, cols):
        self.slot, self.pieces, self.rows, self.cols = slot, pieces, rows, cols
        self.sizes = [piece.shape[0] for piece in pieces]
        self.total = sum(self.sizes)
        self.block = tile(cols, 512)
        self.steps = cols // self.block
        self.picked = slot is not None
        self.flops = 2 * rows * self.total * cols if self.picked else 0

    def args(self):
        return ([self.slot.reshape(1, self.total)] if self.picked else []) + list(self.pieces)

    def specs(self):
        if not self.picked:
            return [pl.BlockSpec((self.rows, self.block), lambda i: (0, i))]
        return [whole(1, self.total)] + [pl.BlockSpec(memory_space=pl.ANY)] * len(self.sizes)

    def scratch(self):
        if not self.picked:
            return []
        return [
            pltpu.VMEM((self.steps, self.total, self.block), bf16),
            pltpu.VMEM((self.rows, self.total), bf16),
            pltpu.SemaphoreType.DMA((self.steps, len(self.sizes))),
        ]

    def take(self, refs):
        args, scratch = len(self.sizes) + self.picked, len(self.scratch())
        return refs[:args], refs[args : len(refs) - scratch], refs[len(refs) - scratch :]

    def load(self, refs, scratch):
        if not self.picked:
            return refs[0][...]
        slot_ref, *pieces = refs
        held, place, sems = scratch
        step = pl.program_id(0)
        starts = [sum(self.sizes[:k]) for k in range(len(self.sizes))]

        def copy(at, k):
            return pltpu.make_async_copy(
                pieces[k].at[:, pl.ds(pl.multiple_of(at * self.block, LANES), self.block)],
                held.at[at, pl.ds(starts[k], self.sizes[k]), :],
                sems.at[at, k],
            )

        @pl.when(step == 0)
        def _():
            @pl.loop(0, self.steps)
            def _(at):
                for k in range(len(self.sizes)):
                    copy(at, k).start()

            number = lax.broadcasted_iota(jnp.int32, place.shape, 0)
            place[...] = jnp.where(number == slot_ref[...], 1.0, 0.0).astype(bf16)

        for k in range(len(self.sizes)):
            copy(step, k).wait()
        return dot(place[...], held[step], ((1,), (0,))).astype(bf16)


def pick_kernel(source, *refs):
    args, (out_ref,), scratch = source.take(refs)
    out_ref[...] = source.load(args, scratch)


def pick_rows(source):
    return call(
        functools.partial(pick_kernel, source),
        source.flops,
        2 * (source.rows + source.total) * source.cols,
        grid=(source.steps,),
        in_specs=source.specs(),
        out_specs=pl.BlockSpec((source.rows, source.block), lambda i: (0, i)),
        out_shape=jax.ShapeDtypeStruct((source.rows, source.cols), bf16),
        scratch_shapes=source.scratch(),
    )(*source.args())


def forward_kernel(source, *refs):
    args, rest, scratch = source.take(refs)
    gate_ref, up_ref, hidden_ref, active_ref, pull_ref, gate_sum, up_sum = rest
    step = pl.program_id(0)
    x = source.load(args, scratch)

    @pl.when(step == 0)
    def _():
        gate_sum[...] = dot(x, gate_ref[...], ((1,), (0,)))
        up_sum[...] = dot(x, up_ref[...], ((1,), (0,)))

    @pl.when(step > 0)
    def _():
        gate_sum[...] += dot(x, gate_ref[...], ((1,), (0,)))
        up_sum[...] += dot(x, up_ref[...], ((1,), (0,)))

    @pl.when(step == pl.num_programs(0) - 1)
    def _():
        units = gate_sum.shape[1]
        part = tile(units, 256)
        for low in range(0, units, part):
            gate_pre = gate_sum[:, low : low + part].T
            up_pre = up_sum[:, low : low + part].T
            sig = jax.nn.sigmoid(gate_pre)
            active = gate_pre * sig
            hidden_ref[low : low + part, :] = (active * up_pre).astype(bf16)
            active_ref[low : low + part, :] = active.astype(bf16)
            pull_ref[low : low + part, :] = (up_pre * (sig * (1.0 + gate_pre * (1.0 - sig)))).astype(bf16)


def forward(source, w_gate, w_up):
    rows, width = source.rows, source.cols
    units = w_gate.shape[1]
    weight = pl.BlockSpec((source.block, units), lambda i: (i, 0))
    return call(
        functools.partial(forward_kernel, source),
        4 * rows * width * units + source.flops,
        4 * width * units + 2 * source.total * width,
        grid=(source.steps,),
        in_specs=source.specs() + [weight, weight],
        out_specs=[whole(units, rows)] * 3,
        out_shape=[jax.ShapeDtypeStruct((units, rows), bf16)] * 3,
        scratch_shapes=[pltpu.VMEM((rows, units), f32)] * 2 + source.scratch(),
    )(*source.args(), w_gate, w_up)


def back_kernel(source, *refs):
    args, rest, scratch = source.take(refs)
    (gain_col, gain_row, down_ref, hidden_ref, active_ref, pull_ref) = rest[:6]
    (scaled_ref, d_gate_ref, d_up_ref, route_ref, back_sum) = rest[6:]
    step = pl.program_id(0)
    g = source.load(args, scratch)
    scaled_ref[...] = (gain_col[...] * g.astype(f32)).astype(bf16)
    g = g.T

    @pl.when(step == 0)
    def _():
        back_sum[...] = dot(down_ref[...], g, ((1,), (0,)))

    @pl.when(step > 0)
    def _():
        back_sum[...] += dot(down_ref[...], g, ((1,), (0,)))

    @pl.when(step == pl.num_programs(0) - 1)
    def _():
        units = back_sum.shape[0]
        part = tile(units, 256)
        route = jnp.zeros(route_ref.shape, f32)
        for low in range(0, units, part):
            at = slice(low, low + part)
            back = back_sum[at, :]
            d_hidden = gain_row[...] * back
            d_gate_ref[at, :] = (d_hidden * pull_ref[at, :].astype(f32)).astype(bf16)
            d_up_ref[at, :] = (d_hidden * active_ref[at, :].astype(f32)).astype(bf16)
            route = route + jnp.sum(hidden_ref[at, :].astype(f32) * back, axis=0, keepdims=True)
        route_ref[...] = route


def back_project(source, gain, w_down, hidden, active, pull):
    rows, width = source.rows, source.cols
    units = w_down.shape[0]
    unit = whole(units, rows)
    shape = jax.ShapeDtypeStruct((units, rows), bf16)
    return call(
        functools.partial(back_kernel, source),
        2 * rows * width * units + source.flops,
        2 * width * units + 2 * source.total * width,
        grid=(source.steps,),
        in_specs=source.specs()
        + [whole(rows, 1), whole(1, rows), pl.BlockSpec((units, source.block), lambda i: (0, i))]
        + [unit] * 3,
        out_specs=[pl.BlockSpec((rows, source.block), lambda i: (0, i)), unit, unit, whole(1, rows)],
        out_shape=[jax.ShapeDtypeStruct((rows, width), bf16), shape, shape, jax.ShapeDtypeStruct((1, rows), f32)],
        scratch_shapes=[pltpu.VMEM((units, rows), f32)] + source.scratch(),
    )(*source.args(), gain.reshape(rows, 1), gain.reshape(1, rows), w_down, hidden, active, pull)


def token_kernel(steps, spread, d_gate_ref, d_up_ref, slot_ref, route_ref, gate_ref, up_ref, *outs):
    step = pl.program_id(0)

    def store(part):
        half = slot_ref.shape[0] // 2
        width, rows = part.shape
        for k in range(2):
            slot = slot_ref[k * half : (k + 1) * half, :]
            lanes = lax.broadcasted_iota(jnp.int32, (half, rows), 1)
            place = jnp.where(lanes == slot, 1.0, 0.0).astype(bf16)
            outs[k][:, :width] = dot(place, part, ((1,), (1,))).astype(bf16)

    @pl.when(step < steps)
    def _():
        part = dot(gate_ref[...], d_gate_ref[...], ((1,), (0,)))
        part = (part + dot(up_ref[...], d_up_ref[...], ((1,), (0,)))).astype(bf16)
        if spread:
            store(part)
        else:
            outs[0][...] = part.T

    if spread:

        @pl.when(step >= steps)
        def _():
            store(route_ref[...])


def token_grad(d_gate, d_up, slot, route, w_gate, w_up, chunk, chunks, spread):
    units, rows = d_gate.shape
    width = w_gate.shape[0] // chunks
    total = slot.shape[0]
    block = tile(width, 512)
    steps = width // block
    first = chunk * steps
    extra = route.shape[0] if spread and chunk == chunks - 1 else 0
    weight = pl.BlockSpec((block, units), lambda i: (first + jnp.minimum(i, steps - 1), 0))
    out_rows = [total // 2] * 2 if spread else [rows]
    return call(
        functools.partial(token_kernel, steps, spread),
        4 * rows * width * units + 2 * rows * width * total * spread,
        4 * width * units + 2 * total * width,
        grid=(steps + (extra > 0),),
        in_specs=[whole(units, rows), whole(units, rows), whole(total, 1), whole(*route.shape), weight, weight],
        out_specs=[pl.BlockSpec((n, block), lambda i: (0, i)) for n in out_rows],
        out_shape=[jax.ShapeDtypeStruct((n, width + extra), bf16) for n in out_rows],
    )(d_gate, d_up, slot.reshape(total, 1), route, w_gate, w_up)


def down_kernel(hidden_ref, scaled_ref, *refs):
    refs[-1][...] = dot(hidden_ref[...], scaled_ref[...], ((1,), (0,))).astype(bf16)


def down_grad(hidden, scaled, chunk, chunks, into):
    units, rows = hidden.shape
    width = scaled.shape[1]
    block = tile(width // chunks, 512)
    steps = width // chunks // block
    first = chunk * steps
    kept = [] if into is None else [into]
    return call(
        down_kernel,
        2 * rows * width * units // chunks,
        2 * width * units // chunks,
        grid=(steps,),
        in_specs=[whole(units, rows), pl.BlockSpec((rows, block), lambda i: (0, first + i))]
        + [pl.BlockSpec(memory_space=pl.ANY)] * len(kept),
        out_specs=pl.BlockSpec((units, block), lambda i: (0, first + i)),
        out_shape=jax.ShapeDtypeStruct((units, width), bf16),
        input_output_aliases={2: 0} if kept else {},
    )(hidden, scaled, *kept)


def body(tokens, grad_out, expert_ids, route_weights, w_gate, w_up, w_down):
    wide_count = lax.axis_size("wide")
    narrow_count = lax.axis_size("narrow")
    local_experts = w_gate.shape[0]
    experts_all = local_experts * wide_count
    tok_count, top_count = expert_ids.shape
    capacity = min(tok_count, 2 * tok_count * top_count // experts_all)
    rows = wide_count * capacity
    total = wide_count * tok_count
    cols = tokens.shape[1]
    me = lax.axis_index("wide")
    pad = -2 * top_count % LANES
    meta = jnp.concatenate(
        [expert_ids.astype(bf16), route_weights, jnp.zeros((tok_count, pad), bf16)], axis=1
    )
    first_t = gather_z(jnp.concatenate([tokens, meta], axis=1))
    x_t, y_t = gather_sides(first_t)
    first_g = gather_z(after(grad_out, first_t))
    far_t = gather_far(x_t, y_t)
    x_g, y_g = gather_sides(after(first_g, *far_t))
    pieces_t = gather_core([first_t, x_t, y_t] + far_t)
    all_meta = gather_meta(pieces_t, cols)
    all_ids = all_meta[:, :top_count].astype(jnp.int32)
    all_weights = all_meta[:, top_count : 2 * top_count].astype(f32)
    first = me * local_experts
    fused = narrow_count == 1 and local_experts == 1
    chunks = CHUNKS if fused else 1
    picked = []
    for j in range(local_experts):
        match = all_ids == first + j
        chosen = jnp.any(match, axis=1)
        gain = jnp.sum(jnp.where(match, all_weights, 0.0), axis=1)
        rank = jnp.cumsum(chosen.astype(jnp.int32)) - 1
        slot = jnp.where(chosen, rank, -1)
        place = slot[None, :] == jnp.arange(rows, dtype=jnp.int32)[:, None]
        row_gain = jnp.sum(jnp.where(place, gain[None, :], 0.0), axis=1)
        source = Rows(slot, pieces_t, rows, cols)
        if narrow_count > 1:
            x = lax.all_gather(pick_rows(source), "narrow", axis=1, tiled=True)
            source = Rows(None, [x], rows, x.shape[1])
        picked.append((slot, place, row_gain, forward(source, w_gate[j], w_up[j])))
    x_g, y_g, *_ = lax.optimization_barrier((x_g, y_g, *[ahead[0] for *_, ahead in picked]))
    pieces_g = gather_core([first_g, x_g, y_g] + gather_far(x_g, y_g))
    expert_cols = experts_all + -experts_all % LANES
    dense = [0, 0]
    ends = []
    for j in range(local_experts):
        slot, place, row_gain, (hidden, active, pull) = picked[j]
        source = Rows(slot, pieces_g, rows, cols)
        if narrow_count > 1:
            g = lax.all_gather(pick_rows(source), "narrow", axis=1, tiled=True)
            source = Rows(None, [g], rows, g.shape[1])
        scaled, d_gate, d_up, route = back_project(source, row_gain, w_down[j], hidden, active, pull)
        route = lax.psum(route.astype(bf16).astype(f32), "narrow")
        at = jnp.arange(expert_cols, dtype=jnp.int32) == first + j
        route = jnp.where(at[:, None], route, 0.0).astype(bf16)
        ends.append((hidden, scaled))
        if fused:
            own, other = token_grad(d_gate, d_up, slot, route, w_gate[j], w_up[j], 0, chunks, True)
            dense = [own, other]
            continue
        (part,) = token_grad(d_gate, d_up, slot, route, w_gate[j], w_up[j], 0, 1, False)
        part = lax.psum_scatter(part, "narrow", scatter_dimension=1, tiled=True)
        part = jnp.concatenate([part, route.T], axis=1)
        part = dot(place.astype(bf16), part, ((0,), (0,)))
        dense = [dense[0] + part[: total // 2], dense[1] + part[total // 2 :]]
    mine = [add(dense[0].astype(bf16), flip(dense[1].astype(bf16), CORE))]
    if fused and chunks == 2:
        own, other = token_grad(after(d_gate, dense[0]), d_up, slot, route, w_gate[0], w_up[0], 1, chunks, True)
        mine[0] = add(after(dense[0], own), flip(dense[1], CORE))
        mine.append(add(own, flip(other, CORE)))
    sides = [scatter_far(rows_) for rows_ in mine]
    firsts = [scatter_sides(*side) for side in sides]
    shares = [scatter_z(first_) for first_ in firsts]
    grad_downs = []
    for hidden, scaled in ends:
        out = down_grad(after(hidden, mine[0]), scaled, 0, 2, None)
        grad_downs.append(down_grad(after(hidden, *sides[0]), scaled, 1, 2, out))
    joined = jnp.concatenate(shares, axis=1)
    width = tokens.shape[1]
    by_expert = joined[:, width : width + experts_all].astype(f32)
    pick = expert_ids[:, :, None] == jnp.arange(experts_all, dtype=jnp.int32)[None, None, :]
    grad_route = jnp.sum(jnp.where(pick, by_expert[:, None, :], 0.0), axis=2)
    return (joined[:, :width], grad_route.astype(bf16), jnp.stack(grad_downs))


def solution(mesh):
    in_specs = (
        P("wide", "narrow"),
        P("wide", "narrow"),
        P("wide", None),
        P("wide", None),
        P("wide", None, "narrow"),
        P("wide", None, "narrow"),
        P("wide", "narrow", None),
    )
    out_specs = (P("wide", "narrow"), P("wide", None), P("wide", "narrow", None))
    return jax.shard_map(body, mesh=mesh, in_specs=in_specs, out_specs=out_specs, check_vma=False)
```

```python
import functools

import jax
import jax.numpy as jnp
from jax import lax
from jax.experimental import pallas as pl
from jax.experimental.pallas import tpu as pltpu
from jax.sharding import PartitionSpec as P

LANES = 128
CHUNKS = 2
bf16, f32 = jnp.bfloat16, jnp.float32


def dot(a, b, dims):
    return lax.dot_general(a, b, ((dims[0], dims[1]), ((), ())), preferred_element_type=f32)


def add(*terms):
    total = terms[0].astype(f32)
    for term in terms[1:]:
        total = total + term.astype(f32)
    return total.astype(terms[0].dtype)


def tile(size, most):
    fits = [t for t in range(LANES, min(size, most) + 1, LANES) if size % t == 0]
    return fits[-1] if fits else size


def call(kernel, flops, moved, **kwargs):
    return pl.pallas_call(
        kernel,
        compiler_params=pltpu.CompilerParams(vmem_limit_bytes=52 * 1024 * 1024),
        cost_estimate=pl.CostEstimate(flops=flops, bytes_accessed=moved, transcendentals=0),
        **kwargs,
    )


def whole(*shape):
    return pl.BlockSpec(shape, lambda i: (0,) * len(shape))


CORE, X, Y, Z = 1, 2, 4, 8


def flip(value, mask):
    count = lax.axis_size("wide")
    return lax.ppermute(value, "wide", [(i, i ^ mask) for i in range(count)])


def after(value, *deps):
    return lax.optimization_barrier((value, *deps))[0]


def depth():
    return lax.axis_size("wide") // Z


def gather_z(shard):
    blocks = [shard] + [flip(shard, Z * k) for k in range(1, depth())]
    half = depth() // 2
    return jnp.concatenate(blocks[:half], axis=0), blocks[half:]


def join(blocks, *deps):
    return jnp.concatenate(lax.optimization_barrier((*blocks, *deps))[: len(blocks)], axis=0)


def gather_core(pieces):
    return pieces + [flip(piece, CORE) for piece in pieces]


def offsets():
    return [Z * k + m + c for c in (0, CORE) for m in (0, X, Y, X | Y) for k in range(depth())]


def quarters(mine):
    size = mine.shape[0] // 4
    return [mine[k * size : (k + 1) * size] for k in range(4)]


def scatter_z(first):
    step = first.shape[0] // depth()
    blocks = [first[k * step : (k + 1) * step] for k in range(depth())]
    return add(blocks[0], *[flip(blocks[k], Z * k) for k in range(1, depth())])


def meta_kernel(sizes, cols, *refs):
    pieces, (out_ref, sems) = refs[: len(sizes)], refs[len(sizes) :]
    starts = [sum(sizes[:k]) for k in range(len(sizes))]
    copies = [
        pltpu.make_async_copy(
            pieces[k].at[:, pl.ds(cols, LANES)], out_ref.at[pl.ds(starts[k], sizes[k]), :], sems.at[k]
        )
        for k in range(len(sizes))
    ]
    for copy in copies:
        copy.start()
    for copy in copies:
        copy.wait()


def gather_meta(pieces, cols):
    sizes = [piece.shape[0] for piece in pieces]
    return call(
        functools.partial(meta_kernel, sizes, cols),
        0,
        4 * sum(sizes) * LANES,
        grid=(1,),
        in_specs=[pl.BlockSpec(memory_space=pl.ANY)] * len(pieces),
        out_specs=whole(sum(sizes), LANES),
        out_shape=jax.ShapeDtypeStruct((sum(sizes), LANES), bf16),
        scratch_shapes=[pltpu.SemaphoreType.DMA((len(sizes),))],
    )(*pieces)


def pick_kernel(sizes, block, slot_ref, *refs):
    pieces, (out_ref, held, place, sems) = refs[: len(sizes)], refs[len(sizes) :]
    step = pl.program_id(0)
    starts = [sum(sizes[:k]) for k in range(len(sizes))]

    def copy(at, k):
        return pltpu.make_async_copy(
            pieces[k].at[:, pl.ds(pl.multiple_of(at * block, LANES), block)],
            held.at[at, pl.ds(starts[k], sizes[k]), :],
            sems.at[at, k],
        )

    @pl.when(step == 0)
    def _():
        @pl.loop(0, pl.num_programs(0))
        def _(at):
            for k in range(len(sizes)):
                copy(at, k).start()

        rows = lax.broadcasted_iota(jnp.int32, place.shape, 0)
        place[...] = jnp.where(rows == slot_ref[...], 1.0, 0.0).astype(bf16)

    for k in range(len(sizes)):
        copy(step, k).wait()
    out_ref[...] = dot(place[...], held[step], ((1,), (0,))).astype(bf16)


def pick_rows(slot, pieces, rows, cols):
    sizes = [piece.shape[0] for piece in pieces]
    total = sum(sizes)
    block = tile(cols, 512)
    steps = cols // block
    return call(
        functools.partial(pick_kernel, sizes, block),
        2 * rows * total * cols,
        2 * (rows + total) * cols,
        grid=(steps,),
        in_specs=[whole(1, total)] + [pl.BlockSpec(memory_space=pl.ANY)] * len(pieces),
        out_specs=pl.BlockSpec((rows, block), lambda i: (0, i)),
        out_shape=jax.ShapeDtypeStruct((rows, cols), bf16),
        scratch_shapes=[
            pltpu.VMEM((steps, total, block), bf16),
            pltpu.VMEM((rows, total), bf16),
            pltpu.SemaphoreType.DMA((steps, len(sizes))),
        ],
    )(slot.reshape(1, total), *pieces)


def forward_kernel(x_ref, gate_ref, up_ref, hidden_ref, turned_ref, active_ref, pull_ref):
    gate_pre = dot(x_ref[...], gate_ref[...], ((1,), (0,)))
    up_pre = dot(x_ref[...], up_ref[...], ((1,), (0,)))
    sig = jax.nn.sigmoid(gate_pre)
    active = gate_pre * sig
    hidden = active * up_pre
    hidden_ref[...] = hidden.astype(bf16)
    turned_ref[...] = hidden.T.astype(bf16)
    active_ref[...] = active.astype(bf16)
    pull_ref[...] = (up_pre * (sig * (1.0 + gate_pre * (1.0 - sig)))).astype(bf16)


def forward(x, w_gate, w_up, part, parts):
    rows, width = x.shape
    units = w_gate.shape[1] // parts
    block = tile(units, 256)
    first = part * (units // block)
    weight = pl.BlockSpec((width, block), lambda i: (0, first + i))
    unit = pl.BlockSpec((rows, block), lambda i: (0, i))
    turned = pl.BlockSpec((block, rows), lambda i: (i, 0))
    shape = jax.ShapeDtypeStruct((rows, units), bf16)
    return call(
        forward_kernel,
        4 * rows * width * units,
        4 * width * units,
        grid=(units // block,),
        in_specs=[whole(rows, width), weight, weight],
        out_specs=[unit, turned, unit, unit],
        out_shape=[shape, jax.ShapeDtypeStruct((units, rows), bf16), shape, shape],
    )(x, w_gate, w_up)


def back_kernel(steps, g_ref, gain_ref, down_ref, *refs):
    parts, (d_gate_ref, d_up_ref, route_ref) = refs[:-3], refs[-3:]
    step = pl.program_id(0)
    back = dot(g_ref[...], down_ref[...], ((1,), (1,)))
    d_hidden = gain_ref[...] * back

    @pl.when(step == 0)
    def _():
        route_ref[...] = jnp.zeros_like(route_ref)

    for k in range(len(parts) // 3):
        hidden_ref, active_ref, pull_ref = parts[3 * k : 3 * k + 3]

        @pl.when((step >= k * steps) & (step < (k + 1) * steps))
        def _(hidden_ref=hidden_ref, active_ref=active_ref, pull_ref=pull_ref):
            d_gate_ref[...] = (d_hidden * pull_ref[...].astype(f32)).astype(bf16)
            d_up_ref[...] = (d_hidden * active_ref[...].astype(f32)).astype(bf16)
            route_ref[...] += jnp.sum(hidden_ref[...].astype(f32) * back, axis=1, keepdims=True)


def back_project(g, gain, w_down, parts):
    rows, width = g.shape
    units = w_down.shape[0]
    block = tile(parts[0][0].shape[1], 768)
    steps = units // block // len(parts)
    unit = pl.BlockSpec((rows, block), lambda i: (0, i))

    def unit_of(part):
        return pl.BlockSpec((rows, block), lambda i: (0, jnp.clip(i - part * steps, 0, steps - 1)))

    shape = jax.ShapeDtypeStruct((rows, units), bf16)
    return call(
        functools.partial(back_kernel, steps),
        2 * rows * width * units,
        2 * width * units,
        grid=(units // block,),
        in_specs=[
            whole(rows, width),
            whole(rows, 1),
            pl.BlockSpec((block, width), lambda i: (i, 0)),
        ]
        + [unit_of(k) for k in range(len(parts)) for _ in range(3)],
        out_specs=[unit, unit, whole(rows, 1)],
        out_shape=[shape, shape, jax.ShapeDtypeStruct((rows, 1), f32)],
    )(g, gain, w_down, *[array for part in parts for array in part])


def token_kernel(steps, spread, d_gate_ref, d_up_ref, slot_ref, route_ref, gate_ref, up_ref, *outs):
    step = pl.program_id(0)

    def store(part):
        if not spread:
            outs[0][...] = part
            return
        half = slot_ref.shape[0] // 2
        rows, width = part.shape
        for k in range(2):
            slot = slot_ref[k * half : (k + 1) * half, :]
            lanes = lax.broadcasted_iota(jnp.int32, (half, rows), 1)
            place = jnp.where(lanes == slot, 1.0, 0.0).astype(bf16)
            outs[k][:, :width] = dot(place, part, ((1,), (0,))).astype(bf16)

    @pl.when(step < steps)
    def _():
        part = dot(d_gate_ref[...], gate_ref[...], ((1,), (1,)))
        store((part + dot(d_up_ref[...], up_ref[...], ((1,), (1,)))).astype(bf16))

    if spread:

        @pl.when(step >= steps)
        def _():
            store(route_ref[...])


def token_grad(d_gate, d_up, slot, route, w_gate, w_up, chunk, chunks, spread):
    rows, units = d_gate.shape
    width = w_gate.shape[0] // chunks
    total = slot.shape[0]
    block = tile(width, 512)
    steps = width // block
    first = chunk * steps
    extra = route.shape[1] if spread and chunk == chunks - 1 else 0
    weight = pl.BlockSpec((block, units), lambda i: (first + jnp.minimum(i, steps - 1), 0))
    out_rows = [total // 2] * 2 if spread else [rows]
    return call(
        functools.partial(token_kernel, steps, spread),
        4 * rows * width * units + 2 * rows * width * total * spread,
        4 * width * units + 2 * total * width,
        grid=(steps + (extra > 0),),
        in_specs=[whole(rows, units), whole(rows, units), whole(total, 1), whole(*route.shape), weight, weight],
        out_specs=[pl.BlockSpec((n, block), lambda i: (0, i)) for n in out_rows],
        out_shape=[jax.ShapeDtypeStruct((n, width + extra), bf16) for n in out_rows],
    )(d_gate, d_up, slot.reshape(total, 1), route, w_gate, w_up)


def down_kernel(count, g_ref, gain_ref, *refs):
    turned, out_ref = refs[:count], refs[-1]
    scaled = (gain_ref[...] * g_ref[...].astype(f32)).astype(bf16)
    at = 0
    for ref in turned:
        out_ref[at : at + ref.shape[0], :] = dot(ref[...], scaled, ((1,), (0,))).astype(bf16)
        at += ref.shape[0]


def down_grad(turned, g, gain, chunk, chunks, into):
    rows, width = g.shape
    units = sum(part.shape[0] for part in turned)
    block = tile(width // chunks, 512)
    steps = width // chunks // block
    first = chunk * steps
    kept = [] if into is None else [into]
    return call(
        functools.partial(down_kernel, len(turned)),
        2 * rows * width * units // chunks,
        2 * width * units // chunks,
        grid=(steps,),
        in_specs=[pl.BlockSpec((rows, block), lambda i: (0, first + i)), whole(rows, 1)]
        + [whole(*part.shape) for part in turned]
        + [pl.BlockSpec(memory_space=pl.ANY)] * len(kept),
        out_specs=pl.BlockSpec((units, block), lambda i: (0, first + i)),
        out_shape=jax.ShapeDtypeStruct((units, width), bf16),
        input_output_aliases={2 + len(turned): 0} if kept else {},
    )(g, gain, *turned, *kept)


def body(tokens, grad_out, expert_ids, route_weights, w_gate, w_up, w_down):
    wide_count = lax.axis_size("wide")
    narrow_count = lax.axis_size("narrow")
    local_experts = w_gate.shape[0]
    experts_all = local_experts * wide_count
    tok_count, top_count = expert_ids.shape
    capacity = min(tok_count, 2 * tok_count * top_count // experts_all)
    rows = wide_count * capacity
    total = wide_count * tok_count
    cols = tokens.shape[1]
    me = lax.axis_index("wide")
    pad = -2 * top_count % LANES
    meta = jnp.concatenate(
        [expert_ids.astype(bf16), route_weights, jnp.zeros((tok_count, pad), bf16)], axis=1
    )
    t_a, t_b = gather_z(jnp.concatenate([tokens, meta], axis=1))
    t_xa, t_ya = flip(t_a, X), flip(t_a, Y)
    t_b = join(t_b, t_xa, t_ya)
    g_a, g_b = gather_z(after(grad_out, t_b))
    t_xb, t_yb = flip(t_b, X), flip(t_b, Y)
    t_da, t_db = flip(t_ya, X), flip(t_xb, Y)
    pieces_t = gather_core([t_a, t_b, t_xa, t_xb, t_ya, t_yb, t_da, t_db])
    g_a = after(g_a, t_xb, t_yb)
    g_xa, g_ya = flip(g_a, X), flip(g_a, Y)
    g_b = join(g_b, t_da, t_db)
    g_xb, g_yb = flip(g_b, X), flip(g_b, Y)
    all_meta = gather_meta(pieces_t, cols)
    all_ids = all_meta[:, :top_count].astype(jnp.int32)
    all_weights = all_meta[:, top_count : 2 * top_count].astype(f32)
    first = me * local_experts
    fused = narrow_count == 1 and local_experts == 1
    chunks = CHUNKS if fused else 1
    parts = 2 if w_gate.shape[2] % (2 * LANES) == 0 else 1
    picked = []
    for j in range(local_experts):
        match = all_ids == first + j
        chosen = jnp.any(match, axis=1)
        gain = jnp.sum(jnp.where(match, all_weights, 0.0), axis=1)
        rank = jnp.cumsum(chosen.astype(jnp.int32)) - 1
        slot = jnp.where(chosen, rank, -1)
        place = slot[None, :] == jnp.arange(rows, dtype=jnp.int32)[:, None]
        row_gain = jnp.sum(jnp.where(place, gain[None, :], 0.0), axis=1, keepdims=True)
        x = pick_rows(slot, pieces_t, rows, cols)
        x = lax.all_gather(x, "narrow", axis=1, tiled=True)
        picked.append([slot, place, row_gain, x])
    g_xa, g_ya, *_ = lax.optimization_barrier((g_xa, g_ya, *[entry[3] for entry in picked]))
    g_da = flip(g_ya, X)
    for j in range(local_experts):
        x = after(picked[j][3], g_xa, g_ya)
        picked[j] += [x, [forward(x, w_gate[j], w_up[j], 0, parts)]]
    g_xb, g_yb, *_ = lax.optimization_barrier((g_xb, g_yb, *[entry[5][0][0] for entry in picked]))
    g_db = flip(g_xb, Y)
    for j in range(local_experts):
        if parts == 2:
            x = after(picked[j][4], g_xb, g_yb)
            picked[j][5].append(forward(x, w_gate[j], w_up[j], 1, parts))
    g_da, g_db, *_ = lax.optimization_barrier((g_da, g_db, *[entry[5][-1][0] for entry in picked]))
    pieces_g = gather_core([g_a, g_b, g_xa, g_xb, g_ya, g_yb, g_da, g_db])
    expert_cols = experts_all + -experts_all % LANES
    dense = [0, 0]
    ends = []
    for j in range(local_experts):
        slot, place, row_gain, _, _, ahead = picked[j]
        g = pick_rows(slot, pieces_g, rows, cols)
        g = lax.all_gather(g, "narrow", axis=1, tiled=True)
        straight = [(hidden, active, pull) for hidden, _, active, pull in ahead]
        d_gate, d_up, route = back_project(g, row_gain, w_down[j], straight)
        route = lax.psum(route.astype(bf16).astype(f32), "narrow")
        at = jnp.arange(expert_cols, dtype=jnp.int32) == first + j
        route = jnp.where(at[None, :], route, 0.0).astype(bf16)
        ends.append(([part[1] for part in ahead], g, row_gain))
        if fused:
            dense = token_grad(d_gate, d_up, slot, route, w_gate[j], w_up[j], 0, chunks, True)
            continue
        (part,) = token_grad(d_gate, d_up, slot, route, w_gate[j], w_up[j], 0, 1, False)
        part = lax.psum_scatter(part, "narrow", scatter_dimension=1, tiled=True)
        part = jnp.concatenate([part, route], axis=1)
        part = dot(place.astype(bf16), part, ((0,), (0,)))
        dense = [dense[0] + part[: total // 2], dense[1] + part[total // 2 :]]

    def send_far(mine):
        near, by_x, by_y, far = quarters(mine)
        half = far.shape[0] // 2
        return [near, by_x, by_y, flip(far[:half], X), flip(far[half:], Y)]

    def add_far(near, by_x, by_y, to_y, to_x):
        half = to_y.shape[0]
        by_y = jnp.concatenate([add(by_y[:half], to_y), by_y[half:]], axis=0)
        by_x = jnp.concatenate([by_x[:half], add(by_x[half:], to_x)], axis=0)
        return near, by_x, by_y

    def send_sides(near, by_x, by_y):
        return near, flip(by_x, X), flip(by_y, Y)

    mine = add(dense[0].astype(bf16), flip(dense[1].astype(bf16), CORE))
    sent = send_far(mine)
    if fused and chunks == 2:
        (turned, g, row_gain), = ends
        own, other = token_grad(after(d_gate, mine), d_up, slot, route, w_gate[0], w_up[0], 1, chunks, True)
        *_, to_y, to_x = sent
        to_y, to_x, own, other = lax.optimization_barrier((to_y, to_x, own, other))
        near, by_x, by_y = send_sides(*add_far(*sent[:3], to_y, to_x))
        mine = add(own, flip(other, CORE))
        sent = send_far(mine)
        out = down_grad(turned, after(g, mine), row_gain, 0, 2, None)
        *_, to_y, to_x = sent
        by_x, by_y, to_y, to_x, out = lax.optimization_barrier((by_x, by_y, to_y, to_x, out))
        first_near = add(near, by_x, by_y)
        sides = add_far(*sent[:3], to_y, to_x)
        near, by_x, by_y = send_sides(*sides)
        out = down_grad(turned, after(g, *sides, first_near), row_gain, 1, 2, out)
        by_x, by_y, out = lax.optimization_barrier((by_x, by_y, out))
        shares = [scatter_z(first_near), scatter_z(add(near, by_x, by_y))]
        grad_downs = [out]
    else:
        shares = [scatter_z(add(*send_sides(*add_far(*sent))))]
        grad_downs = [down_grad(*end, 0, 1, None) for end in ends]
    joined = jnp.concatenate(shares, axis=1)
    width = tokens.shape[1]
    by_expert = joined[:, width : width + experts_all].astype(f32)
    pick = expert_ids[:, :, None] == jnp.arange(experts_all, dtype=jnp.int32)[None, None, :]
    grad_route = jnp.sum(jnp.where(pick, by_expert[:, None, :], 0.0), axis=2)
    return (joined[:, :width], grad_route.astype(bf16), jnp.stack(grad_downs))


def solution(mesh):
    in_specs = (
        P("wide", "narrow"),
        P("wide", "narrow"),
        P("wide", None),
        P("wide", None),
        P("wide", None, "narrow"),
        P("wide", None, "narrow"),
        P("wide", "narrow", None),
    )
    out_specs = (P("wide", "narrow"), P("wide", None), P("wide", "narrow", None))
    return jax.shard_map(body, mesh=mesh, in_specs=in_specs, out_specs=out_specs, check_vma=False)
```

```python
import functools

import jax
import jax.numpy as jnp
from jax import lax
from jax.experimental import pallas as pl
from jax.experimental.pallas import tpu as pltpu
from jax.sharding import PartitionSpec as P

LANES = 128
CHUNKS = 2
bf16, f32 = jnp.bfloat16, jnp.float32


def dot(a, b, dims):
    return lax.dot_general(a, b, ((dims[0], dims[1]), ((), ())), preferred_element_type=f32)


def add(*terms):
    total = terms[0].astype(f32)
    for term in terms[1:]:
        total = total + term.astype(f32)
    return total.astype(terms[0].dtype)


def tile(size, most):
    fits = [t for t in range(LANES, min(size, most) + 1, LANES) if size % t == 0]
    return fits[-1] if fits else size


def call(kernel, flops, moved, **kwargs):
    return pl.pallas_call(
        kernel,
        compiler_params=pltpu.CompilerParams(vmem_limit_bytes=52 * 1024 * 1024),
        cost_estimate=pl.CostEstimate(flops=flops, bytes_accessed=moved, transcendentals=0),
        **kwargs,
    )


def whole(*shape):
    return pl.BlockSpec(shape, lambda i: (0,) * len(shape))


CORE, X, Y, Z = 1, 2, 4, 8


def silu_parts(gate_pre):
    sigmoid_val = jax.nn.sigmoid(gate_pre)
    return (gate_pre * sigmoid_val, sigmoid_val * (1.0 + gate_pre * (1.0 - sigmoid_val)))


def flip(value, mask):
    count = lax.axis_size("wide")
    return lax.ppermute(value, "wide", [(i, i ^ mask) for i in range(count)])


def after(value, *deps):
    return lax.optimization_barrier((value, *deps))[0]


def depth():
    return lax.axis_size("wide") // Z


def along_z(shard):
    return [flip(shard, Z * k) for k in range(1, depth())]


def far_corner(by_x, by_y):
    cut = (by_x.shape[0] // 16 + 1) * 8
    return [flip(by_y[:cut], X), flip(by_x[cut:], Y)]


def join(*blocks):
    return jnp.concatenate(blocks, axis=0)


def gather_core(pieces):
    return pieces + [flip(piece, CORE) for piece in pieces]


def offsets():
    return [Z * k + m + c for c in (0, CORE) for m in (0, X, Y, X | Y) for k in range(depth())]


def quarters(mine):
    size = mine.shape[0] // 4
    return [mine[k * size : (k + 1) * size] for k in range(4)]


def scatter_z(first):
    step = first.shape[0] // depth()
    blocks = [first[k * step : (k + 1) * step] for k in range(depth())]
    return add(blocks[0], *[flip(blocks[k], Z * k) for k in range(1, depth())])


def meta_kernel(sizes, cols, *refs):
    pieces, (out_ref, sems) = refs[: len(sizes)], refs[len(sizes) :]
    starts = [sum(sizes[:k]) for k in range(len(sizes))]
    copies = [
        pltpu.make_async_copy(
            pieces[k].at[:, pl.ds(cols, LANES)], out_ref.at[pl.ds(starts[k], sizes[k]), :], sems.at[k]
        )
        for k in range(len(sizes))
    ]
    for copy in copies:
        copy.start()
    for copy in copies:
        copy.wait()


def gather_meta(pieces, cols):
    sizes = [piece.shape[0] for piece in pieces]
    return call(
        functools.partial(meta_kernel, sizes, cols),
        0,
        4 * sum(sizes) * LANES,
        grid=(1,),
        in_specs=[pl.BlockSpec(memory_space=pl.ANY)] * len(pieces),
        out_specs=whole(sum(sizes), LANES),
        out_shape=jax.ShapeDtypeStruct((sum(sizes), LANES), bf16),
        scratch_shapes=[pltpu.SemaphoreType.DMA((len(sizes),))],
    )(*pieces)


def pick_kernel(sizes, block, slot_ref, *refs):
    pieces, (out_ref, held, place, sems) = refs[: len(sizes)], refs[len(sizes) :]
    step = pl.program_id(0)
    starts = [sum(sizes[:k]) for k in range(len(sizes))]

    def copy(at, k):
        return pltpu.make_async_copy(
            pieces[k].at[:, pl.ds(pl.multiple_of(at * block, LANES), block)],
            held.at[at, pl.ds(starts[k], sizes[k]), :],
            sems.at[at, k],
        )

    @pl.when(step == 0)
    def _():
        @pl.loop(0, pl.num_programs(0))
        def _(at):
            for k in range(len(sizes)):
                copy(at, k).start()

        rows = lax.broadcasted_iota(jnp.int32, place.shape, 0)
        place[...] = jnp.where(rows == slot_ref[...], 1.0, 0.0).astype(bf16)

    for k in range(len(sizes)):
        copy(step, k).wait()
    out_ref[...] = dot(place[...], held[step], ((1,), (0,))).astype(bf16)


def pick_rows(slot, pieces, rows, cols):
    sizes = [piece.shape[0] for piece in pieces]
    total = sum(sizes)
    block = tile(cols, 512)
    steps = cols // block
    return call(
        functools.partial(pick_kernel, sizes, block),
        2 * rows * total * cols,
        2 * (rows + total) * cols,
        grid=(steps,),
        in_specs=[whole(1, total)] + [pl.BlockSpec(memory_space=pl.ANY)] * len(pieces),
        out_specs=pl.BlockSpec((rows, block), lambda i: (0, i)),
        out_shape=jax.ShapeDtypeStruct((rows, cols), bf16),
        scratch_shapes=[
            pltpu.VMEM((steps, total, block), bf16),
            pltpu.VMEM((rows, total), bf16),
            pltpu.SemaphoreType.DMA((steps, len(sizes))),
        ],
    )(slot.reshape(1, total), *pieces)


def token_kernel(steps, spread, d_gate_ref, d_up_ref, slot_ref, route_ref, gate_ref, up_ref, *outs):
    step = pl.program_id(0)

    def store(part):
        if not spread:
            outs[0][...] = part
            return
        half = slot_ref.shape[0] // 2
        rows, width = part.shape
        for k in range(2):
            slot = slot_ref[k * half : (k + 1) * half, :]
            lanes = lax.broadcasted_iota(jnp.int32, (half, rows), 1)
            place = jnp.where(lanes == slot, 1.0, 0.0).astype(bf16)
            outs[k][:, :width] = dot(place, part, ((1,), (0,))).astype(bf16)

    @pl.when(step < steps)
    def _():
        part = dot(d_gate_ref[...], gate_ref[...], ((1,), (1,)))
        store((part + dot(d_up_ref[...], up_ref[...], ((1,), (1,)))).astype(bf16))

    if spread:

        @pl.when(step >= steps)
        def _():
            store(route_ref[...])


def token_grad(d_gate, d_up, slot, route, w_gate, w_up, chunk, chunks, spread):
    rows, units = d_gate.shape
    width = w_gate.shape[0] // chunks
    total = slot.shape[0]
    block = tile(width, 512)
    steps = width // block
    first = chunk * steps
    extra = route.shape[1] if spread and chunk == chunks - 1 else 0
    weight = pl.BlockSpec((block, units), lambda i: (first + jnp.minimum(i, steps - 1), 0))
    out_rows = [total // 2] * 2 if spread else [rows]
    return call(
        functools.partial(token_kernel, steps, spread),
        4 * rows * width * units + 2 * rows * width * total * spread,
        4 * width * units + 2 * total * width,
        grid=(steps + (extra > 0),),
        in_specs=[whole(rows, units), whole(rows, units), whole(total, 1), whole(*route.shape), weight, weight],
        out_specs=[pl.BlockSpec((n, block), lambda i: (0, i)) for n in out_rows],
        out_shape=[jax.ShapeDtypeStruct((n, width + extra), bf16) for n in out_rows],
    )(d_gate, d_up, slot.reshape(total, 1), route, w_gate, w_up)


def down_kernel(count, g_ref, gain_ref, *refs):
    turned, out_ref = refs[:count], refs[-1]
    scaled = (gain_ref[...] * g_ref[...].astype(f32)).astype(bf16)
    at = 0
    for ref in turned:
        out_ref[at : at + ref.shape[0], :] = dot(ref[...], scaled, ((1,), (0,))).astype(bf16)
        at += ref.shape[0]


def down_grad(turned, g, gain, chunk, chunks, into):
    rows, width = g.shape
    units = sum(part.shape[0] for part in turned)
    block = tile(width // chunks, 512)
    steps = width // chunks // block
    first = chunk * steps
    kept = [] if into is None else [into]
    return call(
        functools.partial(down_kernel, len(turned)),
        2 * rows * width * units // chunks,
        2 * width * units // chunks,
        grid=(steps,),
        in_specs=[pl.BlockSpec((rows, block), lambda i: (0, first + i)), whole(rows, 1)]
        + [whole(*part.shape) for part in turned]
        + [pl.BlockSpec(memory_space=pl.ANY)] * len(kept),
        out_specs=pl.BlockSpec((units, block), lambda i: (0, first + i)),
        out_shape=jax.ShapeDtypeStruct((units, width), bf16),
        input_output_aliases={2 + len(turned): 0} if kept else {},
    )(g, gain, *turned, *kept)


def body(tokens, grad_out, expert_ids, route_weights, w_gate, w_up, w_down):
    wide_count = lax.axis_size("wide")
    narrow_count = lax.axis_size("narrow")
    local_experts = w_gate.shape[0]
    experts_all = local_experts * wide_count
    tok_count, top_count = expert_ids.shape
    capacity = min(tok_count, 2 * tok_count * top_count // experts_all)
    rows = wide_count * capacity
    total = wide_count * tok_count
    cols = tokens.shape[1]
    me = lax.axis_index("wide")
    pad = -2 * top_count % LANES
    meta = jnp.concatenate(
        [expert_ids.astype(bf16), route_weights, jnp.zeros((tok_count, pad), bf16)], axis=1
    )
    tokens = jnp.concatenate([tokens, meta], axis=1)
    t_z = along_z(tokens)
    t_x, t_y = flip(tokens, X), flip(tokens, Y)
    g_x, g_y = flip(grad_out, X), flip(grad_out, Y)
    t_far, g_far = flip(t_y, X), flip(g_x, Y)
    t_rest = join(*t_z)
    g_z = along_z(after(grad_out, t_rest))
    t_xs, t_ys = flip(t_rest, X), flip(t_rest, Y)
    t_fars = far_corner(t_xs, t_ys)
    pieces = gather_core(
        [join(tokens, *t_z), join(t_x, t_xs), join(t_y, t_ys), join(t_far, *t_fars)]
    )
    g_z = lax.optimization_barrier((*g_z, *t_fars))[: len(g_z)]
    g_rest = join(*g_z)
    g_xs, g_ys = flip(g_rest, X), flip(g_rest, Y)
    all_meta = gather_meta(pieces, cols)
    all_ids = all_meta[:, :top_count].astype(jnp.int32)
    all_weights = all_meta[:, top_count : 2 * top_count].astype(f32)
    first = me * local_experts
    fused = narrow_count == 1 and local_experts == 1
    chunks = CHUNKS if fused else 1
    expert_cols = experts_all + -experts_all % LANES
    dense = [0, 0]
    ends = []
    picked = []
    for j in range(local_experts):
        match = all_ids == first + j
        chosen = jnp.any(match, axis=1)
        gain = jnp.sum(jnp.where(match, all_weights, 0.0), axis=1)
        rank = jnp.cumsum(chosen.astype(jnp.int32)) - 1
        slot = jnp.where(chosen, rank, -1)
        numbers = jnp.arange(rows, dtype=jnp.int32)[:, None]
        place = slot[None, :] == numbers
        row_gain = jnp.sum(jnp.where(place, gain[None, :], 0.0), axis=1, keepdims=True)
        x = pick_rows(slot, pieces, rows, cols)
        x = lax.all_gather(x, "narrow", axis=1, tiled=True)
        gate_pre = dot(x, w_gate[j], ((1,), (0,)))
        picked.append((slot, place, row_gain, x, gate_pre))
    g_xs, g_ys, *_ = lax.optimization_barrier((g_xs, g_ys, *[entry[4] for entry in picked]))
    g_fars = far_corner(g_xs, g_ys)
    ups = [
        dot(after(entry[3], g_xs, g_ys), w_up[j], ((1,), (0,))) for j, entry in enumerate(picked)
    ]
    *g_fars, _ = lax.optimization_barrier((*g_fars, ups[-1]))
    pieces_g = gather_core(
        [join(grad_out, *g_z), join(g_x, g_xs), join(g_y, g_ys), join(g_far, *g_fars)]
    )
    for j in range(local_experts):
        slot, place, row_gain, _, gate_pre = picked[j]
        up_pre = ups[j]
        active, slope = silu_parts(gate_pre)
        hidden = (active * up_pre).astype(bf16)
        turned = hidden.T
        g = pick_rows(slot, pieces_g, rows, cols)
        g = lax.all_gather(g, "narrow", axis=1, tiled=True)
        back = dot(g, w_down[j], ((1,), (1,)))
        d_hidden = row_gain * back
        d_gate = (d_hidden * up_pre * slope).astype(bf16)
        d_up = (d_hidden * active).astype(bf16)
        route = jnp.sum(hidden.astype(f32) * back, axis=1, keepdims=True)
        route = lax.psum(route.astype(bf16).astype(f32), "narrow")
        at = jnp.arange(expert_cols, dtype=jnp.int32) == first + j
        route = jnp.where(at[None, :], route, 0.0).astype(bf16)
        ends.append(([turned], g, row_gain))
        if fused:
            dense = token_grad(d_gate, d_up, slot, route, w_gate[j], w_up[j], 0, chunks, True)
            continue
        (part,) = token_grad(d_gate, d_up, slot, route, w_gate[j], w_up[j], 0, 1, False)
        part = lax.psum_scatter(part, "narrow", scatter_dimension=1, tiled=True)
        part = jnp.concatenate([part, route], axis=1)
        part = dot(place.astype(bf16), part, ((0,), (0,)))
        dense = [dense[0] + part[: total // 2], dense[1] + part[total // 2 :]]

    def send_far(mine):
        near, by_x, by_y, far = quarters(mine)
        half = far.shape[0] // 2
        return [near, by_x, by_y, flip(far[:half], X), flip(far[half:], Y)]

    def add_far(near, by_x, by_y, to_y, to_x):
        half = to_y.shape[0]
        by_y = jnp.concatenate([add(by_y[:half], to_y), by_y[half:]], axis=0)
        by_x = jnp.concatenate([by_x[:half], add(by_x[half:], to_x)], axis=0)
        return near, by_x, by_y

    def send_sides(near, by_x, by_y):
        return near, flip(by_x, X), flip(by_y, Y)

    mine = add(dense[0].astype(bf16), flip(dense[1].astype(bf16), CORE))
    sent = send_far(mine)
    if fused and chunks == 2:
        (turned, g, row_gain), = ends
        own, other = token_grad(after(d_gate, mine), d_up, slot, route, w_gate[0], w_up[0], 1, chunks, True)
        *_, to_y, to_x = sent
        to_y, to_x, own, other = lax.optimization_barrier((to_y, to_x, own, other))
        near, by_x, by_y = send_sides(*add_far(*sent[:3], to_y, to_x))
        mine = add(own, flip(other, CORE))
        sent = send_far(mine)
        out = down_grad(turned, after(g, mine), row_gain, 0, 2, None)
        *_, to_y, to_x = sent
        by_x, by_y, to_y, to_x, out = lax.optimization_barrier((by_x, by_y, to_y, to_x, out))
        first_near = add(near, by_x, by_y)
        sides = add_far(*sent[:3], to_y, to_x)
        near, by_x, by_y = send_sides(*sides)
        out = down_grad(turned, after(g, *sides, first_near), row_gain, 1, 2, out)
        by_x, by_y, out = lax.optimization_barrier((by_x, by_y, out))
        shares = [scatter_z(first_near), scatter_z(add(near, by_x, by_y))]
        grad_downs = [out]
    else:
        shares = [scatter_z(add(*send_sides(*add_far(*sent))))]
        grad_downs = [down_grad(*end, 0, 1, None) for end in ends]
    joined = jnp.concatenate(shares, axis=1)
    width = cols
    by_expert = joined[:, width : width + experts_all].astype(f32)
    pick = expert_ids[:, :, None] == jnp.arange(experts_all, dtype=jnp.int32)[None, None, :]
    grad_route = jnp.sum(jnp.where(pick, by_expert[:, None, :], 0.0), axis=2)
    return (joined[:, :width], grad_route.astype(bf16), jnp.stack(grad_downs))


def solution(mesh):
    in_specs = (
        P("wide", "narrow"),
        P("wide", "narrow"),
        P("wide", None),
        P("wide", None),
        P("wide", None, "narrow"),
        P("wide", None, "narrow"),
        P("wide", "narrow", None),
    )
    out_specs = (P("wide", "narrow"), P("wide", None), P("wide", "narrow", None))
    return jax.shard_map(body, mesh=mesh, in_specs=in_specs, out_specs=out_specs, check_vma=False)
```

```python
import functools

import jax
import jax.numpy as jnp
from jax import lax
from jax.experimental import pallas as pl
from jax.experimental.pallas import tpu as pltpu
from jax.sharding import PartitionSpec as P

LANES = 128
bf16, f32 = jnp.bfloat16, jnp.float32


def dot(a, b, dims):
    return lax.dot_general(a, b, ((dims[0], dims[1]), ((), ())), preferred_element_type=f32)


def add(*terms):
    total = terms[0].astype(f32)
    for term in terms[1:]:
        total = total + term.astype(f32)
    return total.astype(terms[0].dtype)


def tile(size, most):
    fits = [t for t in range(LANES, min(size, most) + 1, LANES) if size % t == 0]
    return fits[-1] if fits else size


def call(kernel, flops, moved, **kwargs):
    return pl.pallas_call(
        kernel,
        compiler_params=pltpu.CompilerParams(vmem_limit_bytes=60 * 1024 * 1024),
        cost_estimate=pl.CostEstimate(flops=flops, bytes_accessed=moved, transcendentals=0),
        **kwargs,
    )


def whole(*shape):
    return pl.BlockSpec(shape, lambda i: (0,) * len(shape))


CORE, X, Y, Z = 1, 2, 4, 8


def flip(value, mask):
    count = lax.axis_size("wide")
    return lax.ppermute(value, "wide", [(i, i ^ mask) for i in range(count)])


def after(value, *deps):
    return lax.optimization_barrier((value, *deps))[0]


def depth():
    return lax.axis_size("wide") // Z


def gather_z(shard):
    return jnp.concatenate([shard] + [flip(shard, Z * k) for k in range(1, depth())], axis=0)


def gather_sides(first):
    return flip(first, X), flip(first, Y)


def gather_far(by_x, by_y):
    half = by_x.shape[0] // 2
    return [flip(by_y[:half], X), flip(by_x[half:], Y)]


def gather_core(pieces):
    return pieces + [flip(piece, CORE) for piece in pieces]


def offsets():
    return [Z * k + m + c for c in (0, CORE) for m in (0, X, Y, X | Y) for k in range(depth())]


def quarters(mine):
    size = mine.shape[0] // 4
    return [mine[k * size : (k + 1) * size] for k in range(4)]


def send_z(first):
    step = first.shape[0] // depth()
    blocks = [first[k * step : (k + 1) * step] for k in range(depth())]
    return [blocks[0]] + [flip(blocks[k], Z * k) for k in range(1, depth())]


def meta_kernel(sizes, cols, *refs):
    pieces, (out_ref, sems) = refs[: len(sizes)], refs[len(sizes) :]
    starts = [sum(sizes[:k]) for k in range(len(sizes))]
    copies = [
        pltpu.make_async_copy(
            pieces[k].at[:, pl.ds(cols, LANES)], out_ref.at[pl.ds(starts[k], sizes[k]), :], sems.at[k]
        )
        for k in range(len(sizes))
    ]
    for copy in copies:
        copy.start()
    for copy in copies:
        copy.wait()


def gather_meta(pieces, cols):
    sizes = [piece.shape[0] for piece in pieces]
    return call(
        functools.partial(meta_kernel, sizes, cols),
        0,
        4 * sum(sizes) * LANES,
        grid=(1,),
        in_specs=[pl.BlockSpec(memory_space=pl.ANY)] * len(pieces),
        out_specs=whole(sum(sizes), LANES),
        out_shape=jax.ShapeDtypeStruct((sum(sizes), LANES), bf16),
        scratch_shapes=[pltpu.SemaphoreType.DMA((len(sizes),))],
    )(*pieces)


def pick_kernel(sizes, block, slot_ref, *refs):
    pieces, (out_ref, held, place, sems) = refs[: len(sizes)], refs[len(sizes) :]
    step = pl.program_id(0)
    starts = [sum(sizes[:k]) for k in range(len(sizes))]

    def copy(at, k):
        return pltpu.make_async_copy(
            pieces[k].at[:, pl.ds(pl.multiple_of(at * block, LANES), block)],
            held.at[at, pl.ds(starts[k], sizes[k]), :],
            sems.at[at, k],
        )

    def start(at):
        for k in range(len(sizes)):
            copy(at, k).start()

    @pl.when(step == 0)
    def _():
        start(0)
        rows = lax.broadcasted_iota(jnp.int32, place.shape, 0)
        place[...] = jnp.where(rows == slot_ref[...], 1.0, 0.0).astype(bf16)

    @pl.when(step + 1 < pl.num_programs(0))
    def _():
        start(step + 1)

    for k in range(len(sizes)):
        copy(step, k).wait()
    out_ref[...] = dot(place[...], held[step], ((1,), (0,))).astype(bf16)


def pick_rows(slot, pieces, rows, cols):
    sizes = [piece.shape[0] for piece in pieces]
    total = sum(sizes)
    block = tile(cols, 1024)
    steps = cols // block
    return call(
        functools.partial(pick_kernel, sizes, block),
        2 * rows * total * cols,
        2 * (rows + total) * cols,
        grid=(steps,),
        in_specs=[whole(1, total)] + [pl.BlockSpec(memory_space=pl.ANY)] * len(pieces),
        out_specs=pl.BlockSpec((rows, block), lambda i: (0, i)),
        out_shape=jax.ShapeDtypeStruct((rows, cols), bf16),
        scratch_shapes=[
            pltpu.VMEM((steps, total, block), bf16),
            pltpu.VMEM((rows, total), bf16),
            pltpu.SemaphoreType.DMA((steps, len(sizes))),
        ],
    )(slot.reshape(1, total), *pieces)


def forward_kernel(x_ref, gate_ref, up_ref, hidden_ref, turned_ref, active_ref, pull_ref):
    gate_pre = dot(x_ref[...], gate_ref[...], ((1,), (0,)))
    up_pre = dot(x_ref[...], up_ref[...], ((1,), (0,)))
    sig = jax.nn.sigmoid(gate_pre)
    active = gate_pre * sig
    hidden = active * up_pre
    hidden_ref[...] = hidden.astype(bf16)
    turned_ref[...] = hidden.T.astype(bf16)
    active_ref[...] = active.astype(bf16)
    pull_ref[...] = (up_pre * (sig * (1.0 + gate_pre * (1.0 - sig)))).astype(bf16)


def forward(x, w_gate, w_up, part, parts):
    rows, width = x.shape
    units = w_gate.shape[1] // parts
    block = tile(units, 256)
    first = part * (units // block)
    weight = pl.BlockSpec((width, block), lambda i: (0, first + i))
    unit = pl.BlockSpec((rows, block), lambda i: (0, i))
    turned = pl.BlockSpec((block, rows), lambda i: (i, 0))
    shape = jax.ShapeDtypeStruct((rows, units), bf16)
    return call(
        forward_kernel,
        4 * rows * width * units,
        4 * width * units,
        grid=(units // block,),
        in_specs=[whole(rows, width), weight, weight],
        out_specs=[unit, turned, unit, unit],
        out_shape=[shape, jax.ShapeDtypeStruct((units, rows), bf16), shape, shape],
    )(x, w_gate, w_up)


def back_kernel(steps, g_ref, gain_ref, down_ref, *refs):
    parts, (d_gate_ref, d_up_ref, route_ref) = refs[:-3], refs[-3:]
    step = pl.program_id(0)
    back = dot(g_ref[...], down_ref[...], ((1,), (1,)))
    d_hidden = gain_ref[...] * back

    @pl.when(step == 0)
    def _():
        route_ref[...] = jnp.zeros_like(route_ref)

    for k in range(len(parts) // 3):
        hidden_ref, active_ref, pull_ref = parts[3 * k : 3 * k + 3]

        @pl.when((step >= k * steps) & (step < (k + 1) * steps))
        def _(hidden_ref=hidden_ref, active_ref=active_ref, pull_ref=pull_ref):
            d_gate_ref[...] = (d_hidden * pull_ref[...].astype(f32)).astype(bf16)
            d_up_ref[...] = (d_hidden * active_ref[...].astype(f32)).astype(bf16)
            route_ref[...] += jnp.sum(hidden_ref[...].astype(f32) * back, axis=1, keepdims=True)


def back_project(g, gain, w_down, parts):
    rows, width = g.shape
    units = w_down.shape[0]
    block = tile(parts[0][0].shape[1], 768)
    steps = units // block // len(parts)
    unit = pl.BlockSpec((rows, block), lambda i: (0, i))

    def unit_of(part):
        return pl.BlockSpec((rows, block), lambda i: (0, jnp.clip(i - part * steps, 0, steps - 1)))

    shape = jax.ShapeDtypeStruct((rows, units), bf16)
    return call(
        functools.partial(back_kernel, steps),
        2 * rows * width * units,
        2 * width * units,
        grid=(units // block,),
        in_specs=[
            whole(rows, width),
            whole(rows, 1),
            pl.BlockSpec((block, width), lambda i: (i, 0)),
        ]
        + [unit_of(k) for k in range(len(parts)) for _ in range(3)],
        out_specs=[unit, unit, whole(rows, 1)],
        out_shape=[shape, shape, jax.ShapeDtypeStruct((rows, 1), f32)],
    )(g, gain, w_down, *[array for part in parts for array in part])


def token_kernel(steps, spread, d_gate_ref, d_up_ref, slot_ref, route_ref, gate_ref, up_ref, *outs):
    step = pl.program_id(0)

    def store(part):
        if not spread:
            outs[0][...] = part
            return
        half = slot_ref.shape[0] // 2
        rows, width = part.shape
        for k in range(2):
            slot = slot_ref[k * half : (k + 1) * half, :]
            lanes = lax.broadcasted_iota(jnp.int32, (half, rows), 1)
            place = jnp.where(lanes == slot, 1.0, 0.0).astype(bf16)
            outs[k][:, :width] = dot(place, part, ((1,), (0,))).astype(bf16)

    @pl.when(step < steps)
    def _():
        part = dot(d_gate_ref[...], gate_ref[...], ((1,), (1,)))
        store((part + dot(d_up_ref[...], up_ref[...], ((1,), (1,)))).astype(bf16))

    if spread:

        @pl.when(step >= steps)
        def _():
            store(route_ref[...])


def token_grad(d_gate, d_up, slot, route, w_gate, w_up, low, high, spread):
    rows, units = d_gate.shape
    width = high - low
    total = slot.shape[0]
    block = tile(w_gate.shape[0], 512)
    steps = width // block
    first = low // block
    extra = route.shape[1] if spread and high == w_gate.shape[0] else 0
    weight = pl.BlockSpec((block, units), lambda i: (first + jnp.minimum(i, steps - 1), 0))
    out_rows = [total // 2] * 2 if spread else [rows]
    return call(
        functools.partial(token_kernel, steps, spread),
        4 * rows * width * units + 2 * rows * width * total * spread,
        4 * width * units + 2 * total * width,
        grid=(steps + (extra > 0),),
        in_specs=[whole(rows, units), whole(rows, units), whole(total, 1), whole(*route.shape), weight, weight],
        out_specs=[pl.BlockSpec((n, block), lambda i: (0, i)) for n in out_rows],
        out_shape=[jax.ShapeDtypeStruct((n, width + extra), bf16) for n in out_rows],
    )(d_gate, d_up, slot.reshape(total, 1), route, w_gate, w_up)


def down_kernel(count, g_ref, gain_ref, *refs):
    turned, out_ref = refs[:count], refs[-1]
    scaled = (gain_ref[...] * g_ref[...].astype(f32)).astype(bf16)
    at = 0
    for ref in turned:
        out_ref[at : at + ref.shape[0], :] = dot(ref[...], scaled, ((1,), (0,))).astype(bf16)
        at += ref.shape[0]


def down_grad(turned, g, gain, chunk, chunks, into):
    rows, width = g.shape
    units = sum(part.shape[0] for part in turned)
    block = tile(width // chunks, 512)
    steps = width // chunks // block
    first = chunk * steps
    kept = [] if into is None else [into]
    return call(
        functools.partial(down_kernel, len(turned)),
        2 * rows * width * units // chunks,
        2 * width * units // chunks,
        grid=(steps,),
        in_specs=[pl.BlockSpec((rows, block), lambda i: (0, first + i)), whole(rows, 1)]
        + [whole(*part.shape) for part in turned]
        + [pl.BlockSpec(memory_space=pl.ANY)] * len(kept),
        out_specs=pl.BlockSpec((units, block), lambda i: (0, first + i)),
        out_shape=jax.ShapeDtypeStruct((units, width), bf16),
        input_output_aliases={2 + len(turned): 0} if kept else {},
    )(g, gain, *turned, *kept)


def body(tokens, grad_out, expert_ids, route_weights, w_gate, w_up, w_down):
    wide_count = lax.axis_size("wide")
    narrow_count = lax.axis_size("narrow")
    local_experts = w_gate.shape[0]
    experts_all = local_experts * wide_count
    tok_count, top_count = expert_ids.shape
    capacity = min(tok_count, 2 * tok_count * top_count // experts_all)
    rows = wide_count * capacity
    total = wide_count * tok_count
    cols = tokens.shape[1]
    me = lax.axis_index("wide")
    pad = -2 * top_count % LANES
    meta = jnp.concatenate(
        [expert_ids.astype(bf16), route_weights, jnp.zeros((tok_count, pad), bf16)], axis=1
    )
    first_t = gather_z(jnp.concatenate([tokens, meta], axis=1))
    t_x, t_y = gather_sides(first_t)
    first_g = gather_z(after(grad_out, first_t))
    t_far = gather_far(t_x, t_y)
    g_x, g_y = gather_sides(after(first_g, *t_far))
    pieces_t = gather_core([first_t, t_x, t_y] + t_far)
    all_meta = gather_meta(pieces_t, cols)
    all_ids = all_meta[:, :top_count].astype(jnp.int32)
    all_weights = all_meta[:, top_count : 2 * top_count].astype(f32)
    first = me * local_experts
    fused = narrow_count == 1 and local_experts == 1
    width = w_gate.shape[1]
    cut = width * 5 // 8
    parts = 2 if w_gate.shape[2] % (2 * LANES) == 0 else 1
    picked = []
    for j in range(local_experts):
        match = all_ids == first + j
        chosen = jnp.any(match, axis=1)
        gain = jnp.sum(jnp.where(match, all_weights, 0.0), axis=1)
        rank = jnp.cumsum(chosen.astype(jnp.int32)) - 1
        slot = jnp.where(chosen, rank, -1)
        place = slot[None, :] == jnp.arange(rows, dtype=jnp.int32)[:, None]
        row_gain = jnp.sum(jnp.where(place, gain[None, :], 0.0), axis=1, keepdims=True)
        x = pick_rows(slot, pieces_t, rows, cols)
        x = lax.all_gather(x, "narrow", axis=1, tiled=True)
        picked.append([slot, place, row_gain, x])
    for j in range(local_experts):
        picked[j].append([forward(picked[j][3], w_gate[j], w_up[j], 0, parts)])
    g_x, g_y, *_ = lax.optimization_barrier((g_x, g_y, *[entry[4][0][0] for entry in picked]))
    g_far = gather_far(g_x, g_y)
    for j in range(local_experts):
        if parts == 2:
            picked[j][4].append(forward(after(picked[j][3], g_x, g_y), w_gate[j], w_up[j], 1, parts))
    g_far = lax.optimization_barrier((*g_far, *[entry[4][-1][0] for entry in picked]))[: len(g_far)]
    pieces_g = gather_core([first_g, g_x, g_y, *g_far])
    expert_cols = experts_all + -experts_all % LANES
    dense = [0, 0]
    ends = []
    for j in range(local_experts):
        slot, place, row_gain, _, ahead = picked[j]
        g = pick_rows(slot, pieces_g, rows, cols)
        g = lax.all_gather(g, "narrow", axis=1, tiled=True)
        straight = [(hidden, active, pull) for hidden, _, active, pull in ahead]
        d_gate, d_up, route = back_project(g, row_gain, w_down[j], straight)
        route = lax.psum(route.astype(bf16).astype(f32), "narrow")
        at = jnp.arange(expert_cols, dtype=jnp.int32) == first + j
        route = jnp.where(at[None, :], route, 0.0).astype(bf16)
        ends.append(([part[1] for part in ahead], g, row_gain))
        if fused:
            dense = token_grad(d_gate, d_up, slot, route, w_gate[j], w_up[j], 0, cut, True)
            continue
        (part,) = token_grad(d_gate, d_up, slot, route, w_gate[j], w_up[j], 0, width, False)
        part = lax.psum_scatter(part, "narrow", scatter_dimension=1, tiled=True)
        part = jnp.concatenate([part, route], axis=1)
        part = dot(place.astype(bf16), part, ((0,), (0,)))
        dense = [dense[0] + part[: total // 2], dense[1] + part[total // 2 :]]

    def send_square(mine):
        near, by_x, by_y, far = quarters(mine)
        return [near, flip(by_x, X), flip(by_y, Y), flip(far, X | Y)]

    mine = add(dense[0].astype(bf16), flip(dense[1].astype(bf16), CORE))
    sent = send_square(mine)
    if fused:
        (turned, g, row_gain), = ends
        own, other = token_grad(after(d_gate, mine), d_up, slot, route, w_gate[0], w_up[0], cut, width, True)
        *sent, own = lax.optimization_barrier((*sent, own))
        mine = add(own, flip(other, CORE))
        near = add(*sent)
        sent = send_square(mine)
        out = down_grad(turned, after(g, near), row_gain, 0, 2, None)
        near, out = lax.optimization_barrier((near, out))
        share = send_z(near)
        *sent, share[1] = lax.optimization_barrier((*sent, share[1]))
        near_1 = add(*sent)
        out = down_grad(turned, after(g, near_1), row_gain, 1, 2, out)
        shares = [add(*share), add(*send_z(near_1))]
        grad_downs = [out]
    else:
        shares = [add(*send_z(add(*sent)))]
        grad_downs = [down_grad(*end, 0, 1, None) for end in ends]
    joined = jnp.concatenate(shares, axis=1)
    by_expert = joined[:, cols : cols + experts_all].astype(f32)
    pick = expert_ids[:, :, None] == jnp.arange(experts_all, dtype=jnp.int32)[None, None, :]
    grad_route = jnp.sum(jnp.where(pick, by_expert[:, None, :], 0.0), axis=2)
    return (joined[:, :cols], grad_route.astype(bf16), jnp.stack(grad_downs))


def solution(mesh):
    in_specs = (
        P("wide", "narrow"),
        P("wide", "narrow"),
        P("wide", None),
        P("wide", None),
        P("wide", None, "narrow"),
        P("wide", None, "narrow"),
        P("wide", "narrow", None),
    )
    out_specs = (P("wide", "narrow"), P("wide", None), P("wide", "narrow", None))
    return jax.shard_map(body, mesh=mesh, in_specs=in_specs, out_specs=out_specs, check_vma=False)
```

```python
import functools

import jax
import jax.numpy as jnp
from jax import lax
from jax.experimental import pallas as pl
from jax.experimental.pallas import tpu as pltpu
from jax.sharding import PartitionSpec as P

LANES = 128
CHUNKS = 2
bf16, f32 = jnp.bfloat16, jnp.float32


def dot(a, b, dims):
    return lax.dot_general(a, b, ((dims[0], dims[1]), ((), ())), preferred_element_type=f32)


def add(*terms):
    total = terms[0].astype(f32)
    for term in terms[1:]:
        total = total + term.astype(f32)
    return total.astype(terms[0].dtype)


def tile(size, most):
    fits = [t for t in range(LANES, min(size, most) + 1, LANES) if size % t == 0]
    return fits[-1] if fits else size


def call(kernel, flops, moved, **kwargs):
    return pl.pallas_call(
        kernel,
        compiler_params=pltpu.CompilerParams(vmem_limit_bytes=28 * 1024 * 1024),
        cost_estimate=pl.CostEstimate(flops=flops, bytes_accessed=moved, transcendentals=0),
        **kwargs,
    )


def whole(*shape):
    return pl.BlockSpec(shape, lambda i: (0,) * len(shape))


CORE, X, Y, Z = 1, 2, 4, 8


def flip(value, mask):
    count = lax.axis_size("wide")
    return lax.ppermute(value, "wide", [(i, i ^ mask) for i in range(count)])


def after(value, *deps):
    return lax.optimization_barrier((value, *deps))[0]


def depth():
    return lax.axis_size("wide") // Z


def gather_z(shard):
    return jnp.concatenate([shard] + [flip(shard, Z * k) for k in range(1, depth())], axis=0)


def gather_sides(first):
    return flip(first, X), flip(first, Y)


def gather_far(by_x, by_y):
    half = by_x.shape[0] // 2
    return [flip(by_y[:half], X), flip(by_x[half:], Y)]


def gather_core(pieces):
    return pieces + [flip(piece, CORE) for piece in pieces]


def offsets():
    return [Z * k + m + c for c in (0, CORE) for m in (0, X, Y, X | Y) for k in range(depth())]


def quarters(mine):
    size = mine.shape[0] // 4
    return [mine[k * size : (k + 1) * size] for k in range(4)]


def scatter_far(mine):
    first, by_x, by_y, far = quarters(mine)
    half = far.shape[0] // 2
    to_y, to_x = flip(far[:half], X), flip(far[half:], Y)
    by_y = jnp.concatenate([add(by_y[:half], to_y), by_y[half:]], axis=0)
    by_x = jnp.concatenate([by_x[:half], add(by_x[half:], to_x)], axis=0)
    return first, by_x, by_y


def scatter_sides(first, by_x, by_y):
    return add(first, flip(by_x, X), flip(by_y, Y))


def scatter_z(first):
    step = first.shape[0] // depth()
    blocks = [first[k * step : (k + 1) * step] for k in range(depth())]
    return add(blocks[0], *[flip(blocks[k], Z * k) for k in range(1, depth())])


def meta_kernel(sizes, cols, *refs):
    pieces, (out_ref, sems) = refs[: len(sizes)], refs[len(sizes) :]
    starts = [sum(sizes[:k]) for k in range(len(sizes))]
    copies = [
        pltpu.make_async_copy(
            pieces[k].at[:, pl.ds(cols, LANES)], out_ref.at[pl.ds(starts[k], sizes[k]), :], sems.at[k]
        )
        for k in range(len(sizes))
    ]
    for copy in copies:
        copy.start()
    for copy in copies:
        copy.wait()


def gather_meta(pieces, cols):
    sizes = [piece.shape[0] for piece in pieces]
    return call(
        functools.partial(meta_kernel, sizes, cols),
        0,
        4 * sum(sizes) * LANES,
        grid=(1,),
        in_specs=[pl.BlockSpec(memory_space=pl.ANY)] * len(pieces),
        out_specs=whole(sum(sizes), LANES),
        out_shape=jax.ShapeDtypeStruct((sum(sizes), LANES), bf16),
        scratch_shapes=[pltpu.SemaphoreType.DMA((len(sizes),))],
    )(*pieces)


def pick_kernel(sizes, block, slot_ref, *refs):
    pieces, (out_ref, held, place, sems) = refs[: len(sizes)], refs[len(sizes) :]
    step = pl.program_id(0)
    starts = [sum(sizes[:k]) for k in range(len(sizes))]

    def copy(at, k):
        return pltpu.make_async_copy(
            pieces[k].at[:, pl.ds(pl.multiple_of(at * block, LANES), block)],
            held.at[at, pl.ds(starts[k], sizes[k]), :],
            sems.at[at, k],
        )

    @pl.when(step == 0)
    def _():
        @pl.loop(0, pl.num_programs(0))
        def _(at):
            for k in range(len(sizes)):
                copy(at, k).start()

        rows = lax.broadcasted_iota(jnp.int32, place.shape, 0)
        place[...] = jnp.where(rows == slot_ref[...], 1.0, 0.0).astype(bf16)

    for k in range(len(sizes)):
        copy(step, k).wait()
    out_ref[...] = dot(place[...], held[step], ((1,), (0,))).astype(bf16)


def pick_rows(slot, pieces, rows, cols):
    sizes = [piece.shape[0] for piece in pieces]
    total = sum(sizes)
    block = tile(cols, 512)
    steps = cols // block
    return call(
        functools.partial(pick_kernel, sizes, block),
        2 * rows * total * cols,
        2 * (rows + total) * cols,
        grid=(steps,),
        in_specs=[whole(1, total)] + [pl.BlockSpec(memory_space=pl.ANY)] * len(pieces),
        out_specs=pl.BlockSpec((rows, block), lambda i: (0, i)),
        out_shape=jax.ShapeDtypeStruct((rows, cols), bf16),
        scratch_shapes=[
            pltpu.VMEM((steps, total, block), bf16),
            pltpu.VMEM((rows, total), bf16),
            pltpu.SemaphoreType.DMA((steps, len(sizes))),
        ],
    )(slot.reshape(1, total), *pieces)


def forward_kernel(x_ref, gate_ref, up_ref, hidden_ref, turned_ref, active_ref, pull_ref):
    gate_pre = dot(x_ref[...], gate_ref[...], ((1,), (0,)))
    up_pre = dot(x_ref[...], up_ref[...], ((1,), (0,)))
    sig = jax.nn.sigmoid(gate_pre)
    active = gate_pre * sig
    hidden = active * up_pre
    hidden_ref[...] = hidden.astype(bf16)
    turned_ref[...] = hidden.T.astype(bf16)
    active_ref[...] = active.astype(bf16)
    pull_ref[...] = (up_pre * (sig * (1.0 + gate_pre * (1.0 - sig)))).astype(bf16)


def forward(x, w_gate, w_up, part, parts):
    rows, width = x.shape
    units = w_gate.shape[1] // parts
    block = tile(units, 256)
    first = part * (units // block)
    weight = pl.BlockSpec((width, block), lambda i: (0, first + i))
    unit = pl.BlockSpec((rows, block), lambda i: (0, i))
    turned = pl.BlockSpec((block, rows), lambda i: (i, 0))
    shape = jax.ShapeDtypeStruct((rows, units), bf16)
    return call(
        forward_kernel,
        4 * rows * width * units,
        4 * width * units,
        grid=(units // block,),
        in_specs=[whole(rows, width), weight, weight],
        out_specs=[unit, turned, unit, unit],
        out_shape=[shape, jax.ShapeDtypeStruct((units, rows), bf16), shape, shape],
    )(x, w_gate, w_up)


def back_kernel(steps, g_ref, gain_ref, down_ref, *refs):
    parts, (d_gate_ref, d_up_ref, route_ref) = refs[:-3], refs[-3:]
    step = pl.program_id(0)
    back = dot(g_ref[...], down_ref[...], ((1,), (1,)))
    d_hidden = gain_ref[...] * back

    @pl.when(step == 0)
    def _():
        route_ref[...] = jnp.zeros_like(route_ref)

    for k in range(len(parts) // 3):
        hidden_ref, active_ref, pull_ref = parts[3 * k : 3 * k + 3]

        @pl.when((step >= k * steps) & (step < (k + 1) * steps))
        def _(hidden_ref=hidden_ref, active_ref=active_ref, pull_ref=pull_ref):
            d_gate_ref[...] = (d_hidden * pull_ref[...].astype(f32)).astype(bf16)
            d_up_ref[...] = (d_hidden * active_ref[...].astype(f32)).astype(bf16)
            route_ref[...] += jnp.sum(hidden_ref[...].astype(f32) * back, axis=1, keepdims=True)


def back_project(g, gain, w_down, parts):
    rows, width = g.shape
    units = w_down.shape[0]
    block = tile(parts[0][0].shape[1], 256)
    steps = units // block // len(parts)
    unit = pl.BlockSpec((rows, block), lambda i: (0, i))

    def unit_of(part):
        return pl.BlockSpec((rows, block), lambda i: (0, jnp.clip(i - part * steps, 0, steps - 1)))

    shape = jax.ShapeDtypeStruct((rows, units), bf16)
    return call(
        functools.partial(back_kernel, steps),
        2 * rows * width * units,
        2 * width * units,
        grid=(units // block,),
        in_specs=[
            whole(rows, width),
            whole(rows, 1),
            pl.BlockSpec((block, width), lambda i: (i, 0)),
        ]
        + [unit_of(k) for k in range(len(parts)) for _ in range(3)],
        out_specs=[unit, unit, whole(rows, 1)],
        out_shape=[shape, shape, jax.ShapeDtypeStruct((rows, 1), f32)],
    )(g, gain, w_down, *[array for part in parts for array in part])


def token_kernel(steps, spread, d_gate_ref, d_up_ref, slot_ref, route_ref, gate_ref, up_ref, *outs):
    step = pl.program_id(0)

    def store(part):
        if not spread:
            outs[0][...] = part
            return
        half = slot_ref.shape[0] // 2
        width = part.shape[1]
        for k in range(2):
            slot = slot_ref[k * half : (k + 1) * half, :]
            lanes = lax.broadcasted_iota(jnp.int32, (half, part.shape[0]), 1)
            place = jnp.where(lanes == slot, 1.0, 0.0).astype(bf16)
            outs[k][:, :width] = dot(place, part, ((1,), (0,))).astype(bf16)

    @pl.when(step < steps)
    def _():
        part = dot(d_gate_ref[...], gate_ref[...], ((1,), (1,)))
        store((part + dot(d_up_ref[...], up_ref[...], ((1,), (1,)))).astype(bf16))

    if spread:

        @pl.when(step >= steps)
        def _():
            store(route_ref[...])


def token_grad(d_gate, d_up, slot, route, w_gate, w_up, chunk, chunks, spread):
    rows, units = d_gate.shape
    width = w_gate.shape[0] // chunks
    total = slot.shape[0]
    block = tile(width, 512)
    steps = width // block
    first = chunk * steps
    extra = route.shape[1] if spread and chunk == chunks - 1 else 0
    weight = pl.BlockSpec((block, units), lambda i: (first + jnp.minimum(i, steps - 1), 0))
    out_rows = [total // 2] * 2 if spread else [rows]
    return call(
        functools.partial(token_kernel, steps, spread),
        4 * rows * width * units + 2 * rows * width * total * spread,
        4 * width * units + 2 * total * width,
        grid=(steps + (extra > 0),),
        in_specs=[whole(rows, units), whole(rows, units), whole(total, 1), whole(*route.shape), weight, weight],
        out_specs=[pl.BlockSpec((n, block), lambda i: (0, i)) for n in out_rows],
        out_shape=[jax.ShapeDtypeStruct((n, width + extra), bf16) for n in out_rows],
    )(d_gate, d_up, slot.reshape(total, 1), route, w_gate, w_up)


def down_kernel(count, g_ref, gain_ref, *refs):
    turned, out_ref = refs[:count], refs[-1]
    scaled = (gain_ref[...] * g_ref[...].astype(f32)).astype(bf16)
    at = 0
    for ref in turned:
        out_ref[at : at + ref.shape[0], :] = dot(ref[...], scaled, ((1,), (0,))).astype(bf16)
        at += ref.shape[0]


def down_grad(turned, g, gain, chunk, chunks, into):
    rows, width = g.shape
    units = sum(part.shape[0] for part in turned)
    block = tile(width // chunks, 512)
    steps = width // chunks // block
    first = chunk * steps
    kept = [] if into is None else [into]
    return call(
        functools.partial(down_kernel, len(turned)),
        2 * rows * width * units // chunks,
        2 * width * units // chunks,
        grid=(steps,),
        in_specs=[pl.BlockSpec((rows, block), lambda i: (0, first + i)), whole(rows, 1)]
        + [whole(*part.shape) for part in turned]
        + [pl.BlockSpec(memory_space=pl.ANY)] * len(kept),
        out_specs=pl.BlockSpec((units, block), lambda i: (0, first + i)),
        out_shape=jax.ShapeDtypeStruct((units, width), bf16),
        input_output_aliases={2 + len(turned): 0} if kept else {},
    )(g, gain, *turned, *kept)


def body(tokens, grad_out, expert_ids, route_weights, w_gate, w_up, w_down):
    wide_count = lax.axis_size("wide")
    narrow_count = lax.axis_size("narrow")
    local_experts = w_gate.shape[0]
    experts_all = local_experts * wide_count
    tok_count, top_count = expert_ids.shape
    capacity = min(tok_count, 2 * tok_count * top_count // experts_all)
    rows = wide_count * capacity
    total = wide_count * tok_count
    cols = tokens.shape[1]
    me = lax.axis_index("wide")
    pad = -2 * top_count % LANES
    meta = jnp.concatenate(
        [expert_ids.astype(bf16), route_weights, jnp.zeros((tok_count, pad), bf16)], axis=1
    )
    first_t = gather_z(jnp.concatenate([tokens, meta], axis=1))
    x_t, y_t = gather_sides(first_t)
    first_g = gather_z(after(grad_out, first_t))
    far_t = gather_far(x_t, y_t)
    x_g, y_g = gather_sides(after(first_g, *far_t))
    pieces_t = gather_core([first_t, x_t, y_t] + far_t)
    all_meta = gather_meta(pieces_t, cols)
    all_ids = all_meta[:, :top_count].astype(jnp.int32)
    all_weights = all_meta[:, top_count : 2 * top_count].astype(f32)
    first = me * local_experts
    fused = narrow_count == 1 and local_experts == 1
    chunks = CHUNKS if fused else 1
    units = w_gate.shape[2]
    parts = 2 if units % (2 * LANES) == 0 else 1
    picked = []
    for j in range(local_experts):
        match = all_ids == first + j
        chosen = jnp.any(match, axis=1)
        gain = jnp.sum(jnp.where(match, all_weights, 0.0), axis=1)
        rank = jnp.cumsum(chosen.astype(jnp.int32)) - 1
        slot = jnp.where(chosen, rank, -1)
        place = slot[None, :] == jnp.arange(rows, dtype=jnp.int32)[:, None]
        row_gain = jnp.sum(jnp.where(place, gain[None, :], 0.0), axis=1, keepdims=True)
        x = pick_rows(slot, pieces_t, rows, cols)
        x = lax.all_gather(x, "narrow", axis=1, tiled=True)
        ahead = [forward(x, w_gate[j], w_up[j], 0, parts)]
        picked.append((slot, place, row_gain, x, ahead))
    x_g, y_g, *_ = lax.optimization_barrier((x_g, y_g, *[ahead[0][0] for *_, ahead in picked]))
    far_g = gather_far(x_g, y_g)
    for j in range(local_experts):
        slot, place, row_gain, x, ahead = picked[j]
        if parts == 2:
            ahead.append(forward(after(x, x_g, y_g), w_gate[j], w_up[j], 1, parts))
    far_g = lax.optimization_barrier((*far_g, *[ahead[-1][0] for *_, ahead in picked]))[: len(far_g)]
    pieces_g = gather_core([first_g, x_g, y_g, *far_g])
    expert_cols = experts_all + -experts_all % LANES
    dense = [0, 0]
    route_all = 0
    ends = []
    for j in range(local_experts):
        slot, place, row_gain, x, ahead = picked[j]
        g = pick_rows(slot, pieces_g, rows, cols)
        g = lax.all_gather(g, "narrow", axis=1, tiled=True)
        straight = [(hidden, active, pull) for hidden, _, active, pull in ahead]
        d_gate, d_up, route = back_project(g, row_gain, w_down[j], straight)
        route = lax.psum(route.astype(bf16).astype(f32), "narrow")
        at = jnp.arange(expert_cols, dtype=jnp.int32) == first + j
        route = jnp.where(at[None, :], route, 0.0).astype(bf16)
        ends.append(([part[1] for part in ahead], g, row_gain))
        if fused:
            own, other = token_grad(d_gate, d_up, slot, route, w_gate[j], w_up[j], 0, chunks, True)
            dense = [own, other]
            continue
        (part,) = token_grad(d_gate, d_up, slot, route, w_gate[j], w_up[j], 0, 1, False)
        part = lax.psum_scatter(part, "narrow", scatter_dimension=1, tiled=True)
        part = jnp.concatenate([part, route], axis=1)
        part = dot(place.astype(bf16), part, ((0,), (0,)))
        dense = [dense[0] + part[: total // 2], dense[1] + part[total // 2 :]]
    mine = [add(dense[0].astype(bf16), flip(dense[1].astype(bf16), CORE))]
    if fused and chunks == 2:
        own, other = token_grad(after(d_gate, dense[0]), d_up, slot, route, w_gate[0], w_up[0], 1, chunks, True)
        mine[0] = add(after(dense[0], own), flip(dense[1], CORE))
        mine.append(add(own, flip(other, CORE)))
    sides = [scatter_far(rows_) for rows_ in mine]
    firsts = [scatter_sides(*side) for side in sides]
    shares = [scatter_z(first_) for first_ in firsts]
    gates = [mine[0], sides[0][1], firsts[0], firsts[-1]] if fused else [mine[0]]
    grad_downs = []
    for turned, g, row_gain in ends:
        out = None
        for k, gate in enumerate(gates):
            out = down_grad(turned, after(g, gate), row_gain, k, len(gates), out)
        grad_downs.append(out)
    joined = jnp.concatenate(shares, axis=1)
    width = tokens.shape[1]
    by_expert = joined[:, width : width + experts_all].astype(f32)
    pick = expert_ids[:, :, None] == jnp.arange(experts_all, dtype=jnp.int32)[None, None, :]
    grad_route = jnp.sum(jnp.where(pick, by_expert[:, None, :], 0.0), axis=2)
    return (joined[:, :width], grad_route.astype(bf16), jnp.stack(grad_downs))


def solution(mesh):
    in_specs = (
        P("wide", "narrow"),
        P("wide", "narrow"),
        P("wide", None),
        P("wide", None),
        P("wide", None, "narrow"),
        P("wide", None, "narrow"),
        P("wide", "narrow", None),
    )
    out_specs = (P("wide", "narrow"), P("wide", None), P("wide", "narrow", None))
    return jax.shard_map(body, mesh=mesh, in_specs=in_specs, out_specs=out_specs, check_vma=False)
```

```python
import functools

import jax
import jax.numpy as jnp
from jax import lax
from jax.experimental import pallas as pl
from jax.experimental.pallas import tpu as pltpu
from jax.sharding import PartitionSpec as P

LANES = 128
CHUNKS = 2
bf16, f32 = jnp.bfloat16, jnp.float32


def dot(a, b, dims):
    return lax.dot_general(a, b, ((dims[0], dims[1]), ((), ())), preferred_element_type=f32)


def add(*terms):
    total = terms[0].astype(f32)
    for term in terms[1:]:
        total = total + term.astype(f32)
    return total.astype(terms[0].dtype)


def tile(size, most):
    fits = [t for t in range(LANES, min(size, most) + 1, LANES) if size % t == 0]
    return fits[-1] if fits else size


def call(kernel, flops, moved, **kwargs):
    return pl.pallas_call(
        kernel,
        compiler_params=pltpu.CompilerParams(vmem_limit_bytes=52 * 1024 * 1024),
        cost_estimate=pl.CostEstimate(flops=flops, bytes_accessed=moved, transcendentals=0),
        **kwargs,
    )


def split(size, count, unit):
    return next(n for n in range(count, 0, -1) if size % (n * unit) == 0 or n == 1)


def columns(rows, width, count):
    return [pl.BlockSpec((rows, width // count), lambda i, q=q: (0, q)) for q in range(count)]


def whole(*shape):
    return pl.BlockSpec(shape, lambda i: (0,) * len(shape))


CORE, X, Y, Z = 1, 2, 4, 8


def flip(value, mask):
    count = lax.axis_size("wide")
    return lax.ppermute(value, "wide", [(i, i ^ mask) for i in range(count)])


def after(value, *deps):
    return lax.optimization_barrier((value, *deps))[0]


def depth():
    return lax.axis_size("wide") // Z


def gather_z(shard):
    return jnp.concatenate([shard] + [flip(shard, Z * k) for k in range(1, depth())], axis=0)


def gather_sides(first):
    return flip(first, X), flip(first, Y)


def gather_far(by_x, by_y):
    half = by_x.shape[0] // 2
    return [flip(by_y[:half], X), flip(by_x[half:], Y)]


def gather_core(pieces):
    return pieces + [flip(piece, CORE) for piece in pieces]


def offsets():
    return [Z * k + m + c for c in (0, CORE) for m in (0, X, Y, X | Y) for k in range(depth())]


def quarters(mine):
    size = mine.shape[0] // 4
    return [mine[k * size : (k + 1) * size] for k in range(4)]


def scatter_far(mine):
    first, by_x, by_y, far = quarters(mine)
    half = far.shape[0] // 2
    to_y, to_x = flip(far[:half], X), flip(far[half:], Y)
    by_y = jnp.concatenate([add(by_y[:half], to_y), by_y[half:]], axis=0)
    by_x = jnp.concatenate([by_x[:half], add(by_x[half:], to_x)], axis=0)
    return first, by_x, by_y


def scatter_sides(first, by_x, by_y):
    return add(first, flip(by_x, X), flip(by_y, Y))


def scatter_z(first):
    step = first.shape[0] // depth()
    blocks = [first[k * step : (k + 1) * step] for k in range(depth())]
    return add(blocks[0], *[flip(blocks[k], Z * k) for k in range(1, depth())])


def meta_kernel(sizes, cols, *refs):
    pieces, (out_ref, sems) = refs[: len(sizes)], refs[len(sizes) :]
    starts = [sum(sizes[:k]) for k in range(len(sizes))]
    copies = [
        pltpu.make_async_copy(
            pieces[k].at[:, pl.ds(cols, LANES)], out_ref.at[pl.ds(starts[k], sizes[k]), :], sems.at[k]
        )
        for k in range(len(sizes))
    ]
    for copy in copies:
        copy.start()
    for copy in copies:
        copy.wait()


def gather_meta(pieces, cols):
    sizes = [piece.shape[0] for piece in pieces]
    return call(
        functools.partial(meta_kernel, sizes, cols),
        0,
        4 * sum(sizes) * LANES,
        grid=(1,),
        in_specs=[pl.BlockSpec(memory_space=pl.ANY)] * len(pieces),
        out_specs=whole(sum(sizes), LANES),
        out_shape=jax.ShapeDtypeStruct((sum(sizes), LANES), bf16),
        scratch_shapes=[pltpu.SemaphoreType.DMA((len(sizes),))],
    )(*pieces)


def pick_kernel(sizes, block, slot_ref, *refs):
    pieces, (out_ref, held, place, sems) = refs[: len(sizes)], refs[len(sizes) :]
    step = pl.program_id(0)
    starts = [sum(sizes[:k]) for k in range(len(sizes))]

    def copy(at, k):
        return pltpu.make_async_copy(
            pieces[k].at[:, pl.ds(pl.multiple_of(at * block, LANES), block)],
            held.at[at, pl.ds(starts[k], sizes[k]), :],
            sems.at[at, k],
        )

    @pl.when(step == 0)
    def _():
        @pl.loop(0, pl.num_programs(0))
        def _(at):
            for k in range(len(sizes)):
                copy(at, k).start()

        rows = lax.broadcasted_iota(jnp.int32, place.shape, 0)
        place[...] = jnp.where(rows == slot_ref[...], 1.0, 0.0).astype(bf16)

    for k in range(len(sizes)):
        copy(step, k).wait()
    out_ref[...] = dot(place[...], held[step], ((1,), (0,))).astype(bf16)


def pick_rows(slot, pieces, rows, cols):
    sizes = [piece.shape[0] for piece in pieces]
    total = sum(sizes)
    block = tile(cols, 512)
    steps = cols // block
    return call(
        functools.partial(pick_kernel, sizes, block),
        2 * rows * total * cols,
        2 * (rows + total) * cols,
        grid=(steps,),
        in_specs=[whole(1, total)] + [pl.BlockSpec(memory_space=pl.ANY)] * len(pieces),
        out_specs=pl.BlockSpec((rows, block), lambda i: (0, i)),
        out_shape=jax.ShapeDtypeStruct((rows, cols), bf16),
        scratch_shapes=[
            pltpu.VMEM((steps, total, block), bf16),
            pltpu.VMEM((rows, total), bf16),
            pltpu.SemaphoreType.DMA((steps, len(sizes))),
        ],
    )(slot.reshape(1, total), *pieces)


def forward_kernel(count, *refs):
    x_refs, gate_refs, up_refs = refs[:count], refs[count : 2 * count], refs[2 * count : 3 * count]
    hidden_ref, turned_ref, active_ref, pull_ref = refs[3 * count :]
    gate_pre = sum(dot(x[...], w[...], ((1,), (0,))) for x, w in zip(x_refs, gate_refs))
    up_pre = sum(dot(x[...], w[...], ((1,), (0,))) for x, w in zip(x_refs, up_refs))
    sig = jax.nn.sigmoid(gate_pre)
    active = gate_pre * sig
    hidden = active * up_pre
    hidden_ref[...] = hidden.astype(bf16)
    turned_ref[...] = hidden.T.astype(bf16)
    active_ref[...] = active.astype(bf16)
    pull_ref[...] = (up_pre * (sig * (1.0 + gate_pre * (1.0 - sig)))).astype(bf16)


def forward(x, w_gate, w_up, part, parts):
    rows, width = x.shape
    units = w_gate.shape[1] // parts
    block = tile(units, 256)
    first = part * (units // block)
    count = split(width, 4, LANES)
    weights = [
        pl.BlockSpec((width // count, block), lambda i, q=q: (q, first + i)) for q in range(count)
    ]
    unit = pl.BlockSpec((rows, block), lambda i: (0, i))
    turned = pl.BlockSpec((block, rows), lambda i: (i, 0))
    shape = jax.ShapeDtypeStruct((rows, units), bf16)
    return call(
        functools.partial(forward_kernel, count),
        4 * rows * width * units,
        4 * width * units,
        grid=(units // block,),
        in_specs=columns(rows, width, count) + weights * 2,
        out_specs=[unit, turned, unit, unit],
        out_shape=[shape, jax.ShapeDtypeStruct((units, rows), bf16), shape, shape],
    )(*[x] * count, *[w_gate] * count, *[w_up] * count)


def back_kernel(steps, count, gain_ref, *refs):
    g_refs, down_refs, refs = refs[:count], refs[count : 2 * count], refs[2 * count :]
    parts, (d_gate_ref, d_up_ref, route_ref) = refs[:-3], refs[-3:]
    step = pl.program_id(0)
    back = sum(dot(g[...], w[...], ((1,), (1,))) for g, w in zip(g_refs, down_refs))
    d_hidden = gain_ref[...] * back

    @pl.when(step == 0)
    def _():
        route_ref[...] = jnp.zeros_like(route_ref)

    for k in range(len(parts) // 3):
        hidden_ref, active_ref, pull_ref = parts[3 * k : 3 * k + 3]

        @pl.when((step >= k * steps) & (step < (k + 1) * steps))
        def _(hidden_ref=hidden_ref, active_ref=active_ref, pull_ref=pull_ref):
            d_gate_ref[...] = (d_hidden * pull_ref[...].astype(f32)).astype(bf16)
            d_up_ref[...] = (d_hidden * active_ref[...].astype(f32)).astype(bf16)
            route_ref[...] += jnp.sum(hidden_ref[...].astype(f32) * back, axis=1, keepdims=True)


def back_project(g, gain, w_down, parts):
    rows, width = g.shape
    units = w_down.shape[0]
    block = tile(parts[0][0].shape[1], 256)
    steps = units // block // len(parts)
    unit = pl.BlockSpec((rows, block), lambda i: (0, i))

    def unit_of(part):
        return pl.BlockSpec((rows, block), lambda i: (0, jnp.clip(i - part * steps, 0, steps - 1)))

    count = split(width, 4, LANES)
    shape = jax.ShapeDtypeStruct((rows, units), bf16)
    return call(
        functools.partial(back_kernel, steps, count),
        2 * rows * width * units,
        2 * width * units,
        grid=(units // block,),
        in_specs=[whole(rows, 1)]
        + columns(rows, width, count)
        + [pl.BlockSpec((block, width // count), lambda i, q=q: (i, q)) for q in range(count)]
        + [unit_of(k) for k in range(len(parts)) for _ in range(3)],
        out_specs=[unit, unit, whole(rows, 1)],
        out_shape=[shape, shape, jax.ShapeDtypeStruct((rows, 1), f32)],
    )(gain, *[g] * count, *[w_down] * count, *[array for part in parts for array in part])


def token_kernel(steps, spread, count, d_gate_ref, d_up_ref, slot_ref, route_ref, *refs):
    gate_refs, up_refs, outs = refs[:count], refs[count : 2 * count], refs[2 * count :]
    step = pl.program_id(0)

    def store(part, low):
        if not spread:
            outs[0][:, low : low + part.shape[1]] = part
            return
        half = slot_ref.shape[0] // 2
        width = part.shape[1]
        for k in range(2):
            slot = slot_ref[k * half : (k + 1) * half, :]
            lanes = lax.broadcasted_iota(jnp.int32, (half, part.shape[0]), 1)
            place = jnp.where(lanes == slot, 1.0, 0.0).astype(bf16)
            outs[k][:, low : low + width] = dot(place, part, ((1,), (0,))).astype(bf16)

    @pl.when(step < steps)
    def _():
        low = 0
        for gate_ref, up_ref in zip(gate_refs, up_refs):
            part = dot(d_gate_ref[...], gate_ref[...], ((1,), (1,)))
            part = part + dot(d_up_ref[...], up_ref[...], ((1,), (1,)))
            store(part.astype(bf16), low)
            low += part.shape[1]

    if spread:

        @pl.when(step >= steps)
        def _():
            store(route_ref[...], 0)


def token_grad(d_gate, d_up, slot, route, w_gate, w_up, chunk, chunks, spread):
    rows, units = d_gate.shape
    width = w_gate.shape[0] // chunks
    total = slot.shape[0]
    block = tile(width, 512)
    steps = width // block
    first = chunk * steps
    extra = route.shape[1] if spread and chunk == chunks - 1 else 0
    count = split(block, 2, 2 * LANES)
    weights = [
        pl.BlockSpec(
            (block // count, units),
            lambda i, q=q: ((first + jnp.minimum(i, steps - 1)) * count + q, 0),
        )
        for q in range(count)
    ]
    out_rows = [total // 2] * 2 if spread else [rows]
    return call(
        functools.partial(token_kernel, steps, spread, count),
        4 * rows * width * units + 2 * rows * width * total * spread,
        4 * width * units + 2 * total * width,
        grid=(steps + (extra > 0),),
        in_specs=[whole(rows, units), whole(rows, units), whole(total, 1), whole(*route.shape)]
        + weights * 2,
        out_specs=[pl.BlockSpec((n, block), lambda i: (0, i)) for n in out_rows],
        out_shape=[jax.ShapeDtypeStruct((n, width + extra), bf16) for n in out_rows],
    )(d_gate, d_up, slot.reshape(total, 1), route, *[w_gate] * count, *[w_up] * count)


def down_kernel(count, first, block, ways, g_ref, gain_ref, *refs):
    turned, (out_ref, held, sems) = refs[:count], refs[-3:]
    step, steps = pl.program_id(0), pl.num_programs(0)
    size = held.shape[1] // ways

    def copies(at):
        target = pl.ds(pl.multiple_of((first + at) * block, LANES), block)
        return [
            pltpu.make_async_copy(
                held.at[at % 2, pl.ds(k * size, size), :],
                out_ref.at[pl.ds(k * size, size), target],
                sems.at[at % 2, k],
            )
            for k in range(ways)
        ]

    @pl.when(step >= 2)
    def _():
        for copy in copies(step - 2):
            copy.wait()

    scaled = (gain_ref[...] * g_ref[...].astype(f32)).astype(bf16)
    at = 0
    for ref in turned:
        held[step % 2, at : at + ref.shape[0], :] = dot(ref[...], scaled, ((1,), (0,))).astype(bf16)
        at += ref.shape[0]
    for copy in copies(step):
        copy.start()

    @pl.when(step == steps - 1)
    def _():
        @pl.when(steps > 1)
        def _():
            for copy in copies(step - 1):
                copy.wait()

        for copy in copies(step):
            copy.wait()


def down_grad(turned, g, gain, chunk, chunks, into):
    rows, width = g.shape
    units = sum(part.shape[0] for part in turned)
    block = tile(width // chunks, 512)
    steps = width // chunks // block
    first = chunk * steps
    ways = split(units, 6, 16)
    kept = [] if into is None else [into]
    return call(
        functools.partial(down_kernel, len(turned), first, block, ways),
        2 * rows * width * units // chunks,
        2 * width * units // chunks,
        grid=(steps,),
        in_specs=[pl.BlockSpec((rows, block), lambda i: (0, first + i)), whole(rows, 1)]
        + [whole(*part.shape) for part in turned]
        + [pl.BlockSpec(memory_space=pl.ANY)] * len(kept),
        out_specs=pl.BlockSpec(memory_space=pl.ANY),
        out_shape=jax.ShapeDtypeStruct((units, width), bf16),
        scratch_shapes=[pltpu.VMEM((2, units, block), bf16), pltpu.SemaphoreType.DMA((2, ways))],
        input_output_aliases={2 + len(turned): 0} if kept else {},
    )(g, gain, *turned, *kept)


def body(tokens, grad_out, expert_ids, route_weights, w_gate, w_up, w_down):
    wide_count = lax.axis_size("wide")
    narrow_count = lax.axis_size("narrow")
    local_experts = w_gate.shape[0]
    experts_all = local_experts * wide_count
    tok_count, top_count = expert_ids.shape
    capacity = min(tok_count, 2 * tok_count * top_count // experts_all)
    rows = wide_count * capacity
    total = wide_count * tok_count
    cols = tokens.shape[1]
    me = lax.axis_index("wide")
    pad = -2 * top_count % LANES
    meta = jnp.concatenate(
        [expert_ids.astype(bf16), route_weights, jnp.zeros((tok_count, pad), bf16)], axis=1
    )
    first_t = gather_z(jnp.concatenate([tokens, meta], axis=1))
    x_t, y_t = gather_sides(first_t)
    first_g = gather_z(after(grad_out, first_t))
    far_t = gather_far(x_t, y_t)
    x_g, y_g = gather_sides(after(first_g, *far_t))
    pieces_t = gather_core([first_t, x_t, y_t] + far_t)
    all_meta = gather_meta(pieces_t, cols)
    all_ids = all_meta[:, :top_count].astype(jnp.int32)
    all_weights = all_meta[:, top_count : 2 * top_count].astype(f32)
    first = me * local_experts
    fused = narrow_count == 1 and local_experts == 1
    chunks = CHUNKS if fused else 1
    units = w_gate.shape[2]
    parts = 2 if units % (2 * LANES) == 0 else 1
    picked = []
    for j in range(local_experts):
        match = all_ids == first + j
        chosen = jnp.any(match, axis=1)
        gain = jnp.sum(jnp.where(match, all_weights, 0.0), axis=1)
        rank = jnp.cumsum(chosen.astype(jnp.int32)) - 1
        slot = jnp.where(chosen, rank, -1)
        place = slot[None, :] == jnp.arange(rows, dtype=jnp.int32)[:, None]
        row_gain = jnp.sum(jnp.where(place, gain[None, :], 0.0), axis=1, keepdims=True)
        x = pick_rows(slot, pieces_t, rows, cols)
        x = lax.all_gather(x, "narrow", axis=1, tiled=True)
        ahead = [forward(x, w_gate[j], w_up[j], 0, parts)]
        picked.append((slot, place, row_gain, x, ahead))
    x_g, y_g, *_ = lax.optimization_barrier((x_g, y_g, *[ahead[0][0] for *_, ahead in picked]))
    far_g = gather_far(x_g, y_g)
    for j in range(local_experts):
        slot, place, row_gain, x, ahead = picked[j]
        if parts == 2:
            ahead.append(forward(after(x, x_g, y_g), w_gate[j], w_up[j], 1, parts))
    far_g = lax.optimization_barrier((*far_g, *[ahead[-1][0] for *_, ahead in picked]))[: len(far_g)]
    pieces_g = gather_core([first_g, x_g, y_g, *far_g])
    expert_cols = experts_all + -experts_all % LANES
    dense = [0, 0]
    route_all = 0
    ends = []
    for j in range(local_experts):
        slot, place, row_gain, x, ahead = picked[j]
        g = pick_rows(slot, pieces_g, rows, cols)
        g = lax.all_gather(g, "narrow", axis=1, tiled=True)
        straight = [(hidden, active, pull) for hidden, _, active, pull in ahead]
        d_gate, d_up, route = back_project(g, row_gain, w_down[j], straight)
        route = lax.psum(route.astype(bf16).astype(f32), "narrow")
        at = jnp.arange(expert_cols, dtype=jnp.int32) == first + j
        route = jnp.where(at[None, :], route, 0.0).astype(bf16)
        ends.append(([part[1] for part in ahead], g, row_gain))
        if fused:
            own, other = token_grad(d_gate, d_up, slot, route, w_gate[j], w_up[j], 0, chunks, True)
            dense = [own, other]
            continue
        (part,) = token_grad(d_gate, d_up, slot, route, w_gate[j], w_up[j], 0, 1, False)
        part = lax.psum_scatter(part, "narrow", scatter_dimension=1, tiled=True)
        part = jnp.concatenate([part, route], axis=1)
        part = dot(place.astype(bf16), part, ((0,), (0,)))
        dense = [dense[0] + part[: total // 2], dense[1] + part[total // 2 :]]
    mine = [add(dense[0].astype(bf16), flip(dense[1].astype(bf16), CORE))]
    if fused and chunks == 2:
        own, other = token_grad(after(d_gate, dense[0]), d_up, slot, route, w_gate[0], w_up[0], 1, chunks, True)
        mine[0] = add(after(dense[0], own), flip(dense[1], CORE))
        mine.append(add(own, flip(other, CORE)))
    sides = [scatter_far(rows_) for rows_ in mine]
    firsts = [scatter_sides(*side) for side in sides]
    shares = [scatter_z(first_) for first_ in firsts]
    gates = [mine[0], sides[0][1], firsts[0], firsts[-1]] if fused else [mine[0]]
    grad_downs = []
    for turned, g, row_gain in ends:
        out = None
        for k, gate in enumerate(gates):
            out = down_grad(turned, after(g, gate), row_gain, k, len(gates), out)
        grad_downs.append(out)
    joined = jnp.concatenate(shares, axis=1)
    width = tokens.shape[1]
    by_expert = joined[:, width : width + experts_all].astype(f32)
    pick = expert_ids[:, :, None] == jnp.arange(experts_all, dtype=jnp.int32)[None, None, :]
    grad_route = jnp.sum(jnp.where(pick, by_expert[:, None, :], 0.0), axis=2)
    return (joined[:, :width], grad_route.astype(bf16), jnp.stack(grad_downs))


def solution(mesh):
    in_specs = (
        P("wide", "narrow"),
        P("wide", "narrow"),
        P("wide", None),
        P("wide", None),
        P("wide", None, "narrow"),
        P("wide", None, "narrow"),
        P("wide", "narrow", None),
    )
    out_specs = (P("wide", "narrow"), P("wide", None), P("wide", "narrow", None))
    return jax.shard_map(body, mesh=mesh, in_specs=in_specs, out_specs=out_specs, check_vma=False)
```

```python
import functools

import jax
import jax.numpy as jnp
from jax import lax
from jax.experimental import pallas as pl
from jax.experimental.pallas import tpu as pltpu
from jax.sharding import PartitionSpec as P

LANES = 128
CHUNKS = 2
bf16, f32 = jnp.bfloat16, jnp.float32


def dot(a, b, dims):
    return lax.dot_general(a, b, ((dims[0], dims[1]), ((), ())), preferred_element_type=f32)


def add(*terms):
    total = terms[0].astype(f32)
    for term in terms[1:]:
        total = total + term.astype(f32)
    return total.astype(terms[0].dtype)


def tile(size, most):
    fits = [t for t in range(LANES, min(size, most) + 1, LANES) if size % t == 0]
    return fits[-1] if fits else size


def call(kernel, flops, moved, **kwargs):
    return pl.pallas_call(
        kernel,
        compiler_params=pltpu.CompilerParams(vmem_limit_bytes=52 * 1024 * 1024),
        cost_estimate=pl.CostEstimate(flops=flops, bytes_accessed=moved, transcendentals=0),
        **kwargs,
    )


ANY = pl.BlockSpec(memory_space=pl.ANY)


def held_blocks(steps, copies):
    step = pl.program_id(0)

    @pl.when(step == 0)
    def _():
        for at in range(steps):
            for copy in copies(at):
                copy.start()

    for at in range(steps):

        @pl.when(step == at)
        def _(at=at):
            for copy in copies(at):
                copy.wait()


def whole(*shape):
    return pl.BlockSpec(shape, lambda i: (0,) * len(shape))


CORE, X, Y, Z = 1, 2, 4, 8


def flip(value, mask):
    count = lax.axis_size("wide")
    return lax.ppermute(value, "wide", [(i, i ^ mask) for i in range(count)])


def after(value, *deps):
    return lax.optimization_barrier((value, *deps))[0]


def depth():
    return lax.axis_size("wide") // Z


def gather_z(shard):
    return jnp.concatenate([shard] + [flip(shard, Z * k) for k in range(1, depth())], axis=0)


def gather_sides(first):
    return flip(first, X), flip(first, Y)


def gather_far(by_x, by_y):
    half = by_x.shape[0] // 2
    return [flip(by_y[:half], X), flip(by_x[half:], Y)]


def gather_core(pieces):
    return pieces + [flip(piece, CORE) for piece in pieces]


def offsets():
    return [Z * k + m + c for c in (0, CORE) for m in (0, X, Y, X | Y) for k in range(depth())]


def quarters(mine):
    size = mine.shape[0] // 4
    return [mine[k * size : (k + 1) * size] for k in range(4)]


def scatter_far(mine):
    first, by_x, by_y, far = quarters(mine)
    half = far.shape[0] // 2
    to_y, to_x = flip(far[:half], X), flip(far[half:], Y)
    by_y = jnp.concatenate([add(by_y[:half], to_y), by_y[half:]], axis=0)
    by_x = jnp.concatenate([by_x[:half], add(by_x[half:], to_x)], axis=0)
    return first, by_x, by_y


def scatter_sides(first, by_x, by_y):
    return add(first, flip(by_x, X), flip(by_y, Y))


def scatter_z(first):
    step = first.shape[0] // depth()
    blocks = [first[k * step : (k + 1) * step] for k in range(depth())]
    return add(blocks[0], *[flip(blocks[k], Z * k) for k in range(1, depth())])


def meta_kernel(sizes, cols, *refs):
    pieces, (out_ref, sems) = refs[: len(sizes)], refs[len(sizes) :]
    starts = [sum(sizes[:k]) for k in range(len(sizes))]
    copies = [
        pltpu.make_async_copy(
            pieces[k].at[:, pl.ds(cols, LANES)], out_ref.at[pl.ds(starts[k], sizes[k]), :], sems.at[k]
        )
        for k in range(len(sizes))
    ]
    for copy in copies:
        copy.start()
    for copy in copies:
        copy.wait()


def gather_meta(pieces, cols):
    sizes = [piece.shape[0] for piece in pieces]
    return call(
        functools.partial(meta_kernel, sizes, cols),
        0,
        4 * sum(sizes) * LANES,
        grid=(1,),
        in_specs=[pl.BlockSpec(memory_space=pl.ANY)] * len(pieces),
        out_specs=whole(sum(sizes), LANES),
        out_shape=jax.ShapeDtypeStruct((sum(sizes), LANES), bf16),
        scratch_shapes=[pltpu.SemaphoreType.DMA((len(sizes),))],
    )(*pieces)


def pick_kernel(sizes, block, slot_ref, *refs):
    pieces, (out_ref, held, place, sems) = refs[: len(sizes)], refs[len(sizes) :]
    step = pl.program_id(0)
    starts = [sum(sizes[:k]) for k in range(len(sizes))]

    def copy(at, k):
        return pltpu.make_async_copy(
            pieces[k].at[:, pl.ds(pl.multiple_of(at * block, LANES), block)],
            held.at[at, pl.ds(starts[k], sizes[k]), :],
            sems.at[at, k],
        )

    @pl.when(step == 0)
    def _():
        @pl.loop(0, pl.num_programs(0))
        def _(at):
            for k in range(len(sizes)):
                copy(at, k).start()

        rows = lax.broadcasted_iota(jnp.int32, place.shape, 0)
        place[...] = jnp.where(rows == slot_ref[...], 1.0, 0.0).astype(bf16)

    for k in range(len(sizes)):
        copy(step, k).wait()
    out_ref[...] = dot(place[...], held[step], ((1,), (0,))).astype(bf16)


def pick_rows(slot, pieces, rows, cols):
    sizes = [piece.shape[0] for piece in pieces]
    total = sum(sizes)
    block = tile(cols, 512)
    steps = cols // block
    return call(
        functools.partial(pick_kernel, sizes, block),
        2 * rows * total * cols,
        2 * (rows + total) * cols,
        grid=(steps,),
        in_specs=[whole(1, total)] + [pl.BlockSpec(memory_space=pl.ANY)] * len(pieces),
        out_specs=pl.BlockSpec((rows, block), lambda i: (0, i)),
        out_shape=jax.ShapeDtypeStruct((rows, cols), bf16),
        scratch_shapes=[
            pltpu.VMEM((steps, total, block), bf16),
            pltpu.VMEM((rows, total), bf16),
            pltpu.SemaphoreType.DMA((steps, len(sizes))),
        ],
    )(slot.reshape(1, total), *pieces)


def forward_kernel(steps, first, *refs):
    x_any, gate_any, up_any, hidden_ref, turned_ref, active_ref, pull_ref, x, gates, ups, sems = refs
    block = gates.shape[2]

    def copies(at):
        source = pl.ds((first + at) * block, block)
        listed = [pltpu.make_async_copy(x_any, x, sems.at[2, 0])] if at == 0 else []
        return listed + [
            pltpu.make_async_copy(gate_any.at[:, source], gates.at[at], sems.at[0, at]),
            pltpu.make_async_copy(up_any.at[:, source], ups.at[at], sems.at[1, at]),
        ]

    held_blocks(steps, copies)
    step = pl.program_id(0)
    gate_pre = dot(x[...], gates[step], ((1,), (0,)))
    up_pre = dot(x[...], ups[step], ((1,), (0,)))
    sig = jax.nn.sigmoid(gate_pre)
    active = gate_pre * sig
    hidden = active * up_pre
    hidden_ref[...] = hidden.astype(bf16)
    turned_ref[...] = hidden.T.astype(bf16)
    active_ref[...] = active.astype(bf16)
    pull_ref[...] = (up_pre * (sig * (1.0 + gate_pre * (1.0 - sig)))).astype(bf16)


def forward(x, w_gate, w_up, part, parts):
    rows, width = x.shape
    units = w_gate.shape[1] // parts
    block = tile(units, 256)
    first = part * (units // block)
    steps = units // block
    unit = pl.BlockSpec((rows, block), lambda i: (0, i))
    turned = pl.BlockSpec((block, rows), lambda i: (i, 0))
    shape = jax.ShapeDtypeStruct((rows, units), bf16)
    return call(
        functools.partial(forward_kernel, steps, first),
        4 * rows * width * units,
        4 * width * units,
        grid=(steps,),
        in_specs=[ANY] * 3,
        out_specs=[unit, turned, unit, unit],
        out_shape=[shape, jax.ShapeDtypeStruct((units, rows), bf16), shape, shape],
        scratch_shapes=[pltpu.VMEM((rows, width), bf16)]
        + [pltpu.VMEM((steps, width, block), bf16)] * 2
        + [pltpu.SemaphoreType.DMA((3, steps))],
    )(x, w_gate, w_up)


def back_kernel(steps, g_any, gain_ref, down_any, *refs):
    parts, (d_gate_ref, d_up_ref, route_ref, g, downs, sems) = refs[:-6], refs[-6:]
    step = pl.program_id(0)
    block = downs.shape[1]

    def copies(at):
        listed = [pltpu.make_async_copy(g_any, g, sems.at[1, 0])] if at == 0 else []
        source = down_any.at[pl.ds(at * block, block), :]
        return listed + [pltpu.make_async_copy(source, downs.at[at], sems.at[0, at])]

    held_blocks(downs.shape[0], copies)
    back = dot(g[...], downs[step], ((1,), (1,)))
    d_hidden = gain_ref[...] * back

    @pl.when(step == 0)
    def _():
        route_ref[...] = jnp.zeros_like(route_ref)

    for k in range(len(parts) // 3):
        hidden_ref, active_ref, pull_ref = parts[3 * k : 3 * k + 3]

        @pl.when((step >= k * steps) & (step < (k + 1) * steps))
        def _(hidden_ref=hidden_ref, active_ref=active_ref, pull_ref=pull_ref):
            d_gate_ref[...] = (d_hidden * pull_ref[...].astype(f32)).astype(bf16)
            d_up_ref[...] = (d_hidden * active_ref[...].astype(f32)).astype(bf16)
            route_ref[...] += jnp.sum(hidden_ref[...].astype(f32) * back, axis=1, keepdims=True)


def back_project(g, gain, w_down, parts):
    rows, width = g.shape
    units = w_down.shape[0]
    block = tile(parts[0][0].shape[1], 256)
    steps = units // block // len(parts)
    unit = pl.BlockSpec((rows, block), lambda i: (0, i))

    def unit_of(part):
        return pl.BlockSpec((rows, block), lambda i: (0, jnp.clip(i - part * steps, 0, steps - 1)))

    shape = jax.ShapeDtypeStruct((rows, units), bf16)
    return call(
        functools.partial(back_kernel, steps),
        2 * rows * width * units,
        2 * width * units,
        grid=(units // block,),
        in_specs=[ANY, whole(rows, 1), ANY]
        + [unit_of(k) for k in range(len(parts)) for _ in range(3)],
        out_specs=[unit, unit, whole(rows, 1)],
        out_shape=[shape, shape, jax.ShapeDtypeStruct((rows, 1), f32)],
        scratch_shapes=[
            pltpu.VMEM((rows, width), bf16),
            pltpu.VMEM((units // block, block, width), bf16),
            pltpu.SemaphoreType.DMA((2, units // block)),
        ],
    )(g, gain, w_down, *[array for part in parts for array in part])


def token_kernel(steps, spread, first, d_gate_ref, d_up_ref, slot_ref, route_ref, gate_any, up_any, *refs):
    outs, (gates, ups, sems) = refs[:-3], refs[-3:]
    step = pl.program_id(0)
    block = gates.shape[1]

    def copies(at):
        source = pl.ds((first + at) * block, block)
        return [
            pltpu.make_async_copy(gate_any.at[source, :], gates.at[at], sems.at[0, at]),
            pltpu.make_async_copy(up_any.at[source, :], ups.at[at], sems.at[1, at]),
        ]

    held_blocks(steps, copies)

    def store(part):
        if not spread:
            outs[0][...] = part
            return
        half = slot_ref.shape[0] // 2
        width = part.shape[1]
        for k in range(2):
            slot = slot_ref[k * half : (k + 1) * half, :]
            lanes = lax.broadcasted_iota(jnp.int32, (half, part.shape[0]), 1)
            place = jnp.where(lanes == slot, 1.0, 0.0).astype(bf16)
            outs[k][:, :width] = dot(place, part, ((1,), (0,))).astype(bf16)

    @pl.when(step < steps)
    def _():
        at = jnp.minimum(step, steps - 1)
        part = dot(d_gate_ref[...], gates[at], ((1,), (1,)))
        store((part + dot(d_up_ref[...], ups[at], ((1,), (1,)))).astype(bf16))

    if spread:

        @pl.when(step >= steps)
        def _():
            store(route_ref[...])


def token_grad(d_gate, d_up, slot, route, w_gate, w_up, chunk, chunks, spread):
    rows, units = d_gate.shape
    width = w_gate.shape[0] // chunks
    total = slot.shape[0]
    block = tile(width, 512)
    steps = width // block
    first = chunk * steps
    extra = route.shape[1] if spread and chunk == chunks - 1 else 0
    out_rows = [total // 2] * 2 if spread else [rows]
    return call(
        functools.partial(token_kernel, steps, spread, first),
        4 * rows * width * units + 2 * rows * width * total * spread,
        4 * width * units + 2 * total * width,
        grid=(steps + (extra > 0),),
        in_specs=[whole(rows, units), whole(rows, units), whole(total, 1), whole(*route.shape), ANY, ANY],
        out_specs=[pl.BlockSpec((n, block), lambda i: (0, i)) for n in out_rows],
        out_shape=[jax.ShapeDtypeStruct((n, width + extra), bf16) for n in out_rows],
        scratch_shapes=[pltpu.VMEM((steps, block, units), bf16)] * 2
        + [pltpu.SemaphoreType.DMA((2, steps))],
    )(d_gate, d_up, slot.reshape(total, 1), route, w_gate, w_up)


def down_kernel(count, g_ref, gain_ref, *refs):
    turned, out_ref = refs[:count], refs[-1]
    scaled = (gain_ref[...] * g_ref[...].astype(f32)).astype(bf16)
    at = 0
    for ref in turned:
        out_ref[at : at + ref.shape[0], :] = dot(ref[...], scaled, ((1,), (0,))).astype(bf16)
        at += ref.shape[0]


def down_grad(turned, g, gain, chunk, chunks, into):
    rows, width = g.shape
    units = sum(part.shape[0] for part in turned)
    block = tile(width // chunks, 512)
    steps = width // chunks // block
    first = chunk * steps
    kept = [] if into is None else [into]
    return call(
        functools.partial(down_kernel, len(turned)),
        2 * rows * width * units // chunks,
        2 * width * units // chunks,
        grid=(steps,),
        in_specs=[pl.BlockSpec((rows, block), lambda i: (0, first + i)), whole(rows, 1)]
        + [whole(*part.shape) for part in turned]
        + [pl.BlockSpec(memory_space=pl.ANY)] * len(kept),
        out_specs=pl.BlockSpec((units, block), lambda i: (0, first + i)),
        out_shape=jax.ShapeDtypeStruct((units, width), bf16),
        input_output_aliases={2 + len(turned): 0} if kept else {},
    )(g, gain, *turned, *kept)


def body(tokens, grad_out, expert_ids, route_weights, w_gate, w_up, w_down):
    wide_count = lax.axis_size("wide")
    narrow_count = lax.axis_size("narrow")
    local_experts = w_gate.shape[0]
    experts_all = local_experts * wide_count
    tok_count, top_count = expert_ids.shape
    capacity = min(tok_count, 2 * tok_count * top_count // experts_all)
    rows = wide_count * capacity
    total = wide_count * tok_count
    cols = tokens.shape[1]
    me = lax.axis_index("wide")
    pad = -2 * top_count % LANES
    meta = jnp.concatenate(
        [expert_ids.astype(bf16), route_weights, jnp.zeros((tok_count, pad), bf16)], axis=1
    )
    first_t = gather_z(jnp.concatenate([tokens, meta], axis=1))
    x_t, y_t = gather_sides(first_t)
    first_g = gather_z(after(grad_out, first_t))
    far_t = gather_far(x_t, y_t)
    x_g, y_g = gather_sides(after(first_g, *far_t))
    pieces_t = gather_core([first_t, x_t, y_t] + far_t)
    all_meta = gather_meta(pieces_t, cols)
    all_ids = all_meta[:, :top_count].astype(jnp.int32)
    all_weights = all_meta[:, top_count : 2 * top_count].astype(f32)
    first = me * local_experts
    fused = narrow_count == 1 and local_experts == 1
    chunks = CHUNKS if fused else 1
    units = w_gate.shape[2]
    parts = 2 if units % (2 * LANES) == 0 else 1
    picked = []
    for j in range(local_experts):
        match = all_ids == first + j
        chosen = jnp.any(match, axis=1)
        gain = jnp.sum(jnp.where(match, all_weights, 0.0), axis=1)
        rank = jnp.cumsum(chosen.astype(jnp.int32)) - 1
        slot = jnp.where(chosen, rank, -1)
        place = slot[None, :] == jnp.arange(rows, dtype=jnp.int32)[:, None]
        row_gain = jnp.sum(jnp.where(place, gain[None, :], 0.0), axis=1, keepdims=True)
        x = pick_rows(slot, pieces_t, rows, cols)
        x = lax.all_gather(x, "narrow", axis=1, tiled=True)
        ahead = [forward(x, w_gate[j], w_up[j], 0, parts)]
        picked.append((slot, place, row_gain, x, ahead))
    x_g, y_g, *_ = lax.optimization_barrier((x_g, y_g, *[ahead[0][0] for *_, ahead in picked]))
    far_g = gather_far(x_g, y_g)
    for j in range(local_experts):
        slot, place, row_gain, x, ahead = picked[j]
        if parts == 2:
            ahead.append(forward(after(x, x_g, y_g), w_gate[j], w_up[j], 1, parts))
    far_g = lax.optimization_barrier((*far_g, *[ahead[-1][0] for *_, ahead in picked]))[: len(far_g)]
    pieces_g = gather_core([first_g, x_g, y_g, *far_g])
    expert_cols = experts_all + -experts_all % LANES
    dense = [0, 0]
    route_all = 0
    ends = []
    for j in range(local_experts):
        slot, place, row_gain, x, ahead = picked[j]
        g = pick_rows(slot, pieces_g, rows, cols)
        g = lax.all_gather(g, "narrow", axis=1, tiled=True)
        straight = [(hidden, active, pull) for hidden, _, active, pull in ahead]
        d_gate, d_up, route = back_project(g, row_gain, w_down[j], straight)
        route = lax.psum(route.astype(bf16).astype(f32), "narrow")
        at = jnp.arange(expert_cols, dtype=jnp.int32) == first + j
        route = jnp.where(at[None, :], route, 0.0).astype(bf16)
        ends.append(([part[1] for part in ahead], g, row_gain))
        if fused:
            own, other = token_grad(d_gate, d_up, slot, route, w_gate[j], w_up[j], 0, chunks, True)
            dense = [own, other]
            continue
        (part,) = token_grad(d_gate, d_up, slot, route, w_gate[j], w_up[j], 0, 1, False)
        part = lax.psum_scatter(part, "narrow", scatter_dimension=1, tiled=True)
        part = jnp.concatenate([part, route], axis=1)
        part = dot(place.astype(bf16), part, ((0,), (0,)))
        dense = [dense[0] + part[: total // 2], dense[1] + part[total // 2 :]]
    mine = [add(dense[0].astype(bf16), flip(dense[1].astype(bf16), CORE))]
    if fused and chunks == 2:
        own, other = token_grad(after(d_gate, dense[0]), d_up, slot, route, w_gate[0], w_up[0], 1, chunks, True)
        mine[0] = add(after(dense[0], own), flip(dense[1], CORE))
        mine.append(add(own, flip(other, CORE)))
    sides = [scatter_far(rows_) for rows_ in mine]
    firsts = [scatter_sides(*side) for side in sides]
    shares = [scatter_z(first_) for first_ in firsts]
    gates = [mine[0], sides[0][1], firsts[0], firsts[-1]] if fused else [mine[0]]
    grad_downs = []
    for turned, g, row_gain in ends:
        out = None
        for k, gate in enumerate(gates):
            out = down_grad(turned, after(g, gate), row_gain, k, len(gates), out)
        grad_downs.append(out)
    joined = jnp.concatenate(shares, axis=1)
    width = tokens.shape[1]
    by_expert = joined[:, width : width + experts_all].astype(f32)
    pick = expert_ids[:, :, None] == jnp.arange(experts_all, dtype=jnp.int32)[None, None, :]
    grad_route = jnp.sum(jnp.where(pick, by_expert[:, None, :], 0.0), axis=2)
    return (joined[:, :width], grad_route.astype(bf16), jnp.stack(grad_downs))


def solution(mesh):
    in_specs = (
        P("wide", "narrow"),
        P("wide", "narrow"),
        P("wide", None),
        P("wide", None),
        P("wide", None, "narrow"),
        P("wide", None, "narrow"),
        P("wide", "narrow", None),
    )
    out_specs = (P("wide", "narrow"), P("wide", None), P("wide", "narrow", None))
    return jax.shard_map(body, mesh=mesh, in_specs=in_specs, out_specs=out_specs, check_vma=False)
```

```python
import functools

import jax
import jax.numpy as jnp
from jax import lax
from jax.experimental import pallas as pl
from jax.experimental.pallas import tpu as pltpu
from jax.sharding import PartitionSpec as P

LANES = 128
CHUNKS = 2
bf16, f32 = jnp.bfloat16, jnp.float32


def dot(a, b, dims):
    return lax.dot_general(a, b, ((dims[0], dims[1]), ((), ())), preferred_element_type=f32)


def add(*terms):
    total = terms[0].astype(f32)
    for term in terms[1:]:
        total = total + term.astype(f32)
    return total.astype(terms[0].dtype)


def tile(size, most):
    fits = [t for t in range(LANES, min(size, most) + 1, LANES) if size % t == 0]
    return fits[-1] if fits else size


def call(kernel, flops, moved, **kwargs):
    return pl.pallas_call(
        kernel,
        compiler_params=pltpu.CompilerParams(vmem_limit_bytes=52 * 1024 * 1024),
        cost_estimate=pl.CostEstimate(flops=flops, bytes_accessed=moved, transcendentals=0),
        **kwargs,
    )


def whole(*shape):
    return pl.BlockSpec(shape, lambda i: (0,) * len(shape))


CORE, X, Y, Z = 1, 2, 4, 8


def flip(value, mask):
    count = lax.axis_size("wide")
    return lax.ppermute(value, "wide", [(i, i ^ mask) for i in range(count)])


def after(value, *deps):
    return lax.optimization_barrier((value, *deps))[0]


def depth():
    return lax.axis_size("wide") // Z


def gather_z(shard):
    return jnp.concatenate([shard] + [flip(shard, Z * k) for k in range(1, depth())], axis=0)


def gather_sides(first):
    return flip(first, X), flip(first, Y)


def gather_far(by_x, by_y):
    half = by_x.shape[0] // 2
    return [flip(by_y[:half], X), flip(by_x[half:], Y)]


def gather_core(pieces):
    return pieces + [flip(piece, CORE) for piece in pieces]


def offsets():
    return [Z * k + m + c for c in (0, CORE) for m in (0, X, Y, X | Y) for k in range(depth())]


def quarters(mine):
    size = mine.shape[0] // 4
    return [mine[k * size : (k + 1) * size] for k in range(4)]


def scatter_far(mine):
    first, by_x, by_y, far = quarters(mine)
    half = far.shape[0] // 2
    to_y, to_x = flip(far[:half], X), flip(far[half:], Y)
    by_y = jnp.concatenate([add(by_y[:half], to_y), by_y[half:]], axis=0)
    by_x = jnp.concatenate([by_x[:half], add(by_x[half:], to_x)], axis=0)
    return first, by_x, by_y


def scatter_sides(first, by_x, by_y):
    return add(first, flip(by_x, X), flip(by_y, Y))


def scatter_z(first):
    step = first.shape[0] // depth()
    blocks = [first[k * step : (k + 1) * step] for k in range(depth())]
    return add(blocks[0], *[flip(blocks[k], Z * k) for k in range(1, depth())])


def meta_kernel(sizes, cols, *refs):
    pieces, (out_ref, sems) = refs[: len(sizes)], refs[len(sizes) :]
    starts = [sum(sizes[:k]) for k in range(len(sizes))]
    copies = [
        pltpu.make_async_copy(
            pieces[k].at[:, pl.ds(cols, LANES)], out_ref.at[pl.ds(starts[k], sizes[k]), :], sems.at[k]
        )
        for k in range(len(sizes))
    ]
    for copy in copies:
        copy.start()
    for copy in copies:
        copy.wait()


def gather_meta(pieces, cols):
    sizes = [piece.shape[0] for piece in pieces]
    return call(
        functools.partial(meta_kernel, sizes, cols),
        0,
        4 * sum(sizes) * LANES,
        grid=(1,),
        in_specs=[pl.BlockSpec(memory_space=pl.ANY)] * len(pieces),
        out_specs=whole(sum(sizes), LANES),
        out_shape=jax.ShapeDtypeStruct((sum(sizes), LANES), bf16),
        scratch_shapes=[pltpu.SemaphoreType.DMA((len(sizes),))],
    )(*pieces)


def pick_kernel(sizes, block, slot_ref, *refs):
    pieces, (out_ref, held, place, sems) = refs[: len(sizes)], refs[len(sizes) :]
    step = pl.program_id(0)
    starts = [sum(sizes[:k]) for k in range(len(sizes))]

    def copy(at, k):
        return pltpu.make_async_copy(
            pieces[k].at[:, pl.ds(pl.multiple_of(at * block, LANES), block)],
            held.at[at, pl.ds(starts[k], sizes[k]), :],
            sems.at[at, k],
        )

    @pl.when(step == 0)
    def _():
        @pl.loop(0, pl.num_programs(0))
        def _(at):
            for k in range(len(sizes)):
                copy(at, k).start()

        rows = lax.broadcasted_iota(jnp.int32, place.shape, 0)
        place[...] = jnp.where(rows == slot_ref[...], 1.0, 0.0).astype(bf16)

    for k in range(len(sizes)):
        copy(step, k).wait()
    out_ref[...] = dot(place[...], held[step], ((1,), (0,))).astype(bf16)


def pick_rows(slot, pieces, rows, cols):
    sizes = [piece.shape[0] for piece in pieces]
    total = sum(sizes)
    block = tile(cols, 512)
    steps = cols // block
    return call(
        functools.partial(pick_kernel, sizes, block),
        2 * rows * total * cols,
        2 * (rows + total) * cols,
        grid=(steps,),
        in_specs=[whole(1, total)] + [pl.BlockSpec(memory_space=pl.ANY)] * len(pieces),
        out_specs=pl.BlockSpec((rows, block), lambda i: (0, i)),
        out_shape=jax.ShapeDtypeStruct((rows, cols), bf16),
        scratch_shapes=[
            pltpu.VMEM((steps, total, block), bf16),
            pltpu.VMEM((rows, total), bf16),
            pltpu.SemaphoreType.DMA((steps, len(sizes))),
        ],
    )(slot.reshape(1, total), *pieces)


def forward_kernel(x_ref, gate_ref, up_ref, hidden_ref, turned_ref, active_ref, pull_ref):
    gate_pre = dot(x_ref[...], gate_ref[...], ((1,), (0,)))
    up_pre = dot(x_ref[...], up_ref[...], ((1,), (0,)))
    sig = jax.nn.sigmoid(gate_pre)
    active = gate_pre * sig
    hidden = active * up_pre
    hidden_ref[...] = hidden.astype(bf16)
    turned_ref[...] = hidden.T.astype(bf16)
    active_ref[...] = active.astype(bf16)
    pull_ref[...] = (up_pre * (sig * (1.0 + gate_pre * (1.0 - sig)))).astype(bf16)


def forward(x, w_gate, w_up, part, parts):
    rows, width = x.shape
    units = w_gate.shape[1] // parts
    block = tile(units, 256)
    first = part * (units // block)
    weight = pl.BlockSpec((width, block), lambda i: (0, first + i))
    unit = pl.BlockSpec((rows, block), lambda i: (0, i))
    turned = pl.BlockSpec((block, rows), lambda i: (i, 0))
    shape = jax.ShapeDtypeStruct((rows, units), bf16)
    return call(
        forward_kernel,
        4 * rows * width * units,
        4 * width * units,
        grid=(units // block,),
        in_specs=[whole(rows, width), weight, weight],
        out_specs=[unit, turned, unit, unit],
        out_shape=[shape, jax.ShapeDtypeStruct((units, rows), bf16), shape, shape],
    )(x, w_gate, w_up)


def back_kernel(steps, g_ref, gain_ref, down_ref, *refs):
    parts, (d_gate_ref, d_up_ref, route_ref) = refs[:-3], refs[-3:]
    step = pl.program_id(0)
    back = dot(g_ref[...], down_ref[...], ((1,), (1,)))
    d_hidden = gain_ref[...] * back

    @pl.when(step == 0)
    def _():
        route_ref[...] = jnp.zeros_like(route_ref)

    for k in range(len(parts) // 3):
        hidden_ref, active_ref, pull_ref = parts[3 * k : 3 * k + 3]

        @pl.when((step >= k * steps) & (step < (k + 1) * steps))
        def _(hidden_ref=hidden_ref, active_ref=active_ref, pull_ref=pull_ref):
            d_gate_ref[...] = (d_hidden * pull_ref[...].astype(f32)).astype(bf16)
            d_up_ref[...] = (d_hidden * active_ref[...].astype(f32)).astype(bf16)
            route_ref[...] += jnp.sum(hidden_ref[...].astype(f32) * back, axis=1, keepdims=True)


def back_project(g, gain, w_down, parts):
    rows, width = g.shape
    units = w_down.shape[0]
    block = tile(parts[0][0].shape[1], 256)
    steps = units // block // len(parts)
    unit = pl.BlockSpec((rows, block), lambda i: (0, i))

    def unit_of(part):
        return pl.BlockSpec((rows, block), lambda i: (0, jnp.clip(i - part * steps, 0, steps - 1)))

    shape = jax.ShapeDtypeStruct((rows, units), bf16)
    return call(
        functools.partial(back_kernel, steps),
        2 * rows * width * units,
        2 * width * units,
        grid=(units // block,),
        in_specs=[
            whole(rows, width),
            whole(rows, 1),
            pl.BlockSpec((block, width), lambda i: (i, 0)),
        ]
        + [unit_of(k) for k in range(len(parts)) for _ in range(3)],
        out_specs=[unit, unit, whole(rows, 1)],
        out_shape=[shape, shape, jax.ShapeDtypeStruct((rows, 1), f32)],
    )(g, gain, w_down, *[array for part in parts for array in part])


ANY = pl.BlockSpec(memory_space=pl.ANY)


def pick_phase(sizes, picks, blocks, slot_ref, pieces, x_out, scratch, weights):
    held, place, x, piece_sems, x_sems = scratch
    step = pl.program_id(0)
    width = held.shape[2]
    starts = [sum(sizes[:k]) for k in range(len(sizes))]

    def columns(at):
        return pl.ds(pl.multiple_of(at * width, LANES), width)

    def loads(at):
        return [
            pltpu.make_async_copy(
                pieces[k].at[:, columns(at)],
                held.at[at, pl.ds(starts[k], sizes[k]), :],
                piece_sems.at[at, k],
            )
            for k in range(len(sizes))
        ]

    def store(at):
        return pltpu.make_async_copy(x.at[:, columns(at)], x_out.at[:, columns(at)], x_sems.at[at])

    @pl.when(step == 0)
    def _():
        for at in range(min(2, picks)):
            for copy in loads(at):
                copy.start()
        rows = lax.broadcasted_iota(jnp.int32, place.shape, 0)
        place[...] = jnp.where(rows == slot_ref[...], 1.0, 0.0).astype(bf16)

    @pl.when(step + 2 < picks)
    def _():
        for copy in loads(step + 2):
            copy.start()

    @pl.when((step >= 1) & (step <= blocks))
    def _():
        for copy in weights(step - 1):
            copy.start()

    @pl.when(step < picks)
    def _():
        for copy in loads(step):
            copy.wait()
        x[:, columns(step)] = dot(place[...], held[step], ((1,), (0,))).astype(bf16)
        store(step).start()

    @pl.when(step == picks + blocks - 1)
    def _():
        for at in range(picks):
            store(at).wait()

    return x


def pick_scratch(rows, sizes, cols):
    block = tile(cols, 1024)
    picks = cols // block
    return picks, [
        pltpu.VMEM((picks, sum(sizes), block), bf16),
        pltpu.VMEM((rows, sum(sizes)), bf16),
        pltpu.VMEM((rows, cols), bf16),
        pltpu.SemaphoreType.DMA((picks, len(sizes))),
        pltpu.SemaphoreType.DMA((picks,)),
    ]


def pick_forward_kernel(sizes, picks, blocks, slot_ref, *refs):
    count = len(sizes)
    pieces, (gate_any, up_any, x_out, hidden_ref, turned_ref, active_ref, pull_ref) = refs[:count], refs[count : count + 7]
    *scratch, gates, ups, sems = refs[count + 7 :]
    step = pl.program_id(0)
    width = gates.shape[2]

    def weights(at):
        source = pl.ds(pl.multiple_of(at * width, LANES), width)
        return [
            pltpu.make_async_copy(gate_any.at[:, source], gates.at[at], sems.at[0, at]),
            pltpu.make_async_copy(up_any.at[:, source], ups.at[at], sems.at[1, at]),
        ]

    x = pick_phase(sizes, picks, blocks, slot_ref, pieces, x_out, scratch, weights)

    @pl.when(step >= picks)
    def _():
        at = step - picks
        for copy in weights(at):
            copy.wait()
        forward_kernel(x, gates.at[at], ups.at[at], hidden_ref, turned_ref, active_ref, pull_ref)


def pick_forward(slot, pieces, rows, w_gate, w_up, parts):
    sizes = [piece.shape[0] for piece in pieces]
    cols, units = w_gate.shape[0], w_gate.shape[1] // parts
    picks, scratch = pick_scratch(rows, sizes, cols)
    block = tile(units, 256)
    blocks = units // block
    unit = pl.BlockSpec((rows, block), lambda i: (0, jnp.maximum(i - picks, 0)))
    turned = pl.BlockSpec((block, rows), lambda i: (jnp.maximum(i - picks, 0), 0))
    shape = jax.ShapeDtypeStruct((rows, units), bf16)
    x, *ahead = call(
        functools.partial(pick_forward_kernel, sizes, picks, blocks),
        4 * rows * cols * units + 2 * rows * sum(sizes) * cols,
        4 * cols * units + 2 * (rows + sum(sizes)) * cols,
        grid=(picks + blocks,),
        in_specs=[whole(1, sum(sizes))] + [ANY] * (len(sizes) + 2),
        out_specs=[ANY, unit, turned, unit, unit],
        out_shape=[
            jax.ShapeDtypeStruct((rows, cols), bf16),
            shape,
            jax.ShapeDtypeStruct((units, rows), bf16),
            shape,
            shape,
        ],
        scratch_shapes=scratch
        + [pltpu.VMEM((blocks, cols, block), bf16)] * 2
        + [pltpu.SemaphoreType.DMA((2, blocks))],
    )(slot.reshape(1, sum(sizes)), *pieces, w_gate, w_up)
    return x, ahead


def pick_back_kernel(sizes, picks, blocks, steps, slot_ref, gain_ref, *refs):
    count = len(sizes)
    pieces, down_any, refs = refs[:count], refs[count], refs[count + 1 :]
    *refs, held, place, rows_ref, piece_sems, x_sems, downs, sems = refs
    *parts, g_out, d_gate_ref, d_up_ref, route_ref = refs
    step = pl.program_id(0)
    width = downs.shape[1]

    def weights(at):
        source = down_any.at[pl.ds(pl.multiple_of(at * width, LANES), width), :]
        return [pltpu.make_async_copy(source, downs.at[at], sems.at[at])]

    scratch = (held, place, rows_ref, piece_sems, x_sems)
    g = pick_phase(sizes, picks, blocks, slot_ref, pieces, g_out, scratch, weights)

    @pl.when(step == 0)
    def _():
        route_ref[...] = jnp.zeros_like(route_ref)

    for k in range(len(parts) // 3):
        hidden_ref, active_ref, pull_ref = parts[3 * k : 3 * k + 3]

        @pl.when((step >= picks + k * steps) & (step < picks + (k + 1) * steps))
        def _(hidden_ref=hidden_ref, active_ref=active_ref, pull_ref=pull_ref):
            at = step - picks
            for copy in weights(at):
                copy.wait()
            back = dot(g[...], downs[at], ((1,), (1,)))
            d_hidden = gain_ref[...] * back
            d_gate_ref[...] = (d_hidden * pull_ref[...].astype(f32)).astype(bf16)
            d_up_ref[...] = (d_hidden * active_ref[...].astype(f32)).astype(bf16)
            route_ref[...] += jnp.sum(hidden_ref[...].astype(f32) * back, axis=1, keepdims=True)


def pick_back(slot, pieces, gain, w_down, parts):
    sizes = [piece.shape[0] for piece in pieces]
    rows = gain.shape[0]
    units, cols = w_down.shape
    picks, scratch = pick_scratch(rows, sizes, cols)
    block = tile(parts[0][0].shape[1], 256)
    blocks = units // block
    steps = blocks // len(parts)
    unit = pl.BlockSpec((rows, block), lambda i: (0, jnp.maximum(i - picks, 0)))

    def unit_of(part):
        return pl.BlockSpec((rows, block), lambda i: (0, jnp.clip(i - picks - part * steps, 0, steps - 1)))

    shape = jax.ShapeDtypeStruct((rows, units), bf16)
    return call(
        functools.partial(pick_back_kernel, sizes, picks, blocks, steps),
        2 * rows * cols * units + 2 * rows * sum(sizes) * cols,
        2 * cols * units + 2 * (rows + sum(sizes)) * cols,
        grid=(picks + blocks,),
        in_specs=[whole(1, sum(sizes)), whole(rows, 1)]
        + [ANY] * (len(sizes) + 1)
        + [unit_of(k) for k in range(len(parts)) for _ in range(3)],
        out_specs=[ANY, unit, unit, whole(rows, 1)],
        out_shape=[
            jax.ShapeDtypeStruct((rows, cols), bf16),
            shape,
            shape,
            jax.ShapeDtypeStruct((rows, 1), f32),
        ],
        scratch_shapes=scratch
        + [pltpu.VMEM((blocks, block, cols), bf16), pltpu.SemaphoreType.DMA((blocks,))],
    )(slot.reshape(1, sum(sizes)), gain, *pieces, w_down, *[array for part in parts for array in part])


def token_kernel(steps, spread, d_gate_ref, d_up_ref, slot_ref, route_ref, gate_ref, up_ref, *outs):
    step = pl.program_id(0)

    def store(part):
        if not spread:
            outs[0][...] = part
            return
        half = slot_ref.shape[0] // 2
        width = part.shape[1]
        for k in range(2):
            slot = slot_ref[k * half : (k + 1) * half, :]
            lanes = lax.broadcasted_iota(jnp.int32, (half, part.shape[0]), 1)
            place = jnp.where(lanes == slot, 1.0, 0.0).astype(bf16)
            outs[k][:, :width] = dot(place, part, ((1,), (0,))).astype(bf16)

    @pl.when(step < steps)
    def _():
        part = dot(d_gate_ref[...], gate_ref[...], ((1,), (1,)))
        store((part + dot(d_up_ref[...], up_ref[...], ((1,), (1,)))).astype(bf16))

    if spread:

        @pl.when(step >= steps)
        def _():
            store(route_ref[...])


def token_grad(d_gate, d_up, slot, route, w_gate, w_up, chunk, chunks, spread):
    rows, units = d_gate.shape
    width = w_gate.shape[0] // chunks
    total = slot.shape[0]
    block = tile(width, 512)
    steps = width // block
    first = chunk * steps
    extra = route.shape[1] if spread and chunk == chunks - 1 else 0
    weight = pl.BlockSpec((block, units), lambda i: (first + jnp.minimum(i, steps - 1), 0))
    out_rows = [total // 2] * 2 if spread else [rows]
    return call(
        functools.partial(token_kernel, steps, spread),
        4 * rows * width * units + 2 * rows * width * total * spread,
        4 * width * units + 2 * total * width,
        grid=(steps + (extra > 0),),
        in_specs=[whole(rows, units), whole(rows, units), whole(total, 1), whole(*route.shape), weight, weight],
        out_specs=[pl.BlockSpec((n, block), lambda i: (0, i)) for n in out_rows],
        out_shape=[jax.ShapeDtypeStruct((n, width + extra), bf16) for n in out_rows],
    )(d_gate, d_up, slot.reshape(total, 1), route, w_gate, w_up)


def down_kernel(count, g_ref, gain_ref, *refs):
    turned, out_ref = refs[:count], refs[-1]
    scaled = (gain_ref[...] * g_ref[...].astype(f32)).astype(bf16)
    at = 0
    for ref in turned:
        out_ref[at : at + ref.shape[0], :] = dot(ref[...], scaled, ((1,), (0,))).astype(bf16)
        at += ref.shape[0]


def down_grad(turned, g, gain, chunk, chunks, into):
    rows, width = g.shape
    units = sum(part.shape[0] for part in turned)
    block = tile(width // chunks, 512)
    steps = width // chunks // block
    first = chunk * steps
    kept = [] if into is None else [into]
    return call(
        functools.partial(down_kernel, len(turned)),
        2 * rows * width * units // chunks,
        2 * width * units // chunks,
        grid=(steps,),
        in_specs=[pl.BlockSpec((rows, block), lambda i: (0, first + i)), whole(rows, 1)]
        + [whole(*part.shape) for part in turned]
        + [pl.BlockSpec(memory_space=pl.ANY)] * len(kept),
        out_specs=pl.BlockSpec((units, block), lambda i: (0, first + i)),
        out_shape=jax.ShapeDtypeStruct((units, width), bf16),
        input_output_aliases={2 + len(turned): 0} if kept else {},
    )(g, gain, *turned, *kept)


def body(tokens, grad_out, expert_ids, route_weights, w_gate, w_up, w_down):
    wide_count = lax.axis_size("wide")
    narrow_count = lax.axis_size("narrow")
    local_experts = w_gate.shape[0]
    experts_all = local_experts * wide_count
    tok_count, top_count = expert_ids.shape
    capacity = min(tok_count, 2 * tok_count * top_count // experts_all)
    rows = wide_count * capacity
    total = wide_count * tok_count
    cols = tokens.shape[1]
    me = lax.axis_index("wide")
    pad = -2 * top_count % LANES
    meta = jnp.concatenate(
        [expert_ids.astype(bf16), route_weights, jnp.zeros((tok_count, pad), bf16)], axis=1
    )
    first_t = gather_z(jnp.concatenate([tokens, meta], axis=1))
    x_t, y_t = gather_sides(first_t)
    first_g = gather_z(after(grad_out, first_t))
    far_t = gather_far(x_t, y_t)
    x_g, y_g = gather_sides(after(first_g, *far_t))
    pieces_t = gather_core([first_t, x_t, y_t] + far_t)
    all_meta = gather_meta(pieces_t, cols)
    all_ids = all_meta[:, :top_count].astype(jnp.int32)
    all_weights = all_meta[:, top_count : 2 * top_count].astype(f32)
    first = me * local_experts
    fused = narrow_count == 1 and local_experts == 1
    chunks = CHUNKS if fused else 1
    units = w_gate.shape[2]
    parts = 2 if units % (2 * LANES) == 0 else 1
    picked = []
    for j in range(local_experts):
        match = all_ids == first + j
        chosen = jnp.any(match, axis=1)
        gain = jnp.sum(jnp.where(match, all_weights, 0.0), axis=1)
        rank = jnp.cumsum(chosen.astype(jnp.int32)) - 1
        slot = jnp.where(chosen, rank, -1)
        place = slot[None, :] == jnp.arange(rows, dtype=jnp.int32)[:, None]
        row_gain = jnp.sum(jnp.where(place, gain[None, :], 0.0), axis=1, keepdims=True)
        if fused:
            x, first_part = pick_forward(slot, pieces_t, rows, w_gate[j], w_up[j], parts)
        else:
            x = pick_rows(slot, pieces_t, rows, cols)
            x = lax.all_gather(x, "narrow", axis=1, tiled=True)
            first_part = forward(x, w_gate[j], w_up[j], 0, parts)
        ahead = [first_part]
        picked.append((slot, place, row_gain, x, ahead))
    x_g, y_g, *_ = lax.optimization_barrier((x_g, y_g, *[ahead[0][0] for *_, ahead in picked]))
    far_g = gather_far(x_g, y_g)
    for j in range(local_experts):
        slot, place, row_gain, x, ahead = picked[j]
        if parts == 2:
            ahead.append(forward(after(x, x_g, y_g), w_gate[j], w_up[j], 1, parts))
    far_g = lax.optimization_barrier((*far_g, *[ahead[-1][0] for *_, ahead in picked]))[: len(far_g)]
    pieces_g = gather_core([first_g, x_g, y_g, *far_g])
    expert_cols = experts_all + -experts_all % LANES
    dense = [0, 0]
    route_all = 0
    ends = []
    for j in range(local_experts):
        slot, place, row_gain, x, ahead = picked[j]
        straight = [(hidden, active, pull) for hidden, _, active, pull in ahead]
        if fused:
            g, d_gate, d_up, route = pick_back(slot, pieces_g, row_gain, w_down[j], straight)
        else:
            g = pick_rows(slot, pieces_g, rows, cols)
            g = lax.all_gather(g, "narrow", axis=1, tiled=True)
            d_gate, d_up, route = back_project(g, row_gain, w_down[j], straight)
        route = lax.psum(route.astype(bf16).astype(f32), "narrow")
        at = jnp.arange(expert_cols, dtype=jnp.int32) == first + j
        route = jnp.where(at[None, :], route, 0.0).astype(bf16)
        ends.append(([part[1] for part in ahead], g, row_gain))
        if fused:
            own, other = token_grad(d_gate, d_up, slot, route, w_gate[j], w_up[j], 0, chunks, True)
            dense = [own, other]
            continue
        (part,) = token_grad(d_gate, d_up, slot, route, w_gate[j], w_up[j], 0, 1, False)
        part = lax.psum_scatter(part, "narrow", scatter_dimension=1, tiled=True)
        part = jnp.concatenate([part, route], axis=1)
        part = dot(place.astype(bf16), part, ((0,), (0,)))
        dense = [dense[0] + part[: total // 2], dense[1] + part[total // 2 :]]
    mine = [add(dense[0].astype(bf16), flip(dense[1].astype(bf16), CORE))]
    if fused and chunks == 2:
        own, other = token_grad(after(d_gate, dense[0]), d_up, slot, route, w_gate[0], w_up[0], 1, chunks, True)
        mine[0] = add(after(dense[0], own), flip(dense[1], CORE))
        mine.append(add(own, flip(other, CORE)))
    sides = [scatter_far(rows_) for rows_ in mine]
    firsts = [scatter_sides(*side) for side in sides]
    shares = [scatter_z(first_) for first_ in firsts]
    gates = [mine[0], sides[0][1], firsts[0], firsts[-1]] if fused else [mine[0]]
    grad_downs = []
    for turned, g, row_gain in ends:
        out = None
        for k, gate in enumerate(gates):
            out = down_grad(turned, after(g, gate), row_gain, k, len(gates), out)
        grad_downs.append(out)
    joined = jnp.concatenate(shares, axis=1)
    width = tokens.shape[1]
    by_expert = joined[:, width : width + experts_all].astype(f32)
    pick = expert_ids[:, :, None] == jnp.arange(experts_all, dtype=jnp.int32)[None, None, :]
    grad_route = jnp.sum(jnp.where(pick, by_expert[:, None, :], 0.0), axis=2)
    return (joined[:, :width], grad_route.astype(bf16), jnp.stack(grad_downs))


def solution(mesh):
    in_specs = (
        P("wide", "narrow"),
        P("wide", "narrow"),
        P("wide", None),
        P("wide", None),
        P("wide", None, "narrow"),
        P("wide", None, "narrow"),
        P("wide", "narrow", None),
    )
    out_specs = (P("wide", "narrow"), P("wide", None), P("wide", "narrow", None))
    return jax.shard_map(body, mesh=mesh, in_specs=in_specs, out_specs=out_specs, check_vma=False)
```

```python
import functools

import jax
import jax.numpy as jnp
from jax import lax
from jax.experimental import pallas as pl
from jax.experimental.pallas import tpu as pltpu
from jax.sharding import PartitionSpec as P

LANES = 128
CHUNKS = 2
bf16, f32 = jnp.bfloat16, jnp.float32


def dot(a, b, dims):
    return lax.dot_general(a, b, ((dims[0], dims[1]), ((), ())), preferred_element_type=f32)


def add(*terms):
    total = terms[0].astype(f32)
    for term in terms[1:]:
        total = total + term.astype(f32)
    return total.astype(terms[0].dtype)


def tile(size, most):
    fits = [t for t in range(LANES, min(size, most) + 1, LANES) if size % t == 0]
    return fits[-1] if fits else size


def call(kernel, flops, moved, **kwargs):
    return pl.pallas_call(
        kernel,
        compiler_params=pltpu.CompilerParams(vmem_limit_bytes=52 * 1024 * 1024),
        cost_estimate=pl.CostEstimate(flops=flops, bytes_accessed=moved, transcendentals=0),
        **kwargs,
    )


def whole(*shape):
    return pl.BlockSpec(shape, lambda i: (0,) * len(shape))


CORE, X, Y, Z = 1, 2, 4, 8


def flip(value, mask):
    count = lax.axis_size("wide")
    return lax.ppermute(value, "wide", [(i, i ^ mask) for i in range(count)])


def after(value, *deps):
    return lax.optimization_barrier((value, *deps))[0]


def depth():
    return lax.axis_size("wide") // Z


def gather_z(shard):
    return jnp.concatenate([shard] + [flip(shard, Z * k) for k in range(1, depth())], axis=0)


def gather_sides(first):
    return flip(first, X), flip(first, Y)


def gather_far(by_x, by_y):
    half = by_x.shape[0] // 2
    return [flip(by_y[:half], X), flip(by_x[half:], Y)]


def gather_core(pieces):
    return pieces + [flip(piece, CORE) for piece in pieces]


def offsets():
    return [Z * k + m + c for c in (0, CORE) for m in (0, X, Y, X | Y) for k in range(depth())]


def quarters(mine):
    size = mine.shape[0] // 4
    return [mine[k * size : (k + 1) * size] for k in range(4)]


def scatter_far(mine):
    first, by_x, by_y, far = quarters(mine)
    half = far.shape[0] // 2
    to_y, to_x = flip(far[:half], X), flip(far[half:], Y)
    by_y = jnp.concatenate([add(by_y[:half], to_y), by_y[half:]], axis=0)
    by_x = jnp.concatenate([by_x[:half], add(by_x[half:], to_x)], axis=0)
    return first, by_x, by_y


def scatter_sides(first, by_x, by_y):
    return add(first, flip(by_x, X), flip(by_y, Y))


def scatter_z(first):
    step = first.shape[0] // depth()
    blocks = [first[k * step : (k + 1) * step] for k in range(depth())]
    return add(blocks[0], *[flip(blocks[k], Z * k) for k in range(1, depth())])


def meta_kernel(sizes, cols, *refs):
    pieces, (out_ref, sems) = refs[: len(sizes)], refs[len(sizes) :]
    starts = [sum(sizes[:k]) for k in range(len(sizes))]
    copies = [
        pltpu.make_async_copy(
            pieces[k].at[:, pl.ds(cols, LANES)], out_ref.at[pl.ds(starts[k], sizes[k]), :], sems.at[k]
        )
        for k in range(len(sizes))
    ]
    for copy in copies:
        copy.start()
    for copy in copies:
        copy.wait()


def gather_meta(pieces, cols):
    sizes = [piece.shape[0] for piece in pieces]
    return call(
        functools.partial(meta_kernel, sizes, cols),
        0,
        4 * sum(sizes) * LANES,
        grid=(1,),
        in_specs=[pl.BlockSpec(memory_space=pl.ANY)] * len(pieces),
        out_specs=whole(sum(sizes), LANES),
        out_shape=jax.ShapeDtypeStruct((sum(sizes), LANES), bf16),
        scratch_shapes=[pltpu.SemaphoreType.DMA((len(sizes),))],
    )(*pieces)


def pick_kernel(sizes, block, slot_ref, *refs):
    pieces, (out_ref, held, place, sems) = refs[: len(sizes)], refs[len(sizes) :]
    step = pl.program_id(0)
    starts = [sum(sizes[:k]) for k in range(len(sizes))]

    def copy(at, k):
        return pltpu.make_async_copy(
            pieces[k].at[:, pl.ds(pl.multiple_of(at * block, LANES), block)],
            held.at[at, pl.ds(starts[k], sizes[k]), :],
            sems.at[at, k],
        )

    @pl.when(step == 0)
    def _():
        @pl.loop(0, pl.num_programs(0))
        def _(at):
            for k in range(len(sizes)):
                copy(at, k).start()

        rows = lax.broadcasted_iota(jnp.int32, place.shape, 0)
        place[...] = jnp.where(rows == slot_ref[...], 1.0, 0.0).astype(bf16)

    for k in range(len(sizes)):
        copy(step, k).wait()
    out_ref[...] = dot(place[...], held[step], ((1,), (0,))).astype(bf16)


def pick_rows(slot, pieces, rows, cols):
    sizes = [piece.shape[0] for piece in pieces]
    total = sum(sizes)
    block = tile(cols, 512)
    steps = cols // block
    return call(
        functools.partial(pick_kernel, sizes, block),
        2 * rows * total * cols,
        2 * (rows + total) * cols,
        grid=(steps,),
        in_specs=[whole(1, total)] + [pl.BlockSpec(memory_space=pl.ANY)] * len(pieces),
        out_specs=pl.BlockSpec((rows, block), lambda i: (0, i)),
        out_shape=jax.ShapeDtypeStruct((rows, cols), bf16),
        scratch_shapes=[
            pltpu.VMEM((steps, total, block), bf16),
            pltpu.VMEM((rows, total), bf16),
            pltpu.SemaphoreType.DMA((steps, len(sizes))),
        ],
    )(slot.reshape(1, total), *pieces)


def forward_kernel(x_ref, gate_ref, up_ref, hidden_ref, turned_ref, active_ref, pull_ref):
    gate_pre = dot(x_ref[...], gate_ref[...], ((1,), (0,)))
    up_pre = dot(x_ref[...], up_ref[...], ((1,), (0,)))
    sig = jax.nn.sigmoid(gate_pre)
    active = gate_pre * sig
    hidden = active * up_pre
    hidden_ref[...] = hidden.astype(bf16)
    turned_ref[...] = hidden.T.astype(bf16)
    active_ref[...] = active.astype(bf16)
    pull_ref[...] = (up_pre * (sig * (1.0 + gate_pre * (1.0 - sig)))).astype(bf16)


def forward(x, w_gate, w_up, part, parts):
    rows, width = x.shape
    units = w_gate.shape[1] // parts
    block = tile(units, 256)
    first = part * (units // block)
    weight = pl.BlockSpec((width, block), lambda i: (0, first + i))
    unit = pl.BlockSpec((rows, block), lambda i: (0, i))
    turned = pl.BlockSpec((block, rows), lambda i: (i, 0))
    shape = jax.ShapeDtypeStruct((rows, units), bf16)
    return call(
        forward_kernel,
        4 * rows * width * units,
        4 * width * units,
        grid=(units // block,),
        in_specs=[whole(rows, width), weight, weight],
        out_specs=[unit, turned, unit, unit],
        out_shape=[shape, jax.ShapeDtypeStruct((units, rows), bf16), shape, shape],
    )(x, w_gate, w_up)


def back_kernel(steps, g_ref, gain_ref, down_ref, *refs):
    parts, (d_gate_ref, d_up_ref, route_ref) = refs[:-3], refs[-3:]
    step = pl.program_id(0)
    back = dot(g_ref[...], down_ref[...], ((1,), (1,)))
    d_hidden = gain_ref[...] * back

    @pl.when(step == 0)
    def _():
        route_ref[...] = jnp.zeros_like(route_ref)

    for k in range(len(parts) // 3):
        hidden_ref, active_ref, pull_ref = parts[3 * k : 3 * k + 3]

        @pl.when((step >= k * steps) & (step < (k + 1) * steps))
        def _(hidden_ref=hidden_ref, active_ref=active_ref, pull_ref=pull_ref):
            d_gate_ref[...] = (d_hidden * pull_ref[...].astype(f32)).astype(bf16)
            d_up_ref[...] = (d_hidden * active_ref[...].astype(f32)).astype(bf16)
            route_ref[...] += jnp.sum(hidden_ref[...].astype(f32) * back, axis=1, keepdims=True)


def back_project(g, gain, w_down, parts):
    rows, width = g.shape
    units = w_down.shape[0]
    block = tile(parts[0][0].shape[1], 256)
    steps = units // block // len(parts)
    unit = pl.BlockSpec((rows, block), lambda i: (0, i))

    def unit_of(part):
        return pl.BlockSpec((rows, block), lambda i: (0, jnp.clip(i - part * steps, 0, steps - 1)))

    shape = jax.ShapeDtypeStruct((rows, units), bf16)
    return call(
        functools.partial(back_kernel, steps),
        2 * rows * width * units,
        2 * width * units,
        grid=(units // block,),
        in_specs=[
            whole(rows, width),
            whole(rows, 1),
            pl.BlockSpec((block, width), lambda i: (i, 0)),
        ]
        + [unit_of(k) for k in range(len(parts)) for _ in range(3)],
        out_specs=[unit, unit, whole(rows, 1)],
        out_shape=[shape, shape, jax.ShapeDtypeStruct((rows, 1), f32)],
    )(g, gain, w_down, *[array for part in parts for array in part])


ANY = pl.BlockSpec(memory_space=pl.ANY)


def pick_phase(sizes, picks, slot_ref, pieces, x_out, scratch, start_weights):
    held, place, x, piece_sems, x_sems = scratch
    step = pl.program_id(0)
    width = held.shape[2]
    starts = [sum(sizes[:k]) for k in range(len(sizes))]

    def columns(at):
        return pl.ds(pl.multiple_of(at * width, LANES), width)

    def loads(at):
        return [
            pltpu.make_async_copy(
                pieces[k].at[:, columns(at)],
                held.at[at, pl.ds(starts[k], sizes[k]), :],
                piece_sems.at[at, k],
            )
            for k in range(len(sizes))
        ]

    def store(at):
        return pltpu.make_async_copy(x.at[:, columns(at)], x_out.at[:, columns(at)], x_sems.at[at])

    @pl.when(step == 0)
    def _():
        for at in range(min(2, picks)):
            for copy in loads(at):
                copy.start()
        rows = lax.broadcasted_iota(jnp.int32, place.shape, 0)
        place[...] = jnp.where(rows == slot_ref[...], 1.0, 0.0).astype(bf16)

    @pl.when(step + 2 < picks)
    def _():
        for copy in loads(step + 2):
            copy.start()

    @pl.when(step >= 1)
    def _():
        start_weights(step - 1)

    @pl.when(step < picks)
    def _():
        for copy in loads(step):
            copy.wait()
        x[:, columns(step)] = dot(place[...], held[step], ((1,), (0,))).astype(bf16)
        store(step).start()

    @pl.when(step == pl.num_programs(0) - 1)
    def _():
        for at in range(picks):
            store(at).wait()

    return x


def pick_scratch(rows, sizes, cols):
    block = tile(cols, 1024)
    picks = cols // block
    return picks, [
        pltpu.VMEM((picks, sum(sizes), block), bf16),
        pltpu.VMEM((rows, sum(sizes)), bf16),
        pltpu.VMEM((rows, cols), bf16),
        pltpu.SemaphoreType.DMA((picks, len(sizes))),
        pltpu.SemaphoreType.DMA((picks,)),
    ]


def pick_forward_kernel(sizes, picks, blocks, slot_ref, *refs):
    count = len(sizes)
    pieces, (gate_any, up_any, x_out, hidden_ref, turned_ref, active_ref, pull_ref) = refs[:count], refs[count : count + 7]
    *scratch, gates, ups, sems = refs[count + 7 :]
    step = pl.program_id(0)
    width = gates.shape[2]

    def weights(at):
        source = pl.ds(pl.multiple_of(at * width, LANES), width)
        return [
            pltpu.make_async_copy(gate_any.at[:, source], gates.at[at], sems.at[0, at]),
            pltpu.make_async_copy(up_any.at[:, source], ups.at[at], sems.at[1, at]),
        ]

    def start_weights(at):
        @pl.when(at < blocks)
        def _():
            for copy in weights(at):
                copy.start()

    x = pick_phase(sizes, picks, slot_ref, pieces, x_out, scratch, start_weights)

    @pl.when(step >= picks)
    def _():
        at = step - picks
        for copy in weights(at):
            copy.wait()
        forward_kernel(x, gates.at[at], ups.at[at], hidden_ref, turned_ref, active_ref, pull_ref)


def pick_forward(slot, pieces, rows, w_gate, w_up, parts):
    sizes = [piece.shape[0] for piece in pieces]
    cols, units = w_gate.shape[0], w_gate.shape[1] // parts
    picks, scratch = pick_scratch(rows, sizes, cols)
    block = tile(units, 256)
    blocks = units // block
    unit = pl.BlockSpec((rows, block), lambda i: (0, jnp.maximum(i - picks, 0)))
    turned = pl.BlockSpec((block, rows), lambda i: (jnp.maximum(i - picks, 0), 0))
    shape = jax.ShapeDtypeStruct((rows, units), bf16)
    x, *ahead = call(
        functools.partial(pick_forward_kernel, sizes, picks, blocks),
        4 * rows * cols * units + 2 * rows * sum(sizes) * cols,
        4 * cols * units + 2 * (rows + sum(sizes)) * cols,
        grid=(picks + blocks,),
        in_specs=[whole(1, sum(sizes))] + [ANY] * (len(sizes) + 2),
        out_specs=[ANY, unit, turned, unit, unit],
        out_shape=[
            jax.ShapeDtypeStruct((rows, cols), bf16),
            shape,
            jax.ShapeDtypeStruct((units, rows), bf16),
            shape,
            shape,
        ],
        scratch_shapes=scratch
        + [pltpu.VMEM((blocks, cols, block), bf16)] * 2
        + [pltpu.SemaphoreType.DMA((2, blocks))],
    )(slot.reshape(1, sum(sizes)), *pieces, w_gate, w_up)
    return x, ahead


def pick_back_kernel(sizes, picks, blocks, steps, tokens, slot_ref, slot_col, gain_ref, *refs):
    count = len(sizes)
    pieces, (down_any, gate_any, up_any), refs = refs[:count], refs[count : count + 3], refs[count + 3 :]
    *refs, held, place, rows_ref, piece_sems, x_sems, downs, gates, ups, d_gate, d_up, sems, token_sems = refs
    *parts, g_out, d_gate_ref, d_up_ref, route_ref, own_ref, other_ref = refs
    step = pl.program_id(0)
    width, token_width = downs.shape[1], gates.shape[1]

    def weights(at):
        source = down_any.at[pl.ds(pl.multiple_of(at * width, LANES), width), :]
        return [pltpu.make_async_copy(source, downs.at[at], sems.at[at])]

    def token_weights(at):
        source = pl.ds(pl.multiple_of(at * token_width, LANES), token_width)
        return [
            pltpu.make_async_copy(gate_any.at[source, :], gates.at[at], token_sems.at[0, at]),
            pltpu.make_async_copy(up_any.at[source, :], ups.at[at], token_sems.at[1, at]),
        ]

    def start_weights(at):
        @pl.when(at < blocks)
        def _():
            for copy in weights(at):
                copy.start()

        @pl.when((at >= blocks) & (at < blocks + tokens))
        def _():
            for copy in token_weights(at - blocks):
                copy.start()

    scratch = (held, place, rows_ref, piece_sems, x_sems)
    g = pick_phase(sizes, picks, slot_ref, pieces, g_out, scratch, start_weights)

    @pl.when(step == 0)
    def _():
        route_ref[...] = jnp.zeros_like(route_ref)

    for k in range(len(parts) // 3):
        hidden_ref, active_ref, pull_ref = parts[3 * k : 3 * k + 3]

        @pl.when((step >= picks + k * steps) & (step < picks + (k + 1) * steps))
        def _(hidden_ref=hidden_ref, active_ref=active_ref, pull_ref=pull_ref):
            at = step - picks
            for copy in weights(at):
                copy.wait()
            back = dot(g[...], downs[at], ((1,), (1,)))
            d_hidden = gain_ref[...] * back
            units = pl.ds(pl.multiple_of(at * width, LANES), width)
            d_gate_ref[...] = (d_hidden * pull_ref[...].astype(f32)).astype(bf16)
            d_up_ref[...] = (d_hidden * active_ref[...].astype(f32)).astype(bf16)
            d_gate[:, units] = d_gate_ref[...]
            d_up[:, units] = d_up_ref[...]
            route_ref[...] += jnp.sum(hidden_ref[...].astype(f32) * back, axis=1, keepdims=True)

    @pl.when(step >= picks + blocks)
    def _():
        at = step - picks - blocks
        for copy in token_weights(at):
            copy.wait()
        part = dot(d_gate[...], gates[at], ((1,), (1,)))
        part = (part + dot(d_up[...], ups[at], ((1,), (1,)))).astype(bf16)
        spread_rows(slot_col, part, (own_ref, other_ref))


def pick_back(slot, pieces, gain, w_down, w_gate, w_up, parts, high):
    sizes = [piece.shape[0] for piece in pieces]
    total = sum(sizes)
    rows = gain.shape[0]
    units, cols = w_down.shape
    picks, scratch = pick_scratch(rows, sizes, cols)
    block = tile(parts[0][0].shape[1], 256)
    blocks = units // block
    steps = blocks // len(parts)
    token_block = tile(cols, 512)
    tokens = high // token_block
    unit = pl.BlockSpec((rows, block), lambda i: (0, jnp.clip(i - picks, 0, blocks - 1)))
    dense = pl.BlockSpec((total // 2, token_block), lambda i: (0, jnp.maximum(i - picks - blocks, 0)))

    def unit_of(part):
        return pl.BlockSpec((rows, block), lambda i: (0, jnp.clip(i - picks - part * steps, 0, steps - 1)))

    shape = jax.ShapeDtypeStruct((rows, units), bf16)
    return call(
        functools.partial(pick_back_kernel, sizes, picks, blocks, steps, tokens),
        2 * rows * (cols * units + total * cols + 2 * high * units + total * high),
        2 * cols * units + 4 * high * units + 2 * (rows + total) * cols,
        grid=(picks + blocks + tokens,),
        in_specs=[whole(1, total), whole(total, 1), whole(rows, 1)]
        + [ANY] * (len(sizes) + 3)
        + [unit_of(k) for k in range(len(parts)) for _ in range(3)],
        out_specs=[ANY, unit, unit, whole(rows, 1), dense, dense],
        out_shape=[
            jax.ShapeDtypeStruct((rows, cols), bf16),
            shape,
            shape,
            jax.ShapeDtypeStruct((rows, 1), f32),
        ]
        + [jax.ShapeDtypeStruct((total // 2, high), bf16)] * 2,
        scratch_shapes=scratch
        + [pltpu.VMEM((blocks, block, cols), bf16)]
        + [pltpu.VMEM((tokens, token_block, units), bf16)] * 2
        + [pltpu.VMEM((rows, units), bf16)] * 2
        + [pltpu.SemaphoreType.DMA((blocks,)), pltpu.SemaphoreType.DMA((2, tokens))],
    )(
        slot.reshape(1, total),
        slot.reshape(total, 1),
        gain,
        *pieces,
        w_down,
        w_gate,
        w_up,
        *[array for part in parts for array in part],
    )


def spread_rows(slot_ref, part, outs):
    half = slot_ref.shape[0] // 2
    rows, width = part.shape
    for k in range(2):
        slot = slot_ref[k * half : (k + 1) * half, :]
        lanes = lax.broadcasted_iota(jnp.int32, (half, rows), 1)
        place = jnp.where(lanes == slot, 1.0, 0.0).astype(bf16)
        outs[k][:, :width] = dot(place, part, ((1,), (0,))).astype(bf16)


def token_kernel(steps, spread, d_gate_ref, d_up_ref, slot_ref, route_ref, gate_ref, up_ref, *outs):
    step = pl.program_id(0)

    def store(part):
        if spread:
            spread_rows(slot_ref, part, outs)
        else:
            outs[0][...] = part

    @pl.when(step < steps)
    def _():
        part = dot(d_gate_ref[...], gate_ref[...], ((1,), (1,)))
        store((part + dot(d_up_ref[...], up_ref[...], ((1,), (1,)))).astype(bf16))

    if spread:

        @pl.when(step >= steps)
        def _():
            store(route_ref[...])


def token_grad(d_gate, d_up, slot, route, w_gate, w_up, chunk, chunks, spread):
    rows, units = d_gate.shape
    width = w_gate.shape[0] // chunks
    total = slot.shape[0]
    block = tile(width, 512)
    steps = width // block
    first = chunk * steps
    extra = route.shape[1] if spread and chunk == chunks - 1 else 0
    weight = pl.BlockSpec((block, units), lambda i: (first + jnp.minimum(i, steps - 1), 0))
    out_rows = [total // 2] * 2 if spread else [rows]
    return call(
        functools.partial(token_kernel, steps, spread),
        4 * rows * width * units + 2 * rows * width * total * spread,
        4 * width * units + 2 * total * width,
        grid=(steps + (extra > 0),),
        in_specs=[whole(rows, units), whole(rows, units), whole(total, 1), whole(*route.shape), weight, weight],
        out_specs=[pl.BlockSpec((n, block), lambda i: (0, i)) for n in out_rows],
        out_shape=[jax.ShapeDtypeStruct((n, width + extra), bf16) for n in out_rows],
    )(d_gate, d_up, slot.reshape(total, 1), route, w_gate, w_up)


def down_kernel(count, g_ref, gain_ref, *refs):
    turned, out_ref = refs[:count], refs[-1]
    scaled = (gain_ref[...] * g_ref[...].astype(f32)).astype(bf16)
    at = 0
    for ref in turned:
        out_ref[at : at + ref.shape[0], :] = dot(ref[...], scaled, ((1,), (0,))).astype(bf16)
        at += ref.shape[0]


def down_grad(turned, g, gain, chunk, chunks, into):
    rows, width = g.shape
    units = sum(part.shape[0] for part in turned)
    block = tile(width // chunks, 512)
    steps = width // chunks // block
    first = chunk * steps
    kept = [] if into is None else [into]
    return call(
        functools.partial(down_kernel, len(turned)),
        2 * rows * width * units // chunks,
        2 * width * units // chunks,
        grid=(steps,),
        in_specs=[pl.BlockSpec((rows, block), lambda i: (0, first + i)), whole(rows, 1)]
        + [whole(*part.shape) for part in turned]
        + [pl.BlockSpec(memory_space=pl.ANY)] * len(kept),
        out_specs=pl.BlockSpec((units, block), lambda i: (0, first + i)),
        out_shape=jax.ShapeDtypeStruct((units, width), bf16),
        input_output_aliases={2 + len(turned): 0} if kept else {},
    )(g, gain, *turned, *kept)


def body(tokens, grad_out, expert_ids, route_weights, w_gate, w_up, w_down):
    wide_count = lax.axis_size("wide")
    narrow_count = lax.axis_size("narrow")
    local_experts = w_gate.shape[0]
    experts_all = local_experts * wide_count
    tok_count, top_count = expert_ids.shape
    capacity = min(tok_count, 2 * tok_count * top_count // experts_all)
    rows = wide_count * capacity
    total = wide_count * tok_count
    cols = tokens.shape[1]
    me = lax.axis_index("wide")
    pad = -2 * top_count % LANES
    meta = jnp.concatenate(
        [expert_ids.astype(bf16), route_weights, jnp.zeros((tok_count, pad), bf16)], axis=1
    )
    first_t = gather_z(jnp.concatenate([tokens, meta], axis=1))
    x_t, y_t = gather_sides(first_t)
    first_core = flip(first_t, CORE)
    first_g = gather_z(after(grad_out, first_core))
    far_t = gather_far(x_t, y_t)
    x_g, y_g = gather_sides(after(first_g, *far_t))
    pieces_t = [first_t, x_t, y_t, *far_t, first_core]
    pieces_t += [flip(piece, CORE) for piece in pieces_t[1:5]]
    all_meta = gather_meta(pieces_t, cols)
    all_ids = all_meta[:, :top_count].astype(jnp.int32)
    all_weights = all_meta[:, top_count : 2 * top_count].astype(f32)
    first = me * local_experts
    fused = narrow_count == 1 and local_experts == 1
    chunks = CHUNKS if fused else 1
    units = w_gate.shape[2]
    parts = 1 if fused or units % (2 * LANES) else 2
    picked = []
    for j in range(local_experts):
        match = all_ids == first + j
        chosen = jnp.any(match, axis=1)
        gain = jnp.sum(jnp.where(match, all_weights, 0.0), axis=1)
        rank = jnp.cumsum(chosen.astype(jnp.int32)) - 1
        slot = jnp.where(chosen, rank, -1)
        place = slot[None, :] == jnp.arange(rows, dtype=jnp.int32)[:, None]
        row_gain = jnp.sum(jnp.where(place, gain[None, :], 0.0), axis=1, keepdims=True)
        if fused:
            x, first_part = pick_forward(slot, pieces_t, rows, w_gate[j], w_up[j], parts)
        else:
            x = pick_rows(slot, pieces_t, rows, cols)
            x = lax.all_gather(x, "narrow", axis=1, tiled=True)
            first_part = forward(x, w_gate[j], w_up[j], 0, parts)
        ahead = [first_part]
        picked.append((slot, place, row_gain, x, ahead))
    x_g, y_g, *_ = lax.optimization_barrier((x_g, y_g, *[ahead[0][0] for *_, ahead in picked]))
    far_g = gather_far(x_g, y_g)
    for j in range(local_experts):
        slot, place, row_gain, x, ahead = picked[j]
        if parts == 2:
            ahead.append(forward(after(x, x_g, y_g), w_gate[j], w_up[j], 1, parts))
    far_g = lax.optimization_barrier((*far_g, *[ahead[-1][0] for *_, ahead in picked]))[: len(far_g)]
    pieces_g = gather_core([first_g, x_g, y_g, *far_g])
    expert_cols = experts_all + -experts_all % LANES
    dense = [0, 0]
    route_all = 0
    ends = []
    for j in range(local_experts):
        slot, place, row_gain, x, ahead = picked[j]
        straight = [(hidden, active, pull) for hidden, _, active, pull in ahead]
        if fused:
            g, d_gate, d_up, route, *dense = pick_back(
                slot, pieces_g, row_gain, w_down[j], w_gate[j], w_up[j], straight, w_gate.shape[1] // chunks
            )
        else:
            g = pick_rows(slot, pieces_g, rows, cols)
            g = lax.all_gather(g, "narrow", axis=1, tiled=True)
            d_gate, d_up, route = back_project(g, row_gain, w_down[j], straight)
        route = lax.psum(route.astype(bf16).astype(f32), "narrow")
        at = jnp.arange(expert_cols, dtype=jnp.int32) == first + j
        route = jnp.where(at[None, :], route, 0.0).astype(bf16)
        ends.append(([part[1] for part in ahead], g, row_gain))
        if fused:
            continue
        (part,) = token_grad(d_gate, d_up, slot, route, w_gate[j], w_up[j], 0, 1, False)
        part = lax.psum_scatter(part, "narrow", scatter_dimension=1, tiled=True)
        part = jnp.concatenate([part, route], axis=1)
        part = dot(place.astype(bf16), part, ((0,), (0,)))
        dense = [dense[0] + part[: total // 2], dense[1] + part[total // 2 :]]
    mine = [add(dense[0].astype(bf16), flip(dense[1].astype(bf16), CORE))]
    if fused and chunks == 2:
        own, other = token_grad(after(d_gate, dense[0]), d_up, slot, route, w_gate[0], w_up[0], 1, chunks, True)
        mine[0] = add(after(dense[0], own), flip(dense[1], CORE))
        mine.append(add(own, flip(other, CORE)))
    sides = [scatter_far(rows_) for rows_ in mine]
    firsts = [scatter_sides(*side) for side in sides]
    shares = [scatter_z(first_) for first_ in firsts]
    gates = [mine[0], sides[0][1], firsts[0], firsts[-1]] if fused else [mine[0]]
    grad_downs = []
    for turned, g, row_gain in ends:
        out = None
        for k, gate in enumerate(gates):
            out = down_grad(turned, after(g, gate), row_gain, k, len(gates), out)
        grad_downs.append(out)
    joined = jnp.concatenate(shares, axis=1)
    width = tokens.shape[1]
    by_expert = joined[:, width : width + experts_all].astype(f32)
    pick = expert_ids[:, :, None] == jnp.arange(experts_all, dtype=jnp.int32)[None, None, :]
    grad_route = jnp.sum(jnp.where(pick, by_expert[:, None, :], 0.0), axis=2)
    return (joined[:, :width], grad_route.astype(bf16), jnp.stack(grad_downs))


def solution(mesh):
    in_specs = (
        P("wide", "narrow"),
        P("wide", "narrow"),
        P("wide", None),
        P("wide", None),
        P("wide", None, "narrow"),
        P("wide", None, "narrow"),
        P("wide", "narrow", None),
    )
    out_specs = (P("wide", "narrow"), P("wide", None), P("wide", "narrow", None))
    return jax.shard_map(body, mesh=mesh, in_specs=in_specs, out_specs=out_specs, check_vma=False)
```

```python
import functools

import jax
import jax.numpy as jnp
from jax import lax
from jax.experimental import pallas as pl
from jax.experimental.pallas import tpu as pltpu
from jax.sharding import PartitionSpec as P

LANES = 128
CHUNKS = 2
bf16, f32 = jnp.bfloat16, jnp.float32


def dot(a, b, dims):
    return lax.dot_general(a, b, ((dims[0], dims[1]), ((), ())), preferred_element_type=f32)


def add(*terms):
    total = terms[0].astype(f32)
    for term in terms[1:]:
        total = total + term.astype(f32)
    return total.astype(terms[0].dtype)


def tile(size, most):
    fits = [t for t in range(LANES, min(size, most) + 1, LANES) if size % t == 0]
    return fits[-1] if fits else size


def call(kernel, flops, moved, **kwargs):
    return pl.pallas_call(
        kernel,
        compiler_params=pltpu.CompilerParams(vmem_limit_bytes=52 * 1024 * 1024),
        cost_estimate=pl.CostEstimate(flops=flops, bytes_accessed=moved, transcendentals=0),
        **kwargs,
    )


def whole(*shape):
    return pl.BlockSpec(shape, lambda i: (0,) * len(shape))


CORE, X, Y, Z = 1, 2, 4, 8


def flip(value, mask):
    count = lax.axis_size("wide")
    return lax.ppermute(value, "wide", [(i, i ^ mask) for i in range(count)])


def after(value, *deps):
    return lax.optimization_barrier((value, *deps))[0]


def depth():
    return lax.axis_size("wide") // Z


def gather_z(shard):
    return jnp.concatenate([shard] + [flip(shard, Z * k) for k in range(1, depth())], axis=0)


def gather_sides(first):
    return flip(first, X), flip(first, Y)


def gather_far(by_x, by_y):
    half = by_x.shape[0] // 2
    return [flip(by_y[:half], X), flip(by_x[half:], Y)]


def gather_core(pieces):
    return pieces + [flip(piece, CORE) for piece in pieces]


def offsets():
    return [Z * k + m + c for c in (0, CORE) for m in (0, X, Y, X | Y) for k in range(depth())]


def quarters(mine):
    size = mine.shape[0] // 4
    return [mine[k * size : (k + 1) * size] for k in range(4)]


def scatter_far(mine):
    first, by_x, by_y, far = quarters(mine)
    half = far.shape[0] // 2
    to_y, to_x = flip(far[:half], X), flip(far[half:], Y)
    by_y = jnp.concatenate([add(by_y[:half], to_y), by_y[half:]], axis=0)
    by_x = jnp.concatenate([by_x[:half], add(by_x[half:], to_x)], axis=0)
    return first, by_x, by_y


def scatter_sides(first, by_x, by_y):
    return add(first, flip(by_x, X), flip(by_y, Y))


def scatter_z(first):
    step = first.shape[0] // depth()
    blocks = [first[k * step : (k + 1) * step] for k in range(depth())]
    return add(blocks[0], *[flip(blocks[k], Z * k) for k in range(1, depth())])


def meta_kernel(sizes, cols, *refs):
    pieces, (out_ref, sems) = refs[: len(sizes)], refs[len(sizes) :]
    starts = [sum(sizes[:k]) for k in range(len(sizes))]
    copies = [
        pltpu.make_async_copy(
            pieces[k].at[:, pl.ds(cols, LANES)], out_ref.at[pl.ds(starts[k], sizes[k]), :], sems.at[k]
        )
        for k in range(len(sizes))
    ]
    for copy in copies:
        copy.start()
    for copy in copies:
        copy.wait()


def gather_meta(pieces, cols):
    sizes = [piece.shape[0] for piece in pieces]
    return call(
        functools.partial(meta_kernel, sizes, cols),
        0,
        4 * sum(sizes) * LANES,
        grid=(1,),
        in_specs=[pl.BlockSpec(memory_space=pl.ANY)] * len(pieces),
        out_specs=whole(sum(sizes), LANES),
        out_shape=jax.ShapeDtypeStruct((sum(sizes), LANES), bf16),
        scratch_shapes=[pltpu.SemaphoreType.DMA((len(sizes),))],
    )(*pieces)


def pick_kernel(sizes, block, slot_ref, *refs):
    pieces, (out_ref, held, place, sems) = refs[: len(sizes)], refs[len(sizes) :]
    step = pl.program_id(0)
    starts = [sum(sizes[:k]) for k in range(len(sizes))]

    def copy(at, k):
        return pltpu.make_async_copy(
            pieces[k].at[:, pl.ds(pl.multiple_of(at * block, LANES), block)],
            held.at[at, pl.ds(starts[k], sizes[k]), :],
            sems.at[at, k],
        )

    @pl.when(step == 0)
    def _():
        @pl.loop(0, pl.num_programs(0))
        def _(at):
            for k in range(len(sizes)):
                copy(at, k).start()

        rows = lax.broadcasted_iota(jnp.int32, place.shape, 0)
        place[...] = jnp.where(rows == slot_ref[...], 1.0, 0.0).astype(bf16)

    for k in range(len(sizes)):
        copy(step, k).wait()
    out_ref[...] = dot(place[...], held[step], ((1,), (0,))).astype(bf16)


def pick_rows(slot, pieces, rows, cols):
    sizes = [piece.shape[0] for piece in pieces]
    total = sum(sizes)
    block = tile(cols, 512)
    steps = cols // block
    return call(
        functools.partial(pick_kernel, sizes, block),
        2 * rows * total * cols,
        2 * (rows + total) * cols,
        grid=(steps,),
        in_specs=[whole(1, total)] + [pl.BlockSpec(memory_space=pl.ANY)] * len(pieces),
        out_specs=pl.BlockSpec((rows, block), lambda i: (0, i)),
        out_shape=jax.ShapeDtypeStruct((rows, cols), bf16),
        scratch_shapes=[
            pltpu.VMEM((steps, total, block), bf16),
            pltpu.VMEM((rows, total), bf16),
            pltpu.SemaphoreType.DMA((steps, len(sizes))),
        ],
    )(slot.reshape(1, total), *pieces)


def forward_kernel(x_ref, gate_ref, up_ref, hidden_ref, turned_ref, active_ref, pull_ref):
    gate_pre = dot(x_ref[...], gate_ref[...], ((1,), (0,)))
    up_pre = dot(x_ref[...], up_ref[...], ((1,), (0,)))
    sig = jax.nn.sigmoid(gate_pre)
    active = gate_pre * sig
    hidden = active * up_pre
    hidden_ref[...] = hidden.astype(bf16)
    turned_ref[...] = hidden.T.astype(bf16)
    active_ref[...] = active.astype(bf16)
    pull_ref[...] = (up_pre * (sig * (1.0 + gate_pre * (1.0 - sig)))).astype(bf16)


def forward(x, w_gate, w_up, low, high):
    rows, width = x.shape
    units = high - low
    block = tile(units, 256)
    first = low // block
    weight = pl.BlockSpec((width, block), lambda i: (0, first + i))
    unit = pl.BlockSpec((rows, block), lambda i: (0, i))
    turned = pl.BlockSpec((block, rows), lambda i: (i, 0))
    shape = jax.ShapeDtypeStruct((rows, units), bf16)
    return call(
        forward_kernel,
        4 * rows * width * units,
        4 * width * units,
        grid=(units // block,),
        in_specs=[whole(rows, width), weight, weight],
        out_specs=[unit, turned, unit, unit],
        out_shape=[shape, jax.ShapeDtypeStruct((units, rows), bf16), shape, shape],
    )(x, w_gate, w_up)


def back_kernel(steps, g_ref, gain_ref, down_ref, *refs):
    parts, (d_gate_ref, d_up_ref, route_ref) = refs[:-3], refs[-3:]
    step = pl.program_id(0)
    back = dot(g_ref[...], down_ref[...], ((1,), (1,)))
    d_hidden = gain_ref[...] * back

    @pl.when(step == 0)
    def _():
        route_ref[...] = jnp.zeros_like(route_ref)

    for k in range(len(parts) // 3):
        hidden_ref, active_ref, pull_ref = parts[3 * k : 3 * k + 3]

        @pl.when((step >= k * steps) & (step < (k + 1) * steps))
        def _(hidden_ref=hidden_ref, active_ref=active_ref, pull_ref=pull_ref):
            d_gate_ref[...] = (d_hidden * pull_ref[...].astype(f32)).astype(bf16)
            d_up_ref[...] = (d_hidden * active_ref[...].astype(f32)).astype(bf16)
            route_ref[...] += jnp.sum(hidden_ref[...].astype(f32) * back, axis=1, keepdims=True)


def back_project(g, gain, w_down, parts):
    rows, width = g.shape
    units = w_down.shape[0]
    block = tile(parts[0][0].shape[1], 256)
    steps = units // block // len(parts)
    unit = pl.BlockSpec((rows, block), lambda i: (0, i))

    def unit_of(part):
        return pl.BlockSpec((rows, block), lambda i: (0, jnp.clip(i - part * steps, 0, steps - 1)))

    shape = jax.ShapeDtypeStruct((rows, units), bf16)
    return call(
        functools.partial(back_kernel, steps),
        2 * rows * width * units,
        2 * width * units,
        grid=(units // block,),
        in_specs=[
            whole(rows, width),
            whole(rows, 1),
            pl.BlockSpec((block, width), lambda i: (i, 0)),
        ]
        + [unit_of(k) for k in range(len(parts)) for _ in range(3)],
        out_specs=[unit, unit, whole(rows, 1)],
        out_shape=[shape, shape, jax.ShapeDtypeStruct((rows, 1), f32)],
    )(g, gain, w_down, *[array for part in parts for array in part])


ANY = pl.BlockSpec(memory_space=pl.ANY)


def pick_phase(sizes, picks, slot_ref, pieces, x_out, scratch, start_weights):
    held, place, x, piece_sems, x_sems = scratch
    step = pl.program_id(0)
    width = held.shape[2]
    starts = [sum(sizes[:k]) for k in range(len(sizes))]

    def columns(at):
        return pl.ds(pl.multiple_of(at * width, LANES), width)

    def loads(at):
        return [
            pltpu.make_async_copy(
                pieces[k].at[:, columns(at)],
                held.at[at, pl.ds(starts[k], sizes[k]), :],
                piece_sems.at[at, k],
            )
            for k in range(len(sizes))
        ]

    def store(at):
        return pltpu.make_async_copy(x.at[:, columns(at)], x_out.at[:, columns(at)], x_sems.at[at])

    @pl.when(step == 0)
    def _():
        for at in range(min(2, picks)):
            for copy in loads(at):
                copy.start()
        rows = lax.broadcasted_iota(jnp.int32, place.shape, 0)
        place[...] = jnp.where(rows == slot_ref[...], 1.0, 0.0).astype(bf16)

    @pl.when(step + 2 < picks)
    def _():
        for copy in loads(step + 2):
            copy.start()

    @pl.when(step >= 1)
    def _():
        start_weights(step - 1)

    @pl.when(step < picks)
    def _():
        for copy in loads(step):
            copy.wait()
        x[:, columns(step)] = dot(place[...], held[step], ((1,), (0,))).astype(bf16)
        store(step).start()

    @pl.when(step == pl.num_programs(0) - 1)
    def _():
        for at in range(picks):
            store(at).wait()

    return x


def pick_scratch(rows, sizes, cols):
    block = tile(cols, 1024)
    picks = cols // block
    return picks, [
        pltpu.VMEM((picks, sum(sizes), block), bf16),
        pltpu.VMEM((rows, sum(sizes)), bf16),
        pltpu.VMEM((rows, cols), bf16),
        pltpu.SemaphoreType.DMA((picks, len(sizes))),
        pltpu.SemaphoreType.DMA((picks,)),
    ]


def pick_forward_kernel(sizes, picks, blocks, slot_ref, *refs):
    count = len(sizes)
    pieces, (gate_any, up_any, x_out, hidden_ref, turned_ref, active_ref, pull_ref) = refs[:count], refs[count : count + 7]
    *scratch, gates, ups, sems = refs[count + 7 :]
    step = pl.program_id(0)
    width = gates.shape[2]

    def weights(at):
        source = pl.ds(pl.multiple_of(at * width, LANES), width)
        return [
            pltpu.make_async_copy(gate_any.at[:, source], gates.at[at], sems.at[0, at]),
            pltpu.make_async_copy(up_any.at[:, source], ups.at[at], sems.at[1, at]),
        ]

    def start_weights(at):
        @pl.when(at < blocks)
        def _():
            for copy in weights(at):
                copy.start()

    x = pick_phase(sizes, picks, slot_ref, pieces, x_out, scratch, start_weights)

    @pl.when(step >= picks)
    def _():
        at = step - picks
        for copy in weights(at):
            copy.wait()
        forward_kernel(x, gates.at[at], ups.at[at], hidden_ref, turned_ref, active_ref, pull_ref)


def pick_forward(slot, pieces, rows, w_gate, w_up, units):
    sizes = [piece.shape[0] for piece in pieces]
    cols = w_gate.shape[0]
    picks, scratch = pick_scratch(rows, sizes, cols)
    block = tile(units, 256)
    blocks = units // block
    unit = pl.BlockSpec((rows, block), lambda i: (0, jnp.maximum(i - picks, 0)))
    turned = pl.BlockSpec((block, rows), lambda i: (jnp.maximum(i - picks, 0), 0))
    shape = jax.ShapeDtypeStruct((rows, units), bf16)
    x, *ahead = call(
        functools.partial(pick_forward_kernel, sizes, picks, blocks),
        4 * rows * cols * units + 2 * rows * sum(sizes) * cols,
        4 * cols * units + 2 * (rows + sum(sizes)) * cols,
        grid=(picks + blocks,),
        in_specs=[whole(1, sum(sizes))] + [ANY] * (len(sizes) + 2),
        out_specs=[ANY, unit, turned, unit, unit],
        out_shape=[
            jax.ShapeDtypeStruct((rows, cols), bf16),
            shape,
            jax.ShapeDtypeStruct((units, rows), bf16),
            shape,
            shape,
        ],
        scratch_shapes=scratch
        + [pltpu.VMEM((blocks, cols, block), bf16)] * 2
        + [pltpu.SemaphoreType.DMA((2, blocks))],
    )(slot.reshape(1, sum(sizes)), *pieces, w_gate, w_up)
    return x, ahead


def pick_back_kernel(sizes, picks, blocks, ranges, tokens, slot_ref, slot_col, gain_ref, *refs):
    count = len(sizes)
    pieces, (down_any, gate_any, up_any), refs = refs[:count], refs[count : count + 3], refs[count + 3 :]
    *refs, held, place, rows_ref, piece_sems, x_sems, downs, gates, ups, d_gate, d_up, sems, token_sems = refs
    *parts, g_out, d_gate_ref, d_up_ref, route_ref, own_ref, other_ref = refs
    step = pl.program_id(0)
    width, token_width = downs.shape[1], gates.shape[1]

    def weights(at):
        source = down_any.at[pl.ds(pl.multiple_of(at * width, LANES), width), :]
        return [pltpu.make_async_copy(source, downs.at[at], sems.at[at])]

    def token_weights(at):
        source = pl.ds(pl.multiple_of(at * token_width, LANES), token_width)
        return [
            pltpu.make_async_copy(gate_any.at[source, :], gates.at[at], token_sems.at[0, at]),
            pltpu.make_async_copy(up_any.at[source, :], ups.at[at], token_sems.at[1, at]),
        ]

    def start_weights(at):
        @pl.when(at < blocks)
        def _():
            for copy in weights(at):
                copy.start()

        @pl.when((at >= blocks) & (at < blocks + tokens))
        def _():
            for copy in token_weights(at - blocks):
                copy.start()

    scratch = (held, place, rows_ref, piece_sems, x_sems)
    g = pick_phase(sizes, picks, slot_ref, pieces, g_out, scratch, start_weights)

    @pl.when(step == 0)
    def _():
        route_ref[...] = jnp.zeros_like(route_ref)

    for k, (low, high) in enumerate(ranges):
        hidden_ref, active_ref, pull_ref = parts[3 * k : 3 * k + 3]

        @pl.when((step >= picks + low) & (step < picks + high))
        def _(hidden_ref=hidden_ref, active_ref=active_ref, pull_ref=pull_ref):
            at = step - picks
            for copy in weights(at):
                copy.wait()
            back = dot(g[...], downs[at], ((1,), (1,)))
            d_hidden = gain_ref[...] * back
            units = pl.ds(pl.multiple_of(at * width, LANES), width)
            d_gate_ref[...] = (d_hidden * pull_ref[...].astype(f32)).astype(bf16)
            d_up_ref[...] = (d_hidden * active_ref[...].astype(f32)).astype(bf16)
            d_gate[:, units] = d_gate_ref[...]
            d_up[:, units] = d_up_ref[...]
            route_ref[...] += jnp.sum(hidden_ref[...].astype(f32) * back, axis=1, keepdims=True)

    @pl.when(step >= picks + blocks)
    def _():
        at = step - picks - blocks
        for copy in token_weights(at):
            copy.wait()
        part = dot(d_gate[...], gates[at], ((1,), (1,)))
        part = (part + dot(d_up[...], ups[at], ((1,), (1,)))).astype(bf16)
        spread_rows(slot_col, part, (own_ref, other_ref))


def pick_back(slot, pieces, gain, w_down, w_gate, w_up, parts, high):
    sizes = [piece.shape[0] for piece in pieces]
    total = sum(sizes)
    rows = gain.shape[0]
    units, cols = w_down.shape
    picks, scratch = pick_scratch(rows, sizes, cols)
    block = min(tile(part[0].shape[1], 256) for part in parts)
    blocks = units // block
    ends = [sum(part[0].shape[1] for part in parts[: k + 1]) // block for k in range(len(parts))]
    ranges = list(zip([0] + ends[:-1], ends))
    token_block = tile(cols, 512)
    tokens = high // token_block
    unit = pl.BlockSpec((rows, block), lambda i: (0, jnp.clip(i - picks, 0, blocks - 1)))
    dense = pl.BlockSpec((total // 2, token_block), lambda i: (0, jnp.maximum(i - picks - blocks, 0)))

    def unit_of(part):
        return pl.BlockSpec((rows, block), lambda i: (0, jnp.clip(i - picks - part[0], 0, part[1] - part[0] - 1)))

    shape = jax.ShapeDtypeStruct((rows, units), bf16)
    return call(
        functools.partial(pick_back_kernel, sizes, picks, blocks, ranges, tokens),
        2 * rows * (cols * units + total * cols + 2 * high * units + total * high),
        2 * cols * units + 4 * high * units + 2 * (rows + total) * cols,
        grid=(picks + blocks + tokens,),
        in_specs=[whole(1, total), whole(total, 1), whole(rows, 1)]
        + [ANY] * (len(sizes) + 3)
        + [unit_of(part) for part in ranges for _ in range(3)],
        out_specs=[ANY, unit, unit, whole(rows, 1), dense, dense],
        out_shape=[
            jax.ShapeDtypeStruct((rows, cols), bf16),
            shape,
            shape,
            jax.ShapeDtypeStruct((rows, 1), f32),
        ]
        + [jax.ShapeDtypeStruct((total // 2, high), bf16)] * 2,
        scratch_shapes=scratch
        + [pltpu.VMEM((blocks, block, cols), bf16)]
        + [pltpu.VMEM((tokens, token_block, units), bf16)] * 2
        + [pltpu.VMEM((rows, units), bf16)] * 2
        + [pltpu.SemaphoreType.DMA((blocks,)), pltpu.SemaphoreType.DMA((2, tokens))],
    )(
        slot.reshape(1, total),
        slot.reshape(total, 1),
        gain,
        *pieces,
        w_down,
        w_gate,
        w_up,
        *[array for part in parts for array in part],
    )


def spread_rows(slot_ref, part, outs):
    half = slot_ref.shape[0] // 2
    rows, width = part.shape
    for k in range(2):
        slot = slot_ref[k * half : (k + 1) * half, :]
        lanes = lax.broadcasted_iota(jnp.int32, (half, rows), 1)
        place = jnp.where(lanes == slot, 1.0, 0.0).astype(bf16)
        outs[k][:, :width] = dot(place, part, ((1,), (0,))).astype(bf16)


def token_kernel(steps, spread, d_gate_ref, d_up_ref, slot_ref, route_ref, gate_ref, up_ref, *outs):
    step = pl.program_id(0)

    def store(part):
        if spread:
            spread_rows(slot_ref, part, outs)
        else:
            outs[0][...] = part

    @pl.when(step < steps)
    def _():
        part = dot(d_gate_ref[...], gate_ref[...], ((1,), (1,)))
        store((part + dot(d_up_ref[...], up_ref[...], ((1,), (1,)))).astype(bf16))

    if spread:

        @pl.when(step >= steps)
        def _():
            store(route_ref[...])


def token_grad(d_gate, d_up, slot, route, w_gate, w_up, chunk, chunks, spread):
    rows, units = d_gate.shape
    width = w_gate.shape[0] // chunks
    total = slot.shape[0]
    block = tile(width, 512)
    steps = width // block
    first = chunk * steps
    extra = route.shape[1] if spread and chunk == chunks - 1 else 0
    weight = pl.BlockSpec((block, units), lambda i: (first + jnp.minimum(i, steps - 1), 0))
    out_rows = [total // 2] * 2 if spread else [rows]
    return call(
        functools.partial(token_kernel, steps, spread),
        4 * rows * width * units + 2 * rows * width * total * spread,
        4 * width * units + 2 * total * width,
        grid=(steps + (extra > 0),),
        in_specs=[whole(rows, units), whole(rows, units), whole(total, 1), whole(*route.shape), weight, weight],
        out_specs=[pl.BlockSpec((n, block), lambda i: (0, i)) for n in out_rows],
        out_shape=[jax.ShapeDtypeStruct((n, width + extra), bf16) for n in out_rows],
    )(d_gate, d_up, slot.reshape(total, 1), route, w_gate, w_up)


def down_kernel(count, g_ref, gain_ref, *refs):
    turned, out_ref = refs[:count], refs[-1]
    scaled = (gain_ref[...] * g_ref[...].astype(f32)).astype(bf16)
    at = 0
    for ref in turned:
        out_ref[at : at + ref.shape[0], :] = dot(ref[...], scaled, ((1,), (0,))).astype(bf16)
        at += ref.shape[0]


def down_grad(turned, g, gain, chunk, chunks, into):
    rows, width = g.shape
    units = sum(part.shape[0] for part in turned)
    block = tile(width // chunks, 512)
    steps = width // chunks // block
    first = chunk * steps
    kept = [] if into is None else [into]
    return call(
        functools.partial(down_kernel, len(turned)),
        2 * rows * width * units // chunks,
        2 * width * units // chunks,
        grid=(steps,),
        in_specs=[pl.BlockSpec((rows, block), lambda i: (0, first + i)), whole(rows, 1)]
        + [whole(*part.shape) for part in turned]
        + [pl.BlockSpec(memory_space=pl.ANY)] * len(kept),
        out_specs=pl.BlockSpec((units, block), lambda i: (0, first + i)),
        out_shape=jax.ShapeDtypeStruct((units, width), bf16),
        input_output_aliases={2 + len(turned): 0} if kept else {},
    )(g, gain, *turned, *kept)


def body(tokens, grad_out, expert_ids, route_weights, w_gate, w_up, w_down):
    wide_count = lax.axis_size("wide")
    narrow_count = lax.axis_size("narrow")
    local_experts = w_gate.shape[0]
    experts_all = local_experts * wide_count
    tok_count, top_count = expert_ids.shape
    capacity = min(tok_count, 2 * tok_count * top_count // experts_all)
    rows = wide_count * capacity
    total = wide_count * tok_count
    cols = tokens.shape[1]
    me = lax.axis_index("wide")
    pad = -2 * top_count % LANES
    meta = jnp.concatenate(
        [expert_ids.astype(bf16), route_weights, jnp.zeros((tok_count, pad), bf16)], axis=1
    )
    first_t = gather_z(jnp.concatenate([tokens, meta], axis=1))
    x_t, y_t = gather_sides(first_t)
    first_g = gather_z(after(grad_out, first_t))
    far_t = gather_far(x_t, y_t)
    x_g, y_g = gather_sides(after(first_g, *far_t))
    pieces_t = gather_core([first_t, x_t, y_t] + far_t)
    all_meta = gather_meta(pieces_t, cols)
    all_ids = all_meta[:, :top_count].astype(jnp.int32)
    all_weights = all_meta[:, top_count : 2 * top_count].astype(f32)
    first = me * local_experts
    fused = narrow_count == 1 and local_experts == 1
    chunks = CHUNKS if fused else 1
    units = w_gate.shape[2]
    ahead_units = units * 2 // 3 if fused and units % (6 * LANES) == 0 else units
    picked = []
    for j in range(local_experts):
        match = all_ids == first + j
        chosen = jnp.any(match, axis=1)
        gain = jnp.sum(jnp.where(match, all_weights, 0.0), axis=1)
        rank = jnp.cumsum(chosen.astype(jnp.int32)) - 1
        slot = jnp.where(chosen, rank, -1)
        place = slot[None, :] == jnp.arange(rows, dtype=jnp.int32)[:, None]
        row_gain = jnp.sum(jnp.where(place, gain[None, :], 0.0), axis=1, keepdims=True)
        if fused:
            x, first_part = pick_forward(slot, pieces_t, rows, w_gate[j], w_up[j], ahead_units)
        else:
            x = pick_rows(slot, pieces_t, rows, cols)
            x = lax.all_gather(x, "narrow", axis=1, tiled=True)
            first_part = forward(x, w_gate[j], w_up[j], 0, ahead_units)
        ahead = [first_part]
        picked.append((slot, place, row_gain, x, ahead))
    x_g, y_g, *_ = lax.optimization_barrier((x_g, y_g, *[ahead[0][0] for *_, ahead in picked]))
    far_g = gather_far(x_g, y_g)
    for j in range(local_experts):
        slot, place, row_gain, x, ahead = picked[j]
        if ahead_units < units:
            ahead.append(forward(after(x, x_g, y_g), w_gate[j], w_up[j], ahead_units, units))
    far_g = lax.optimization_barrier((*far_g, *[ahead[-1][0] for *_, ahead in picked]))[: len(far_g)]
    pieces_g = gather_core([first_g, x_g, y_g, *far_g])
    expert_cols = experts_all + -experts_all % LANES
    dense = [0, 0]
    route_all = 0
    ends = []
    for j in range(local_experts):
        slot, place, row_gain, x, ahead = picked[j]
        straight = [(hidden, active, pull) for hidden, _, active, pull in ahead]
        if fused:
            g, d_gate, d_up, route, *dense = pick_back(
                slot, pieces_g, row_gain, w_down[j], w_gate[j], w_up[j], straight, w_gate.shape[1] // chunks
            )
        else:
            g = pick_rows(slot, pieces_g, rows, cols)
            g = lax.all_gather(g, "narrow", axis=1, tiled=True)
            d_gate, d_up, route = back_project(g, row_gain, w_down[j], straight)
        route = lax.psum(route.astype(bf16).astype(f32), "narrow")
        at = jnp.arange(expert_cols, dtype=jnp.int32) == first + j
        route = jnp.where(at[None, :], route, 0.0).astype(bf16)
        ends.append(([part[1] for part in ahead], g, row_gain))
        if fused:
            continue
        (part,) = token_grad(d_gate, d_up, slot, route, w_gate[j], w_up[j], 0, 1, False)
        part = lax.psum_scatter(part, "narrow", scatter_dimension=1, tiled=True)
        part = jnp.concatenate([part, route], axis=1)
        part = dot(place.astype(bf16), part, ((0,), (0,)))
        dense = [dense[0] + part[: total // 2], dense[1] + part[total // 2 :]]
    mine = [add(dense[0].astype(bf16), flip(dense[1].astype(bf16), CORE))]
    if fused and chunks == 2:
        own, other = token_grad(after(d_gate, dense[0]), d_up, slot, route, w_gate[0], w_up[0], 1, chunks, True)
        mine[0] = add(after(dense[0], own), flip(dense[1], CORE))
        mine.append(add(own, flip(other, CORE)))
    sides = [scatter_far(rows_) for rows_ in mine]
    firsts = [scatter_sides(*side) for side in sides]
    shares = [scatter_z(first_) for first_ in firsts]
    gates = [mine[0], sides[0][1], firsts[0], firsts[-1]] if fused else [mine[0]]
    grad_downs = []
    for turned, g, row_gain in ends:
        out = None
        for k, gate in enumerate(gates):
            out = down_grad(turned, after(g, gate), row_gain, k, len(gates), out)
        grad_downs.append(out)
    joined = jnp.concatenate(shares, axis=1)
    width = tokens.shape[1]
    by_expert = joined[:, width : width + experts_all].astype(f32)
    pick = expert_ids[:, :, None] == jnp.arange(experts_all, dtype=jnp.int32)[None, None, :]
    grad_route = jnp.sum(jnp.where(pick, by_expert[:, None, :], 0.0), axis=2)
    return (joined[:, :width], grad_route.astype(bf16), jnp.stack(grad_downs))


def solution(mesh):
    in_specs = (
        P("wide", "narrow"),
        P("wide", "narrow"),
        P("wide", None),
        P("wide", None),
        P("wide", None, "narrow"),
        P("wide", None, "narrow"),
        P("wide", "narrow", None),
    )
    out_specs = (P("wide", "narrow"), P("wide", None), P("wide", "narrow", None))
    return jax.shard_map(body, mesh=mesh, in_specs=in_specs, out_specs=out_specs, check_vma=False)
```

```python
import functools

import jax
import jax.numpy as jnp
from jax import lax
from jax.experimental import pallas as pl
from jax.experimental.pallas import tpu as pltpu
from jax.sharding import PartitionSpec as P

LANES = 128
CHUNKS = 2
bf16, f32 = jnp.bfloat16, jnp.float32


def dot(a, b, dims):
    return lax.dot_general(a, b, ((dims[0], dims[1]), ((), ())), preferred_element_type=f32)


def add(*terms):
    total = terms[0].astype(f32)
    for term in terms[1:]:
        total = total + term.astype(f32)
    return total.astype(terms[0].dtype)


def tile(size, most):
    fits = [t for t in range(LANES, min(size, most) + 1, LANES) if size % t == 0]
    return fits[-1] if fits else size


def call(kernel, flops, moved, **kwargs):
    return pl.pallas_call(
        kernel,
        compiler_params=pltpu.CompilerParams(vmem_limit_bytes=52 * 1024 * 1024),
        cost_estimate=pl.CostEstimate(flops=flops, bytes_accessed=moved, transcendentals=0),
        **kwargs,
    )


def whole(*shape):
    return pl.BlockSpec(shape, lambda i: (0,) * len(shape))


CORE, X, Y, Z = 1, 2, 4, 8


def flip(value, mask):
    count = lax.axis_size("wide")
    return lax.ppermute(value, "wide", [(i, i ^ mask) for i in range(count)])


def after(value, *deps):
    return lax.optimization_barrier((value, *deps))[0]


def depth():
    return lax.axis_size("wide") // Z


def gather_z(shard):
    return jnp.concatenate([shard] + [flip(shard, Z * k) for k in range(1, depth())], axis=0)


def gather_sides(first):
    return flip(first, X), flip(first, Y)


def gather_far(by_x, by_y):
    half = by_x.shape[0] // 2
    return [flip(by_y[:half], X), flip(by_x[half:], Y)]


def gather_core(pieces):
    return pieces + [flip(piece, CORE) for piece in pieces]


def offsets():
    return [Z * k + m + c for c in (0, CORE) for m in (0, X, Y, X | Y) for k in range(depth())]


def quarters(mine):
    size = mine.shape[0] // 4
    return [mine[k * size : (k + 1) * size] for k in range(4)]


def scatter_far(mine):
    first, by_x, by_y, far = quarters(mine)
    half = far.shape[0] // 2
    to_y, to_x = flip(far[:half], X), flip(far[half:], Y)
    by_y = jnp.concatenate([add(by_y[:half], to_y), by_y[half:]], axis=0)
    by_x = jnp.concatenate([by_x[:half], add(by_x[half:], to_x)], axis=0)
    return first, by_x, by_y


def scatter_sides(first, by_x, by_y):
    return add(first, flip(by_x, X), flip(by_y, Y))


def scatter_z(first):
    step = first.shape[0] // depth()
    blocks = [first[k * step : (k + 1) * step] for k in range(depth())]
    return add(blocks[0], *[flip(blocks[k], Z * k) for k in range(1, depth())])


def meta_kernel(sizes, cols, *refs):
    pieces, (out_ref, sems) = refs[: len(sizes)], refs[len(sizes) :]
    starts = [sum(sizes[:k]) for k in range(len(sizes))]
    copies = [
        pltpu.make_async_copy(
            pieces[k].at[:, pl.ds(cols, LANES)], out_ref.at[pl.ds(starts[k], sizes[k]), :], sems.at[k]
        )
        for k in range(len(sizes))
    ]
    for copy in copies:
        copy.start()
    for copy in copies:
        copy.wait()


def gather_meta(pieces, cols):
    sizes = [piece.shape[0] for piece in pieces]
    return call(
        functools.partial(meta_kernel, sizes, cols),
        0,
        4 * sum(sizes) * LANES,
        grid=(1,),
        in_specs=[pl.BlockSpec(memory_space=pl.ANY)] * len(pieces),
        out_specs=whole(sum(sizes), LANES),
        out_shape=jax.ShapeDtypeStruct((sum(sizes), LANES), bf16),
        scratch_shapes=[pltpu.SemaphoreType.DMA((len(sizes),))],
    )(*pieces)


def pick_kernel(sizes, block, slot_ref, *refs):
    pieces, (out_ref, held, place, sems) = refs[: len(sizes)], refs[len(sizes) :]
    step = pl.program_id(0)
    starts = [sum(sizes[:k]) for k in range(len(sizes))]

    def copy(at, k):
        return pltpu.make_async_copy(
            pieces[k].at[:, pl.ds(pl.multiple_of(at * block, LANES), block)],
            held.at[at, pl.ds(starts[k], sizes[k]), :],
            sems.at[at, k],
        )

    @pl.when(step == 0)
    def _():
        @pl.loop(0, pl.num_programs(0))
        def _(at):
            for k in range(len(sizes)):
                copy(at, k).start()

        rows = lax.broadcasted_iota(jnp.int32, place.shape, 0)
        place[...] = jnp.where(rows == slot_ref[...], 1.0, 0.0).astype(bf16)

    for k in range(len(sizes)):
        copy(step, k).wait()
    out_ref[...] = dot(place[...], held[step], ((1,), (0,))).astype(bf16)


def pick_rows(slot, pieces, rows, cols):
    sizes = [piece.shape[0] for piece in pieces]
    total = sum(sizes)
    block = tile(cols, 512)
    steps = cols // block
    return call(
        functools.partial(pick_kernel, sizes, block),
        2 * rows * total * cols,
        2 * (rows + total) * cols,
        grid=(steps,),
        in_specs=[whole(1, total)] + [pl.BlockSpec(memory_space=pl.ANY)] * len(pieces),
        out_specs=pl.BlockSpec((rows, block), lambda i: (0, i)),
        out_shape=jax.ShapeDtypeStruct((rows, cols), bf16),
        scratch_shapes=[
            pltpu.VMEM((steps, total, block), bf16),
            pltpu.VMEM((rows, total), bf16),
            pltpu.SemaphoreType.DMA((steps, len(sizes))),
        ],
    )(slot.reshape(1, total), *pieces)


def forward_kernel(x_ref, gate_ref, up_ref, hidden_ref, turned_ref, active_ref, pull_ref):
    gate_pre = dot(x_ref[...], gate_ref[...], ((1,), (0,)))
    up_pre = dot(x_ref[...], up_ref[...], ((1,), (0,)))
    sig = jax.nn.sigmoid(gate_pre)
    active = gate_pre * sig
    hidden = active * up_pre
    hidden_ref[...] = hidden.astype(bf16)
    turned_ref[...] = hidden.T.astype(bf16)
    active_ref[...] = active.astype(bf16)
    pull_ref[...] = (up_pre * (sig * (1.0 + gate_pre * (1.0 - sig)))).astype(bf16)


def forward(x, w_gate, w_up, low, high):
    rows, width = x.shape
    units = high - low
    block = tile(units, 256)
    first = low // block
    weight = pl.BlockSpec((width, block), lambda i: (0, first + i))
    unit = pl.BlockSpec((rows, block), lambda i: (0, i))
    turned = pl.BlockSpec((block, rows), lambda i: (i, 0))
    shape = jax.ShapeDtypeStruct((rows, units), bf16)
    return call(
        forward_kernel,
        4 * rows * width * units,
        4 * width * units,
        grid=(units // block,),
        in_specs=[whole(rows, width), weight, weight],
        out_specs=[unit, turned, unit, unit],
        out_shape=[shape, jax.ShapeDtypeStruct((units, rows), bf16), shape, shape],
    )(x, w_gate, w_up)


def back_kernel(steps, g_ref, gain_ref, down_ref, *refs):
    parts, (d_gate_ref, d_up_ref, route_ref) = refs[:-3], refs[-3:]
    step = pl.program_id(0)
    back = dot(g_ref[...], down_ref[...], ((1,), (1,)))
    d_hidden = gain_ref[...] * back

    @pl.when(step == 0)
    def _():
        route_ref[...] = jnp.zeros_like(route_ref)

    for k in range(len(parts) // 3):
        hidden_ref, active_ref, pull_ref = parts[3 * k : 3 * k + 3]

        @pl.when((step >= k * steps) & (step < (k + 1) * steps))
        def _(hidden_ref=hidden_ref, active_ref=active_ref, pull_ref=pull_ref):
            d_gate_ref[...] = (d_hidden * pull_ref[...].astype(f32)).astype(bf16)
            d_up_ref[...] = (d_hidden * active_ref[...].astype(f32)).astype(bf16)
            route_ref[...] += jnp.sum(hidden_ref[...].astype(f32) * back, axis=1, keepdims=True)


def back_project(g, gain, w_down, parts):
    rows, width = g.shape
    units = w_down.shape[0]
    block = tile(parts[0][0].shape[1], 256)
    steps = units // block // len(parts)
    unit = pl.BlockSpec((rows, block), lambda i: (0, i))

    def unit_of(part):
        return pl.BlockSpec((rows, block), lambda i: (0, jnp.clip(i - part * steps, 0, steps - 1)))

    shape = jax.ShapeDtypeStruct((rows, units), bf16)
    return call(
        functools.partial(back_kernel, steps),
        2 * rows * width * units,
        2 * width * units,
        grid=(units // block,),
        in_specs=[
            whole(rows, width),
            whole(rows, 1),
            pl.BlockSpec((block, width), lambda i: (i, 0)),
        ]
        + [unit_of(k) for k in range(len(parts)) for _ in range(3)],
        out_specs=[unit, unit, whole(rows, 1)],
        out_shape=[shape, shape, jax.ShapeDtypeStruct((rows, 1), f32)],
    )(g, gain, w_down, *[array for part in parts for array in part])


ANY = pl.BlockSpec(memory_space=pl.ANY)


def pick_phase(sizes, picks, slot_ref, pieces, x_out, scratch, start_weights):
    held, place, x, piece_sems, x_sems = scratch
    step = pl.program_id(0)
    width = held.shape[2]
    starts = [sum(sizes[:k]) for k in range(len(sizes))]

    def columns(at):
        return pl.ds(pl.multiple_of(at * width, LANES), width)

    def loads(at):
        return [
            pltpu.make_async_copy(
                pieces[k].at[:, columns(at)],
                held.at[at, pl.ds(starts[k], sizes[k]), :],
                piece_sems.at[at, k],
            )
            for k in range(len(sizes))
        ]

    def store(at):
        return pltpu.make_async_copy(x.at[:, columns(at)], x_out.at[:, columns(at)], x_sems.at[at])

    @pl.when(step == 0)
    def _():
        for at in range(min(2, picks)):
            for copy in loads(at):
                copy.start()
        rows = lax.broadcasted_iota(jnp.int32, place.shape, 0)
        place[...] = jnp.where(rows == slot_ref[...], 1.0, 0.0).astype(bf16)

    @pl.when(step + 2 < picks)
    def _():
        for copy in loads(step + 2):
            copy.start()

    @pl.when(step >= 1)
    def _():
        start_weights(step - 1)

    @pl.when(step < picks)
    def _():
        for copy in loads(step):
            copy.wait()
        x[:, columns(step)] = dot(place[...], held[step], ((1,), (0,))).astype(bf16)
        store(step).start()

    @pl.when(step == pl.num_programs(0) - 1)
    def _():
        for at in range(picks):
            store(at).wait()

    return x


def pick_scratch(rows, sizes, cols):
    block = tile(cols, 1024)
    picks = cols // block
    return picks, [
        pltpu.VMEM((picks, sum(sizes), block), bf16),
        pltpu.VMEM((rows, sum(sizes)), bf16),
        pltpu.VMEM((rows, cols), bf16),
        pltpu.SemaphoreType.DMA((picks, len(sizes))),
        pltpu.SemaphoreType.DMA((picks,)),
    ]


def pick_forward_kernel(sizes, picks, blocks, slot_ref, *refs):
    count = len(sizes)
    pieces, (gate_any, up_any, x_out, hidden_ref, turned_ref, active_ref, pull_ref) = refs[:count], refs[count : count + 7]
    *scratch, gates, ups, sems = refs[count + 7 :]
    step = pl.program_id(0)
    width = gates.shape[2]

    def weights(at):
        source = pl.ds(pl.multiple_of(at * width, LANES), width)
        return [
            pltpu.make_async_copy(gate_any.at[:, source], gates.at[at], sems.at[0, at]),
            pltpu.make_async_copy(up_any.at[:, source], ups.at[at], sems.at[1, at]),
        ]

    def start_weights(at):
        @pl.when(at < blocks)
        def _():
            for copy in weights(at):
                copy.start()

    x = pick_phase(sizes, picks, slot_ref, pieces, x_out, scratch, start_weights)

    @pl.when(step >= picks)
    def _():
        at = step - picks
        for copy in weights(at):
            copy.wait()
        forward_kernel(x, gates.at[at], ups.at[at], hidden_ref, turned_ref, active_ref, pull_ref)


def pick_forward(slot, pieces, rows, w_gate, w_up, units):
    sizes = [piece.shape[0] for piece in pieces]
    cols = w_gate.shape[0]
    picks, scratch = pick_scratch(rows, sizes, cols)
    block = tile(units, 256)
    blocks = units // block
    unit = pl.BlockSpec((rows, block), lambda i: (0, jnp.maximum(i - picks, 0)))
    turned = pl.BlockSpec((block, rows), lambda i: (jnp.maximum(i - picks, 0), 0))
    shape = jax.ShapeDtypeStruct((rows, units), bf16)
    x, *ahead = call(
        functools.partial(pick_forward_kernel, sizes, picks, blocks),
        4 * rows * cols * units + 2 * rows * sum(sizes) * cols,
        4 * cols * units + 2 * (rows + sum(sizes)) * cols,
        grid=(picks + blocks,),
        in_specs=[whole(1, sum(sizes))] + [ANY] * (len(sizes) + 2),
        out_specs=[ANY, unit, turned, unit, unit],
        out_shape=[
            jax.ShapeDtypeStruct((rows, cols), bf16),
            shape,
            jax.ShapeDtypeStruct((units, rows), bf16),
            shape,
            shape,
        ],
        scratch_shapes=scratch
        + [pltpu.VMEM((blocks, cols, block), bf16)] * 2
        + [pltpu.SemaphoreType.DMA((2, blocks))],
    )(slot.reshape(1, sum(sizes)), *pieces, w_gate, w_up)
    return x, ahead


def pick_back_kernel(sizes, picks, blocks, ranges, tokens, slot_ref, slot_col, gain_ref, expert_ref, *refs):
    count = len(sizes)
    pieces, (down_any, gate_any, up_any), refs = refs[:count], refs[count : count + 3], refs[count + 3 :]
    *refs, held, place, rows_ref, piece_sems, x_sems, downs, gates, ups, d_gate, d_up, sems, token_sems = refs
    *parts, g_out, route_ref, own_0, other_0, own_1, other_1 = refs
    step = pl.program_id(0)
    width, token_width = downs.shape[1], gates.shape[1]
    slots = gates.shape[0]
    base = picks + blocks

    def weights(at):
        source = down_any.at[pl.ds(pl.multiple_of(at * width, LANES), width), :]
        return [pltpu.make_async_copy(source, downs.at[at], sems.at[at])]

    def token_weights(at):
        source = pl.ds(pl.multiple_of(at * token_width, LANES), token_width)
        to = lax.rem(at, slots)
        return [
            pltpu.make_async_copy(gate_any.at[source, :], gates.at[to], token_sems.at[0, to]),
            pltpu.make_async_copy(up_any.at[source, :], ups.at[to], token_sems.at[1, to]),
        ]

    def start_weights(at):
        @pl.when(at < blocks)
        def _():
            for copy in weights(at):
                copy.start()

        @pl.when((at >= blocks) & (at < blocks + tokens))
        def _():
            for copy in token_weights(at - blocks):
                copy.start()

    scratch = (held, place, rows_ref, piece_sems, x_sems)
    g = pick_phase(sizes, picks, slot_ref, pieces, g_out, scratch, start_weights)

    @pl.when(step == 0)
    def _():
        route_ref[...] = jnp.zeros_like(route_ref)

    for k, (low, high) in enumerate(ranges):
        hidden_ref, active_ref, pull_ref = parts[3 * k : 3 * k + 3]

        @pl.when((step >= picks + low) & (step < picks + high))
        def _(hidden_ref=hidden_ref, active_ref=active_ref, pull_ref=pull_ref):
            at = step - picks
            for copy in weights(at):
                copy.wait()
            back = dot(g[...], downs[at], ((1,), (1,)))
            d_hidden = gain_ref[...] * back
            units = pl.ds(pl.multiple_of(at * width, LANES), width)
            d_gate[:, units] = (d_hidden * pull_ref[...].astype(f32)).astype(bf16)
            d_up[:, units] = (d_hidden * active_ref[...].astype(f32)).astype(bf16)
            route_ref[...] += jnp.sum(hidden_ref[...].astype(f32) * back, axis=1, keepdims=True)

    @pl.when((step >= base) & (step < base + tokens))
    def _():
        at = step - base
        for copy in token_weights(at):
            copy.wait()
        to = lax.rem(at, slots)
        part = dot(d_gate[...], gates[to], ((1,), (1,)))
        part = (part + dot(d_up[...], ups[to], ((1,), (1,)))).astype(bf16)

        @pl.when(at < tokens // 2)
        def _():
            spread_rows(slot_col, part, (own_0, other_0))

        @pl.when(at >= tokens // 2)
        def _():
            spread_rows(slot_col, part, (own_1, other_1))

    @pl.when(step == base + tokens)
    def _():
        route = route_ref[...].astype(bf16).astype(f32)
        lanes = lax.broadcasted_iota(jnp.int32, (route.shape[0], LANES), 1)
        columns = jnp.where(lanes == expert_ref[...], route, 0.0).astype(bf16)
        spread_rows(slot_col, columns, (own_1, other_1))


def pick_back(slot, pieces, gain, expert, w_down, w_gate, w_up, parts):
    sizes = [piece.shape[0] for piece in pieces]
    total = sum(sizes)
    rows = gain.shape[0]
    units, cols = w_down.shape
    picks, scratch = pick_scratch(rows, sizes, cols)
    block = min(tile(part[0].shape[1], 256) for part in parts)
    blocks = units // block
    ends = [sum(part[0].shape[1] for part in parts[: k + 1]) // block for k in range(len(parts))]
    ranges = list(zip([0] + ends[:-1], ends))
    token_block = tile(cols, 512)
    tokens = cols // token_block
    half = tokens // 2
    base = picks + blocks
    dense_0 = pl.BlockSpec((total // 2, token_block), lambda i: (0, jnp.clip(i - base, 0, half - 1)))
    dense_1 = pl.BlockSpec((total // 2, token_block), lambda i: (0, jnp.maximum(i - base - half, 0)))

    def unit_of(part):
        return pl.BlockSpec((rows, block), lambda i: (0, jnp.clip(i - picks - part[0], 0, part[1] - part[0] - 1)))

    return call(
        functools.partial(pick_back_kernel, sizes, picks, blocks, ranges, tokens),
        2 * rows * (3 * cols * units + 2 * total * cols),
        6 * cols * units + 2 * (rows + 2 * total) * cols,
        grid=(base + tokens + 1,),
        in_specs=[whole(1, total), whole(total, 1), whole(rows, 1), whole(1, 1)]
        + [ANY] * (len(sizes) + 3)
        + [unit_of(part) for part in ranges for _ in range(3)],
        out_specs=[ANY, whole(rows, 1), dense_0, dense_0, dense_1, dense_1],
        out_shape=[jax.ShapeDtypeStruct((rows, cols), bf16), jax.ShapeDtypeStruct((rows, 1), f32)]
        + [jax.ShapeDtypeStruct((total // 2, half * token_block), bf16)] * 2
        + [jax.ShapeDtypeStruct((total // 2, cols - half * token_block + LANES), bf16)] * 2,
        scratch_shapes=scratch
        + [pltpu.VMEM((blocks, block, cols), bf16)]
        + [pltpu.VMEM((picks, token_block, units), bf16)] * 2
        + [pltpu.VMEM((rows, units), bf16)] * 2
        + [pltpu.SemaphoreType.DMA((blocks,)), pltpu.SemaphoreType.DMA((2, picks))],
    )(
        slot.reshape(1, total),
        slot.reshape(total, 1),
        gain,
        expert.reshape(1, 1),
        *pieces,
        w_down,
        w_gate,
        w_up,
        *[array for part in parts for array in part],
    )


def spread_rows(slot_ref, part, outs):
    half = slot_ref.shape[0] // 2
    rows, width = part.shape
    for k in range(2):
        slot = slot_ref[k * half : (k + 1) * half, :]
        lanes = lax.broadcasted_iota(jnp.int32, (half, rows), 1)
        place = jnp.where(lanes == slot, 1.0, 0.0).astype(bf16)
        outs[k][:, :width] = dot(place, part, ((1,), (0,))).astype(bf16)


def token_kernel(steps, spread, d_gate_ref, d_up_ref, slot_ref, route_ref, gate_ref, up_ref, *outs):
    step = pl.program_id(0)

    def store(part):
        if spread:
            spread_rows(slot_ref, part, outs)
        else:
            outs[0][...] = part

    @pl.when(step < steps)
    def _():
        part = dot(d_gate_ref[...], gate_ref[...], ((1,), (1,)))
        store((part + dot(d_up_ref[...], up_ref[...], ((1,), (1,)))).astype(bf16))

    if spread:

        @pl.when(step >= steps)
        def _():
            store(route_ref[...])


def token_grad(d_gate, d_up, slot, route, w_gate, w_up, chunk, chunks, spread):
    rows, units = d_gate.shape
    width = w_gate.shape[0] // chunks
    total = slot.shape[0]
    block = tile(width, 512)
    steps = width // block
    first = chunk * steps
    extra = route.shape[1] if spread and chunk == chunks - 1 else 0
    weight = pl.BlockSpec((block, units), lambda i: (first + jnp.minimum(i, steps - 1), 0))
    out_rows = [total // 2] * 2 if spread else [rows]
    return call(
        functools.partial(token_kernel, steps, spread),
        4 * rows * width * units + 2 * rows * width * total * spread,
        4 * width * units + 2 * total * width,
        grid=(steps + (extra > 0),),
        in_specs=[whole(rows, units), whole(rows, units), whole(total, 1), whole(*route.shape), weight, weight],
        out_specs=[pl.BlockSpec((n, block), lambda i: (0, i)) for n in out_rows],
        out_shape=[jax.ShapeDtypeStruct((n, width + extra), bf16) for n in out_rows],
    )(d_gate, d_up, slot.reshape(total, 1), route, w_gate, w_up)


def down_kernel(count, g_ref, gain_ref, *refs):
    turned, out_ref = refs[:count], refs[-1]
    scaled = (gain_ref[...] * g_ref[...].astype(f32)).astype(bf16)
    at = 0
    for ref in turned:
        out_ref[at : at + ref.shape[0], :] = dot(ref[...], scaled, ((1,), (0,))).astype(bf16)
        at += ref.shape[0]


def down_grad(turned, g, gain, chunk, chunks, into):
    rows, width = g.shape
    units = sum(part.shape[0] for part in turned)
    block = tile(width // chunks, 512)
    steps = width // chunks // block
    first = chunk * steps
    kept = [] if into is None else [into]
    return call(
        functools.partial(down_kernel, len(turned)),
        2 * rows * width * units // chunks,
        2 * width * units // chunks,
        grid=(steps,),
        in_specs=[pl.BlockSpec((rows, block), lambda i: (0, first + i)), whole(rows, 1)]
        + [whole(*part.shape) for part in turned]
        + [pl.BlockSpec(memory_space=pl.ANY)] * len(kept),
        out_specs=pl.BlockSpec((units, block), lambda i: (0, first + i)),
        out_shape=jax.ShapeDtypeStruct((units, width), bf16),
        input_output_aliases={2 + len(turned): 0} if kept else {},
    )(g, gain, *turned, *kept)


def body(tokens, grad_out, expert_ids, route_weights, w_gate, w_up, w_down):
    wide_count = lax.axis_size("wide")
    narrow_count = lax.axis_size("narrow")
    local_experts = w_gate.shape[0]
    experts_all = local_experts * wide_count
    tok_count, top_count = expert_ids.shape
    capacity = min(tok_count, 2 * tok_count * top_count // experts_all)
    rows = wide_count * capacity
    total = wide_count * tok_count
    cols = tokens.shape[1]
    me = lax.axis_index("wide")
    pad = -2 * top_count % LANES
    meta = jnp.concatenate(
        [expert_ids.astype(bf16), route_weights, jnp.zeros((tok_count, pad), bf16)], axis=1
    )
    first_t = gather_z(jnp.concatenate([tokens, meta], axis=1))
    x_t, y_t = gather_sides(first_t)
    first_g = gather_z(after(grad_out, first_t))
    far_t = gather_far(x_t, y_t)
    x_g, y_g = gather_sides(after(first_g, *far_t))
    pieces_t = gather_core([first_t, x_t, y_t] + far_t)
    all_meta = gather_meta(pieces_t, cols)
    all_ids = all_meta[:, :top_count].astype(jnp.int32)
    all_weights = all_meta[:, top_count : 2 * top_count].astype(f32)
    first = me * local_experts
    fused = narrow_count == 1 and local_experts == 1 and experts_all <= LANES
    chunks = CHUNKS if fused else 1
    units = w_gate.shape[2]
    ahead_units = units * 2 // 3 if fused and units % (6 * LANES) == 0 else units
    picked = []
    for j in range(local_experts):
        match = all_ids == first + j
        chosen = jnp.any(match, axis=1)
        gain = jnp.sum(jnp.where(match, all_weights, 0.0), axis=1)
        rank = jnp.cumsum(chosen.astype(jnp.int32)) - 1
        slot = jnp.where(chosen, rank, -1)
        place = slot[None, :] == jnp.arange(rows, dtype=jnp.int32)[:, None]
        row_gain = jnp.sum(jnp.where(place, gain[None, :], 0.0), axis=1, keepdims=True)
        if fused:
            x, first_part = pick_forward(slot, pieces_t, rows, w_gate[j], w_up[j], ahead_units)
        else:
            x = pick_rows(slot, pieces_t, rows, cols)
            x = lax.all_gather(x, "narrow", axis=1, tiled=True)
            first_part = forward(x, w_gate[j], w_up[j], 0, ahead_units)
        ahead = [first_part]
        picked.append((slot, place, row_gain, x, ahead))
    x_g, y_g, *_ = lax.optimization_barrier((x_g, y_g, *[ahead[0][0] for *_, ahead in picked]))
    far_g = gather_far(x_g, y_g)
    for j in range(local_experts):
        slot, place, row_gain, x, ahead = picked[j]
        if ahead_units < units:
            ahead.append(forward(after(x, x_g, y_g), w_gate[j], w_up[j], ahead_units, units))
    far_g = lax.optimization_barrier((*far_g, *[ahead[-1][0] for *_, ahead in picked]))[: len(far_g)]
    pieces_g = gather_core([first_g, x_g, y_g, *far_g])
    expert_cols = experts_all + -experts_all % LANES
    dense = [0, 0]
    route_all = 0
    ends = []
    for j in range(local_experts):
        slot, place, row_gain, x, ahead = picked[j]
        straight = [(hidden, active, pull) for hidden, _, active, pull in ahead]
        if fused:
            g, _, *dense = pick_back(
                slot, pieces_g, row_gain, first + j, w_down[j], w_gate[j], w_up[j], straight
            )
            ends.append(([part[1] for part in ahead], g, row_gain))
            continue
        g = pick_rows(slot, pieces_g, rows, cols)
        g = lax.all_gather(g, "narrow", axis=1, tiled=True)
        d_gate, d_up, route = back_project(g, row_gain, w_down[j], straight)
        route = lax.psum(route.astype(bf16).astype(f32), "narrow")
        at = jnp.arange(expert_cols, dtype=jnp.int32) == first + j
        route = jnp.where(at[None, :], route, 0.0).astype(bf16)
        ends.append(([part[1] for part in ahead], g, row_gain))
        (part,) = token_grad(d_gate, d_up, slot, route, w_gate[j], w_up[j], 0, 1, False)
        part = lax.psum_scatter(part, "narrow", scatter_dimension=1, tiled=True)
        part = jnp.concatenate([part, route], axis=1)
        part = dot(place.astype(bf16), part, ((0,), (0,)))
        dense = [dense[0] + part[: total // 2], dense[1] + part[total // 2 :]]
    grad_downs = []
    if fused:
        (turned, g, row_gain), = ends
        out = down_grad(turned, g, row_gain, 0, 4, None)
        dense[0], out = lax.optimization_barrier((dense[0], out))
        mine = [add(dense[k], flip(dense[k + 1], CORE)) for k in (0, 2)]
        sides = [scatter_far(rows_) for rows_ in mine]
        firsts = [scatter_sides(*side) for side in sides]
        shares = [scatter_z(first_) for first_ in firsts]
        for k, gate in enumerate([sides[1][1], *firsts]):
            out = down_grad(turned, after(g, gate), row_gain, k + 1, 4, out)
        grad_downs.append(out)
    else:
        mine = add(dense[0].astype(bf16), flip(dense[1].astype(bf16), CORE))
        shares = [scatter_z(scatter_sides(*scatter_far(mine)))]
        grad_downs += [down_grad(*end, 0, 1, None) for end in ends]
    joined = jnp.concatenate(shares, axis=1)
    width = tokens.shape[1]
    by_expert = joined[:, width : width + experts_all].astype(f32)
    pick = expert_ids[:, :, None] == jnp.arange(experts_all, dtype=jnp.int32)[None, None, :]
    grad_route = jnp.sum(jnp.where(pick, by_expert[:, None, :], 0.0), axis=2)
    return (joined[:, :width], grad_route.astype(bf16), jnp.stack(grad_downs))


def solution(mesh):
    in_specs = (
        P("wide", "narrow"),
        P("wide", "narrow"),
        P("wide", None),
        P("wide", None),
        P("wide", None, "narrow"),
        P("wide", None, "narrow"),
        P("wide", "narrow", None),
    )
    out_specs = (P("wide", "narrow"), P("wide", None), P("wide", "narrow", None))
    return jax.shard_map(body, mesh=mesh, in_specs=in_specs, out_specs=out_specs, check_vma=False)
```

```python
import functools

import jax
import jax.numpy as jnp
from jax import lax
from jax.experimental import pallas as pl
from jax.experimental.pallas import tpu as pltpu
from jax.sharding import PartitionSpec as P

LANES = 128
CHUNKS = 2
bf16, f32 = jnp.bfloat16, jnp.float32


def dot(a, b, dims):
    return lax.dot_general(a, b, ((dims[0], dims[1]), ((), ())), preferred_element_type=f32)


def add(*terms):
    total = terms[0].astype(f32)
    for term in terms[1:]:
        total = total + term.astype(f32)
    return total.astype(terms[0].dtype)


def tile(size, most):
    fits = [t for t in range(LANES, min(size, most) + 1, LANES) if size % t == 0]
    return fits[-1] if fits else size


def call(kernel, flops, moved, **kwargs):
    return pl.pallas_call(
        kernel,
        compiler_params=pltpu.CompilerParams(vmem_limit_bytes=52 * 1024 * 1024),
        cost_estimate=pl.CostEstimate(flops=flops, bytes_accessed=moved, transcendentals=0),
        **kwargs,
    )


def whole(*shape):
    return pl.BlockSpec(shape, lambda i: (0,) * len(shape))


CORE, X, Y, Z = 1, 2, 4, 8


def flip(value, mask):
    count = lax.axis_size("wide")
    return lax.ppermute(value, "wide", [(i, i ^ mask) for i in range(count)])


def after(value, *deps):
    return lax.optimization_barrier((value, *deps))[0]


def depth():
    return lax.axis_size("wide") // Z


def gather_z(shard):
    return jnp.concatenate([shard] + [flip(shard, Z * k) for k in range(1, depth())], axis=0)


def gather_sides(first):
    return flip(first, X), flip(first, Y)


def gather_far(by_x, by_y):
    half = by_x.shape[0] // 2
    return [flip(by_y[:half], X), flip(by_x[half:], Y)]


def gather_core(pieces):
    return pieces + [flip(piece, CORE) for piece in pieces]


def offsets():
    return [Z * k + m + c for c in (0, CORE) for m in (0, X, Y, X | Y) for k in range(depth())]


def quarters(mine):
    size = mine.shape[0] // 4
    return [mine[k * size : (k + 1) * size] for k in range(4)]


def scatter_far(mine):
    first, by_x, by_y, far = quarters(mine)
    half = far.shape[0] // 2
    to_y, to_x = flip(far[:half], X), flip(far[half:], Y)
    by_y = jnp.concatenate([add(by_y[:half], to_y), by_y[half:]], axis=0)
    by_x = jnp.concatenate([by_x[:half], add(by_x[half:], to_x)], axis=0)
    return first, by_x, by_y


def send_sides(first, by_x, by_y):
    return [first, flip(by_x, X), flip(by_y, Y)]


def send_z(first):
    step = first.shape[0] // depth()
    blocks = [first[k * step : (k + 1) * step] for k in range(depth())]
    return [blocks[0]] + [flip(blocks[k], Z * k) for k in range(1, depth())]


def meta_kernel(sizes, cols, *refs):
    pieces, (out_ref, sems) = refs[: len(sizes)], refs[len(sizes) :]
    starts = [sum(sizes[:k]) for k in range(len(sizes))]
    copies = [
        pltpu.make_async_copy(
            pieces[k].at[:, pl.ds(cols, LANES)], out_ref.at[pl.ds(starts[k], sizes[k]), :], sems.at[k]
        )
        for k in range(len(sizes))
    ]
    for copy in copies:
        copy.start()
    for copy in copies:
        copy.wait()


def gather_meta(pieces, cols):
    sizes = [piece.shape[0] for piece in pieces]
    return call(
        functools.partial(meta_kernel, sizes, cols),
        0,
        4 * sum(sizes) * LANES,
        grid=(1,),
        in_specs=[pl.BlockSpec(memory_space=pl.ANY)] * len(pieces),
        out_specs=whole(sum(sizes), LANES),
        out_shape=jax.ShapeDtypeStruct((sum(sizes), LANES), bf16),
        scratch_shapes=[pltpu.SemaphoreType.DMA((len(sizes),))],
    )(*pieces)


def pick_kernel(sizes, block, slot_ref, *refs):
    pieces, (out_ref, held, place, sems) = refs[: len(sizes)], refs[len(sizes) :]
    step = pl.program_id(0)
    starts = [sum(sizes[:k]) for k in range(len(sizes))]

    def copy(at, k):
        return pltpu.make_async_copy(
            pieces[k].at[:, pl.ds(pl.multiple_of(at * block, LANES), block)],
            held.at[at, pl.ds(starts[k], sizes[k]), :],
            sems.at[at, k],
        )

    @pl.when(step == 0)
    def _():
        @pl.loop(0, pl.num_programs(0))
        def _(at):
            for k in range(len(sizes)):
                copy(at, k).start()

        rows = lax.broadcasted_iota(jnp.int32, place.shape, 0)
        place[...] = jnp.where(rows == slot_ref[...], 1.0, 0.0).astype(bf16)

    for k in range(len(sizes)):
        copy(step, k).wait()
    out_ref[...] = dot(place[...], held[step], ((1,), (0,))).astype(bf16)


def pick_rows(slot, pieces, rows, cols):
    sizes = [piece.shape[0] for piece in pieces]
    total = sum(sizes)
    block = tile(cols, 512)
    steps = cols // block
    return call(
        functools.partial(pick_kernel, sizes, block),
        2 * rows * total * cols,
        2 * (rows + total) * cols,
        grid=(steps,),
        in_specs=[whole(1, total)] + [pl.BlockSpec(memory_space=pl.ANY)] * len(pieces),
        out_specs=pl.BlockSpec((rows, block), lambda i: (0, i)),
        out_shape=jax.ShapeDtypeStruct((rows, cols), bf16),
        scratch_shapes=[
            pltpu.VMEM((steps, total, block), bf16),
            pltpu.VMEM((rows, total), bf16),
            pltpu.SemaphoreType.DMA((steps, len(sizes))),
        ],
    )(slot.reshape(1, total), *pieces)


def forward_kernel(x_ref, gate_ref, up_ref, hidden_ref, turned_ref, active_ref, pull_ref):
    gate_pre = dot(x_ref[...], gate_ref[...], ((1,), (0,)))
    up_pre = dot(x_ref[...], up_ref[...], ((1,), (0,)))
    sig = jax.nn.sigmoid(gate_pre)
    active = gate_pre * sig
    hidden = active * up_pre
    hidden_ref[...] = hidden.astype(bf16)
    turned_ref[...] = hidden.T.astype(bf16)
    active_ref[...] = active.astype(bf16)
    pull_ref[...] = (up_pre * (sig * (1.0 + gate_pre * (1.0 - sig)))).astype(bf16)


def forward(x, w_gate, w_up, low, high):
    rows, width = x.shape
    units = high - low
    block = tile(units, 256)
    first = low // block
    weight = pl.BlockSpec((width, block), lambda i: (0, first + i))
    unit = pl.BlockSpec((rows, block), lambda i: (0, i))
    turned = pl.BlockSpec((block, rows), lambda i: (i, 0))
    shape = jax.ShapeDtypeStruct((rows, units), bf16)
    return call(
        forward_kernel,
        4 * rows * width * units,
        4 * width * units,
        grid=(units // block,),
        in_specs=[whole(rows, width), weight, weight],
        out_specs=[unit, turned, unit, unit],
        out_shape=[shape, jax.ShapeDtypeStruct((units, rows), bf16), shape, shape],
    )(x, w_gate, w_up)


def back_kernel(steps, g_ref, gain_ref, down_ref, *refs):
    parts, (d_gate_ref, d_up_ref, route_ref) = refs[:-3], refs[-3:]
    step = pl.program_id(0)
    back = dot(g_ref[...], down_ref[...], ((1,), (1,)))
    d_hidden = gain_ref[...] * back

    @pl.when(step == 0)
    def _():
        route_ref[...] = jnp.zeros_like(route_ref)

    for k in range(len(parts) // 3):
        hidden_ref, active_ref, pull_ref = parts[3 * k : 3 * k + 3]

        @pl.when((step >= k * steps) & (step < (k + 1) * steps))
        def _(hidden_ref=hidden_ref, active_ref=active_ref, pull_ref=pull_ref):
            d_gate_ref[...] = (d_hidden * pull_ref[...].astype(f32)).astype(bf16)
            d_up_ref[...] = (d_hidden * active_ref[...].astype(f32)).astype(bf16)
            route_ref[...] += jnp.sum(hidden_ref[...].astype(f32) * back, axis=1, keepdims=True)


def back_project(g, gain, w_down, parts):
    rows, width = g.shape
    units = w_down.shape[0]
    block = tile(parts[0][0].shape[1], 256)
    steps = units // block // len(parts)
    unit = pl.BlockSpec((rows, block), lambda i: (0, i))

    def unit_of(part):
        return pl.BlockSpec((rows, block), lambda i: (0, jnp.clip(i - part * steps, 0, steps - 1)))

    shape = jax.ShapeDtypeStruct((rows, units), bf16)
    return call(
        functools.partial(back_kernel, steps),
        2 * rows * width * units,
        2 * width * units,
        grid=(units // block,),
        in_specs=[
            whole(rows, width),
            whole(rows, 1),
            pl.BlockSpec((block, width), lambda i: (i, 0)),
        ]
        + [unit_of(k) for k in range(len(parts)) for _ in range(3)],
        out_specs=[unit, unit, whole(rows, 1)],
        out_shape=[shape, shape, jax.ShapeDtypeStruct((rows, 1), f32)],
    )(g, gain, w_down, *[array for part in parts for array in part])


ANY = pl.BlockSpec(memory_space=pl.ANY)


def pick_phase(sizes, picks, slot_ref, pieces, x_out, scratch, start_weights):
    held, place, x, piece_sems, x_sems = scratch
    step = pl.program_id(0)
    width = held.shape[2]
    starts = [sum(sizes[:k]) for k in range(len(sizes))]

    def columns(at):
        return pl.ds(pl.multiple_of(at * width, LANES), width)

    def loads(at):
        return [
            pltpu.make_async_copy(
                pieces[k].at[:, columns(at)],
                held.at[at, pl.ds(starts[k], sizes[k]), :],
                piece_sems.at[at, k],
            )
            for k in range(len(sizes))
        ]

    def store(at):
        return pltpu.make_async_copy(x.at[:, columns(at)], x_out.at[:, columns(at)], x_sems.at[at])

    @pl.when(step == 0)
    def _():
        for at in range(min(2, picks)):
            for copy in loads(at):
                copy.start()
        rows = lax.broadcasted_iota(jnp.int32, place.shape, 0)
        place[...] = jnp.where(rows == slot_ref[...], 1.0, 0.0).astype(bf16)

    @pl.when(step + 2 < picks)
    def _():
        for copy in loads(step + 2):
            copy.start()

    @pl.when(step >= 1)
    def _():
        start_weights(step - 1)

    @pl.when(step < picks)
    def _():
        for copy in loads(step):
            copy.wait()
        x[:, columns(step)] = dot(place[...], held[step], ((1,), (0,))).astype(bf16)
        store(step).start()

    @pl.when(step == pl.num_programs(0) - 1)
    def _():
        for at in range(picks):
            store(at).wait()

    return x


def pick_scratch(rows, sizes, cols):
    block = tile(cols, 1024)
    picks = cols // block
    return picks, [
        pltpu.VMEM((picks, sum(sizes), block), bf16),
        pltpu.VMEM((rows, sum(sizes)), bf16),
        pltpu.VMEM((rows, cols), bf16),
        pltpu.SemaphoreType.DMA((picks, len(sizes))),
        pltpu.SemaphoreType.DMA((picks,)),
    ]


def pick_forward_kernel(sizes, picks, blocks, slot_ref, *refs):
    count = len(sizes)
    pieces, (gate_any, up_any, x_out, hidden_ref, turned_ref, active_ref, pull_ref) = refs[:count], refs[count : count + 7]
    *scratch, gates, ups, sems = refs[count + 7 :]
    step = pl.program_id(0)
    width = gates.shape[2]

    def weights(at):
        source = pl.ds(pl.multiple_of(at * width, LANES), width)
        return [
            pltpu.make_async_copy(gate_any.at[:, source], gates.at[at], sems.at[0, at]),
            pltpu.make_async_copy(up_any.at[:, source], ups.at[at], sems.at[1, at]),
        ]

    def start_weights(at):
        @pl.when(at < blocks)
        def _():
            for copy in weights(at):
                copy.start()

    x = pick_phase(sizes, picks, slot_ref, pieces, x_out, scratch, start_weights)

    @pl.when(step >= picks)
    def _():
        at = step - picks
        for copy in weights(at):
            copy.wait()
        forward_kernel(x, gates.at[at], ups.at[at], hidden_ref, turned_ref, active_ref, pull_ref)


def pick_forward(slot, pieces, rows, w_gate, w_up, units):
    sizes = [piece.shape[0] for piece in pieces]
    cols = w_gate.shape[0]
    picks, scratch = pick_scratch(rows, sizes, cols)
    block = tile(units, 256)
    blocks = units // block
    unit = pl.BlockSpec((rows, block), lambda i: (0, jnp.maximum(i - picks, 0)))
    turned = pl.BlockSpec((block, rows), lambda i: (jnp.maximum(i - picks, 0), 0))
    shape = jax.ShapeDtypeStruct((rows, units), bf16)
    x, *ahead = call(
        functools.partial(pick_forward_kernel, sizes, picks, blocks),
        4 * rows * cols * units + 2 * rows * sum(sizes) * cols,
        4 * cols * units + 2 * (rows + sum(sizes)) * cols,
        grid=(picks + blocks,),
        in_specs=[whole(1, sum(sizes))] + [ANY] * (len(sizes) + 2),
        out_specs=[ANY, unit, turned, unit, unit],
        out_shape=[
            jax.ShapeDtypeStruct((rows, cols), bf16),
            shape,
            jax.ShapeDtypeStruct((units, rows), bf16),
            shape,
            shape,
        ],
        scratch_shapes=scratch
        + [pltpu.VMEM((blocks, cols, block), bf16)] * 2
        + [pltpu.SemaphoreType.DMA((2, blocks))],
    )(slot.reshape(1, sum(sizes)), *pieces, w_gate, w_up)
    return x, ahead


def pick_back_kernel(sizes, picks, blocks, ranges, tokens, slot_ref, slot_col, gain_ref, expert_ref, *refs):
    count = len(sizes)
    pieces, (down_any, gate_any, up_any), refs = refs[:count], refs[count : count + 3], refs[count + 3 :]
    *refs, held, place, rows_ref, piece_sems, x_sems, downs, gates, ups, d_gate, d_up, sems, token_sems = refs
    *parts, g_out, route_ref, own_0, other_0, own_1, other_1 = refs
    step = pl.program_id(0)
    width, token_width = downs.shape[1], gates.shape[1]
    slots = gates.shape[0]
    base = picks + blocks

    def weights(at):
        source = down_any.at[pl.ds(pl.multiple_of(at * width, LANES), width), :]
        return [pltpu.make_async_copy(source, downs.at[at], sems.at[at])]

    def token_weights(at):
        source = pl.ds(pl.multiple_of(at * token_width, LANES), token_width)
        to = lax.rem(at, slots)
        return [
            pltpu.make_async_copy(gate_any.at[source, :], gates.at[to], token_sems.at[0, to]),
            pltpu.make_async_copy(up_any.at[source, :], ups.at[to], token_sems.at[1, to]),
        ]

    def start_weights(at):
        @pl.when(at < blocks)
        def _():
            for copy in weights(at):
                copy.start()

        @pl.when((at >= blocks) & (at < blocks + tokens))
        def _():
            for copy in token_weights(at - blocks):
                copy.start()

    scratch = (held, place, rows_ref, piece_sems, x_sems)
    g = pick_phase(sizes, picks, slot_ref, pieces, g_out, scratch, start_weights)

    @pl.when(step == 0)
    def _():
        route_ref[...] = jnp.zeros_like(route_ref)

    for k, (low, high) in enumerate(ranges):
        hidden_ref, active_ref, pull_ref = parts[3 * k : 3 * k + 3]

        @pl.when((step >= picks + low) & (step < picks + high))
        def _(hidden_ref=hidden_ref, active_ref=active_ref, pull_ref=pull_ref):
            at = step - picks
            for copy in weights(at):
                copy.wait()
            back = dot(g[...], downs[at], ((1,), (1,)))
            d_hidden = gain_ref[...] * back
            units = pl.ds(pl.multiple_of(at * width, LANES), width)
            d_gate[:, units] = (d_hidden * pull_ref[...].astype(f32)).astype(bf16)
            d_up[:, units] = (d_hidden * active_ref[...].astype(f32)).astype(bf16)
            route_ref[...] += jnp.sum(hidden_ref[...].astype(f32) * back, axis=1, keepdims=True)

    @pl.when((step >= base) & (step < base + tokens))
    def _():
        at = step - base
        for copy in token_weights(at):
            copy.wait()
        to = lax.rem(at, slots)
        part = dot(d_gate[...], gates[to], ((1,), (1,)))
        part = (part + dot(d_up[...], ups[to], ((1,), (1,)))).astype(bf16)

        @pl.when(at < tokens // 2)
        def _():
            spread_rows(slot_col, part, (own_0, other_0))

        @pl.when(at >= tokens // 2)
        def _():
            spread_rows(slot_col, part, (own_1, other_1))

    @pl.when(step == base + tokens)
    def _():
        route = route_ref[...].astype(bf16).astype(f32)
        lanes = lax.broadcasted_iota(jnp.int32, (route.shape[0], LANES), 1)
        columns = jnp.where(lanes == expert_ref[...], route, 0.0).astype(bf16)
        spread_rows(slot_col, columns, (own_1, other_1))


def pick_back(slot, pieces, gain, expert, w_down, w_gate, w_up, parts):
    sizes = [piece.shape[0] for piece in pieces]
    total = sum(sizes)
    rows = gain.shape[0]
    units, cols = w_down.shape
    picks, scratch = pick_scratch(rows, sizes, cols)
    block = min(tile(part[0].shape[1], 256) for part in parts)
    blocks = units // block
    ends = [sum(part[0].shape[1] for part in parts[: k + 1]) // block for k in range(len(parts))]
    ranges = list(zip([0] + ends[:-1], ends))
    token_block = tile(cols, 512)
    tokens = cols // token_block
    half = tokens // 2
    base = picks + blocks
    dense_0 = pl.BlockSpec((total // 2, token_block), lambda i: (0, jnp.clip(i - base, 0, half - 1)))
    dense_1 = pl.BlockSpec((total // 2, token_block), lambda i: (0, jnp.maximum(i - base - half, 0)))

    def unit_of(part):
        return pl.BlockSpec((rows, block), lambda i: (0, jnp.clip(i - picks - part[0], 0, part[1] - part[0] - 1)))

    return call(
        functools.partial(pick_back_kernel, sizes, picks, blocks, ranges, tokens),
        2 * rows * (3 * cols * units + 2 * total * cols),
        6 * cols * units + 2 * (rows + 2 * total) * cols,
        grid=(base + tokens + 1,),
        in_specs=[whole(1, total), whole(total, 1), whole(rows, 1), whole(1, 1)]
        + [ANY] * (len(sizes) + 3)
        + [unit_of(part) for part in ranges for _ in range(3)],
        out_specs=[ANY, whole(rows, 1), dense_0, dense_0, dense_1, dense_1],
        out_shape=[jax.ShapeDtypeStruct((rows, cols), bf16), jax.ShapeDtypeStruct((rows, 1), f32)]
        + [jax.ShapeDtypeStruct((total // 2, half * token_block), bf16)] * 2
        + [jax.ShapeDtypeStruct((total // 2, cols - half * token_block + LANES), bf16)] * 2,
        scratch_shapes=scratch
        + [pltpu.VMEM((blocks, block, cols), bf16)]
        + [pltpu.VMEM((picks, token_block, units), bf16)] * 2
        + [pltpu.VMEM((rows, units), bf16)] * 2
        + [pltpu.SemaphoreType.DMA((blocks,)), pltpu.SemaphoreType.DMA((2, picks))],
    )(
        slot.reshape(1, total),
        slot.reshape(total, 1),
        gain,
        expert.reshape(1, 1),
        *pieces,
        w_down,
        w_gate,
        w_up,
        *[array for part in parts for array in part],
    )


def spread_rows(slot_ref, part, outs):
    half = slot_ref.shape[0] // 2
    rows, width = part.shape
    for k in range(2):
        slot = slot_ref[k * half : (k + 1) * half, :]
        lanes = lax.broadcasted_iota(jnp.int32, (half, rows), 1)
        place = jnp.where(lanes == slot, 1.0, 0.0).astype(bf16)
        outs[k][:, :width] = dot(place, part, ((1,), (0,))).astype(bf16)


def token_kernel(steps, spread, d_gate_ref, d_up_ref, slot_ref, route_ref, gate_ref, up_ref, *outs):
    step = pl.program_id(0)

    def store(part):
        if spread:
            spread_rows(slot_ref, part, outs)
        else:
            outs[0][...] = part

    @pl.when(step < steps)
    def _():
        part = dot(d_gate_ref[...], gate_ref[...], ((1,), (1,)))
        store((part + dot(d_up_ref[...], up_ref[...], ((1,), (1,)))).astype(bf16))

    if spread:

        @pl.when(step >= steps)
        def _():
            store(route_ref[...])


def token_grad(d_gate, d_up, slot, route, w_gate, w_up, chunk, chunks, spread):
    rows, units = d_gate.shape
    width = w_gate.shape[0] // chunks
    total = slot.shape[0]
    block = tile(width, 512)
    steps = width // block
    first = chunk * steps
    extra = route.shape[1] if spread and chunk == chunks - 1 else 0
    weight = pl.BlockSpec((block, units), lambda i: (first + jnp.minimum(i, steps - 1), 0))
    out_rows = [total // 2] * 2 if spread else [rows]
    return call(
        functools.partial(token_kernel, steps, spread),
        4 * rows * width * units + 2 * rows * width * total * spread,
        4 * width * units + 2 * total * width,
        grid=(steps + (extra > 0),),
        in_specs=[whole(rows, units), whole(rows, units), whole(total, 1), whole(*route.shape), weight, weight],
        out_specs=[pl.BlockSpec((n, block), lambda i: (0, i)) for n in out_rows],
        out_shape=[jax.ShapeDtypeStruct((n, width + extra), bf16) for n in out_rows],
    )(d_gate, d_up, slot.reshape(total, 1), route, w_gate, w_up)


def down_kernel(count, g_ref, gain_ref, *refs):
    turned, out_ref = refs[:count], refs[-1]
    scaled = (gain_ref[...] * g_ref[...].astype(f32)).astype(bf16)
    at = 0
    for ref in turned:
        out_ref[at : at + ref.shape[0], :] = dot(ref[...], scaled, ((1,), (0,))).astype(bf16)
        at += ref.shape[0]


def down_grad(turned, g, gain, chunk, chunks, into):
    rows, width = g.shape
    units = sum(part.shape[0] for part in turned)
    block = tile(width // chunks, 512)
    steps = width // chunks // block
    first = chunk * steps
    kept = [] if into is None else [into]
    return call(
        functools.partial(down_kernel, len(turned)),
        2 * rows * width * units // chunks,
        2 * width * units // chunks,
        grid=(steps,),
        in_specs=[pl.BlockSpec((rows, block), lambda i: (0, first + i)), whole(rows, 1)]
        + [whole(*part.shape) for part in turned]
        + [pl.BlockSpec(memory_space=pl.ANY)] * len(kept),
        out_specs=pl.BlockSpec((units, block), lambda i: (0, first + i)),
        out_shape=jax.ShapeDtypeStruct((units, width), bf16),
        input_output_aliases={2 + len(turned): 0} if kept else {},
    )(g, gain, *turned, *kept)


def body(tokens, grad_out, expert_ids, route_weights, w_gate, w_up, w_down):
    wide_count = lax.axis_size("wide")
    narrow_count = lax.axis_size("narrow")
    local_experts = w_gate.shape[0]
    experts_all = local_experts * wide_count
    tok_count, top_count = expert_ids.shape
    capacity = min(tok_count, 2 * tok_count * top_count // experts_all)
    rows = wide_count * capacity
    total = wide_count * tok_count
    cols = tokens.shape[1]
    me = lax.axis_index("wide")
    pad = -2 * top_count % LANES
    meta = jnp.concatenate(
        [expert_ids.astype(bf16), route_weights, jnp.zeros((tok_count, pad), bf16)], axis=1
    )
    first_t = gather_z(jnp.concatenate([tokens, meta], axis=1))
    x_t, y_t = gather_sides(first_t)
    first_g = gather_z(after(grad_out, first_t))
    far_t = gather_far(x_t, y_t)
    x_g, y_g = gather_sides(after(first_g, *far_t))
    pieces_t = gather_core([first_t, x_t, y_t] + far_t)
    all_meta = gather_meta(pieces_t, cols)
    all_ids = all_meta[:, :top_count].astype(jnp.int32)
    all_weights = all_meta[:, top_count : 2 * top_count].astype(f32)
    first = me * local_experts
    fused = narrow_count == 1 and local_experts == 1 and experts_all <= LANES
    chunks = CHUNKS if fused else 1
    units = w_gate.shape[2]
    ahead_units = units * 2 // 3 if fused and units % (6 * LANES) == 0 else units
    picked = []
    for j in range(local_experts):
        match = all_ids == first + j
        chosen = jnp.any(match, axis=1)
        gain = jnp.sum(jnp.where(match, all_weights, 0.0), axis=1)
        rank = jnp.cumsum(chosen.astype(jnp.int32)) - 1
        slot = jnp.where(chosen, rank, -1)
        place = slot[None, :] == jnp.arange(rows, dtype=jnp.int32)[:, None]
        row_gain = jnp.sum(jnp.where(place, gain[None, :], 0.0), axis=1, keepdims=True)
        if fused:
            x, first_part = pick_forward(slot, pieces_t, rows, w_gate[j], w_up[j], ahead_units)
        else:
            x = pick_rows(slot, pieces_t, rows, cols)
            x = lax.all_gather(x, "narrow", axis=1, tiled=True)
            first_part = forward(x, w_gate[j], w_up[j], 0, ahead_units)
        ahead = [first_part]
        picked.append((slot, place, row_gain, x, ahead))
    x_g, y_g, *_ = lax.optimization_barrier((x_g, y_g, *[ahead[0][0] for *_, ahead in picked]))
    far_g = gather_far(x_g, y_g)
    for j in range(local_experts):
        slot, place, row_gain, x, ahead = picked[j]
        if ahead_units < units:
            ahead.append(forward(after(x, x_g, y_g), w_gate[j], w_up[j], ahead_units, units))
    far_g = lax.optimization_barrier((*far_g, *[ahead[-1][0] for *_, ahead in picked]))[: len(far_g)]
    pieces_g = gather_core([first_g, x_g, y_g, *far_g])
    expert_cols = experts_all + -experts_all % LANES
    dense = [0, 0]
    route_all = 0
    ends = []
    for j in range(local_experts):
        slot, place, row_gain, x, ahead = picked[j]
        straight = [(hidden, active, pull) for hidden, _, active, pull in ahead]
        if fused:
            g, _, *dense = pick_back(
                slot, pieces_g, row_gain, first + j, w_down[j], w_gate[j], w_up[j], straight
            )
            ends.append(([part[1] for part in ahead], g, row_gain))
            continue
        g = pick_rows(slot, pieces_g, rows, cols)
        g = lax.all_gather(g, "narrow", axis=1, tiled=True)
        d_gate, d_up, route = back_project(g, row_gain, w_down[j], straight)
        route = lax.psum(route.astype(bf16).astype(f32), "narrow")
        at = jnp.arange(expert_cols, dtype=jnp.int32) == first + j
        route = jnp.where(at[None, :], route, 0.0).astype(bf16)
        ends.append(([part[1] for part in ahead], g, row_gain))
        (part,) = token_grad(d_gate, d_up, slot, route, w_gate[j], w_up[j], 0, 1, False)
        part = lax.psum_scatter(part, "narrow", scatter_dimension=1, tiled=True)
        part = jnp.concatenate([part, route], axis=1)
        part = dot(place.astype(bf16), part, ((0,), (0,)))
        dense = [dense[0] + part[: total // 2], dense[1] + part[total // 2 :]]
    grad_downs = []
    if fused:
        (turned, g, row_gain), = ends
        out = down_grad(turned, g, row_gain, 0, 4, None)
        dense[0], out = lax.optimization_barrier((dense[0], out))
        mine = [add(dense[k], flip(dense[k + 1], CORE)) for k in (0, 2)]
        out = down_grad(turned, after(g, mine[1]), row_gain, 1, 4, out)
        sides = [scatter_far(rows_) for rows_ in mine]
        sent = [send_sides(*side) for side in sides]
        out = down_grad(turned, after(g, sides[1][1]), row_gain, 2, 4, out)
        *sent[0], out = lax.optimization_barrier((*sent[0], out))
        firsts = [add(*rows_) for rows_ in sent]
        shares = [send_z(first_) for first_ in firsts]
        shares[0] = [after(block, firsts[1]) for block in shares[0]]
        out = down_grad(turned, after(g, firsts[1]), row_gain, 3, 4, out)
        shares = [add(*share) for share in shares]
        grad_downs.append(out)
    else:
        mine = add(dense[0].astype(bf16), flip(dense[1].astype(bf16), CORE))
        shares = [add(*send_z(add(*send_sides(*scatter_far(mine)))))]
        grad_downs += [down_grad(*end, 0, 1, None) for end in ends]
    joined = jnp.concatenate(shares, axis=1)
    width = tokens.shape[1]
    by_expert = joined[:, width : width + experts_all].astype(f32)
    pick = expert_ids[:, :, None] == jnp.arange(experts_all, dtype=jnp.int32)[None, None, :]
    grad_route = jnp.sum(jnp.where(pick, by_expert[:, None, :], 0.0), axis=2)
    return (joined[:, :width], grad_route.astype(bf16), jnp.stack(grad_downs))


def solution(mesh):
    in_specs = (
        P("wide", "narrow"),
        P("wide", "narrow"),
        P("wide", None),
        P("wide", None),
        P("wide", None, "narrow"),
        P("wide", None, "narrow"),
        P("wide", "narrow", None),
    )
    out_specs = (P("wide", "narrow"), P("wide", None), P("wide", "narrow", None))
    return jax.shard_map(body, mesh=mesh, in_specs=in_specs, out_specs=out_specs, check_vma=False)
```

```python
import functools

import jax
import jax.numpy as jnp
from jax import lax
from jax.experimental import pallas as pl
from jax.experimental.pallas import tpu as pltpu
from jax.sharding import PartitionSpec as P

LANES = 128
CHUNKS = 2
bf16, f32 = jnp.bfloat16, jnp.float32


def dot(a, b, dims):
    return lax.dot_general(a, b, ((dims[0], dims[1]), ((), ())), preferred_element_type=f32)


def add(*terms):
    total = terms[0].astype(f32)
    for term in terms[1:]:
        total = total + term.astype(f32)
    return total.astype(terms[0].dtype)


def tile(size, most):
    fits = [t for t in range(LANES, min(size, most) + 1, LANES) if size % t == 0]
    return fits[-1] if fits else size


def call(kernel, flops, moved, **kwargs):
    return pl.pallas_call(
        kernel,
        compiler_params=pltpu.CompilerParams(vmem_limit_bytes=52 * 1024 * 1024),
        cost_estimate=pl.CostEstimate(flops=flops, bytes_accessed=moved, transcendentals=0),
        **kwargs,
    )


def whole(*shape):
    return pl.BlockSpec(shape, lambda i: (0,) * len(shape))


CORE, X, Y, Z = 1, 2, 4, 8


def flip(value, mask):
    count = lax.axis_size("wide")
    return lax.ppermute(value, "wide", [(i, i ^ mask) for i in range(count)])


def after(value, *deps):
    return lax.optimization_barrier((value, *deps))[0]


def depth():
    return lax.axis_size("wide") // Z


def gather_z(shard):
    return jnp.concatenate([shard] + [flip(shard, Z * k) for k in range(1, depth())], axis=0)


def gather_sides(first):
    return flip(first, X), flip(first, Y)


def gather_far(by_x, by_y):
    half = by_x.shape[0] // 2
    return [flip(by_y[:half], X), flip(by_x[half:], Y)]


def gather_core(pieces):
    return pieces + [flip(piece, CORE) for piece in pieces]


def offsets():
    return [Z * k + m + c for c in (0, CORE) for m in (0, X, Y, X | Y) for k in range(depth())]


def quarters(mine):
    size = mine.shape[0] // 4
    return [mine[k * size : (k + 1) * size] for k in range(4)]


def scatter_far(mine):
    first, by_x, by_y, far = quarters(mine)
    half = far.shape[0] // 2
    to_y, to_x = flip(far[:half], X), flip(far[half:], Y)
    by_y = jnp.concatenate([add(by_y[:half], to_y), by_y[half:]], axis=0)
    by_x = jnp.concatenate([by_x[:half], add(by_x[half:], to_x)], axis=0)
    return first, by_x, by_y


def send_sides(first, by_x, by_y):
    return [first, flip(by_x, X), flip(by_y, Y)]


def send_z(first):
    step = first.shape[0] // depth()
    blocks = [first[k * step : (k + 1) * step] for k in range(depth())]
    return [blocks[0]] + [flip(blocks[k], Z * k) for k in range(1, depth())]


def meta_kernel(sizes, cols, *refs):
    pieces, (out_ref, sems) = refs[: len(sizes)], refs[len(sizes) :]
    starts = [sum(sizes[:k]) for k in range(len(sizes))]
    copies = [
        pltpu.make_async_copy(
            pieces[k].at[:, pl.ds(cols, LANES)], out_ref.at[pl.ds(starts[k], sizes[k]), :], sems.at[k]
        )
        for k in range(len(sizes))
    ]
    for copy in copies:
        copy.start()
    for copy in copies:
        copy.wait()


def gather_meta(pieces, cols):
    sizes = [piece.shape[0] for piece in pieces]
    return call(
        functools.partial(meta_kernel, sizes, cols),
        0,
        4 * sum(sizes) * LANES,
        grid=(1,),
        in_specs=[pl.BlockSpec(memory_space=pl.ANY)] * len(pieces),
        out_specs=whole(sum(sizes), LANES),
        out_shape=jax.ShapeDtypeStruct((sum(sizes), LANES), bf16),
        scratch_shapes=[pltpu.SemaphoreType.DMA((len(sizes),))],
    )(*pieces)


def pick_kernel(sizes, block, slot_ref, *refs):
    pieces, (out_ref, held, place, sems) = refs[: len(sizes)], refs[len(sizes) :]
    step = pl.program_id(0)
    starts = [sum(sizes[:k]) for k in range(len(sizes))]

    def copy(at, k):
        return pltpu.make_async_copy(
            pieces[k].at[:, pl.ds(pl.multiple_of(at * block, LANES), block)],
            held.at[at, pl.ds(starts[k], sizes[k]), :],
            sems.at[at, k],
        )

    @pl.when(step == 0)
    def _():
        @pl.loop(0, pl.num_programs(0))
        def _(at):
            for k in range(len(sizes)):
                copy(at, k).start()

        rows = lax.broadcasted_iota(jnp.int32, place.shape, 0)
        place[...] = jnp.where(rows == slot_ref[...], 1.0, 0.0).astype(bf16)

    for k in range(len(sizes)):
        copy(step, k).wait()
    out_ref[...] = dot(place[...], held[step], ((1,), (0,))).astype(bf16)


def pick_rows(slot, pieces, rows, cols):
    sizes = [piece.shape[0] for piece in pieces]
    total = sum(sizes)
    block = tile(cols, 512)
    steps = cols // block
    return call(
        functools.partial(pick_kernel, sizes, block),
        2 * rows * total * cols,
        2 * (rows + total) * cols,
        grid=(steps,),
        in_specs=[whole(1, total)] + [pl.BlockSpec(memory_space=pl.ANY)] * len(pieces),
        out_specs=pl.BlockSpec((rows, block), lambda i: (0, i)),
        out_shape=jax.ShapeDtypeStruct((rows, cols), bf16),
        scratch_shapes=[
            pltpu.VMEM((steps, total, block), bf16),
            pltpu.VMEM((rows, total), bf16),
            pltpu.SemaphoreType.DMA((steps, len(sizes))),
        ],
    )(slot.reshape(1, total), *pieces)


def forward_kernel(x_ref, gate_ref, up_ref, hidden_ref, turned_ref, active_ref, pull_ref):
    gate_pre = dot(x_ref[...], gate_ref[...], ((1,), (0,)))
    up_pre = dot(x_ref[...], up_ref[...], ((1,), (0,)))
    sig = jax.nn.sigmoid(gate_pre)
    active = gate_pre * sig
    hidden = active * up_pre
    hidden_ref[...] = hidden.astype(bf16)
    turned_ref[...] = hidden.T.astype(bf16)
    active_ref[...] = active.astype(bf16)
    pull_ref[...] = (up_pre * (sig * (1.0 + gate_pre * (1.0 - sig)))).astype(bf16)


def forward(x, w_gate, w_up, low, high):
    rows, width = x.shape
    units = high - low
    block = tile(units, 256)
    first = low // block
    weight = pl.BlockSpec((width, block), lambda i: (0, first + i))
    unit = pl.BlockSpec((rows, block), lambda i: (0, i))
    turned = pl.BlockSpec((block, rows), lambda i: (i, 0))
    shape = jax.ShapeDtypeStruct((rows, units), bf16)
    return call(
        forward_kernel,
        4 * rows * width * units,
        4 * width * units,
        grid=(units // block,),
        in_specs=[whole(rows, width), weight, weight],
        out_specs=[unit, turned, unit, unit],
        out_shape=[shape, jax.ShapeDtypeStruct((units, rows), bf16), shape, shape],
    )(x, w_gate, w_up)


def back_kernel(steps, g_ref, gain_ref, down_ref, *refs):
    parts, (d_gate_ref, d_up_ref, route_ref) = refs[:-3], refs[-3:]
    step = pl.program_id(0)
    back = dot(g_ref[...], down_ref[...], ((1,), (1,)))
    d_hidden = gain_ref[...] * back

    @pl.when(step == 0)
    def _():
        route_ref[...] = jnp.zeros_like(route_ref)

    for k in range(len(parts) // 3):
        hidden_ref, active_ref, pull_ref = parts[3 * k : 3 * k + 3]

        @pl.when((step >= k * steps) & (step < (k + 1) * steps))
        def _(hidden_ref=hidden_ref, active_ref=active_ref, pull_ref=pull_ref):
            d_gate_ref[...] = (d_hidden * pull_ref[...].astype(f32)).astype(bf16)
            d_up_ref[...] = (d_hidden * active_ref[...].astype(f32)).astype(bf16)
            route_ref[...] += jnp.sum(hidden_ref[...].astype(f32) * back, axis=1, keepdims=True)


def back_project(g, gain, w_down, parts):
    rows, width = g.shape
    units = w_down.shape[0]
    block = tile(parts[0][0].shape[1], 256)
    steps = units // block // len(parts)
    unit = pl.BlockSpec((rows, block), lambda i: (0, i))

    def unit_of(part):
        return pl.BlockSpec((rows, block), lambda i: (0, jnp.clip(i - part * steps, 0, steps - 1)))

    shape = jax.ShapeDtypeStruct((rows, units), bf16)
    return call(
        functools.partial(back_kernel, steps),
        2 * rows * width * units,
        2 * width * units,
        grid=(units // block,),
        in_specs=[
            whole(rows, width),
            whole(rows, 1),
            pl.BlockSpec((block, width), lambda i: (i, 0)),
        ]
        + [unit_of(k) for k in range(len(parts)) for _ in range(3)],
        out_specs=[unit, unit, whole(rows, 1)],
        out_shape=[shape, shape, jax.ShapeDtypeStruct((rows, 1), f32)],
    )(g, gain, w_down, *[array for part in parts for array in part])


ANY = pl.BlockSpec(memory_space=pl.ANY)


def pick_phase(sizes, picks, slot_ref, pieces, x_out, scratch, start_weights):
    held, place, x, piece_sems, x_sems = scratch
    step = pl.program_id(0)
    width = held.shape[2]
    starts = [sum(sizes[:k]) for k in range(len(sizes))]

    def columns(at):
        return pl.ds(pl.multiple_of(at * width, LANES), width)

    def loads(at):
        return [
            pltpu.make_async_copy(
                pieces[k].at[:, columns(at)],
                held.at[at, pl.ds(starts[k], sizes[k]), :],
                piece_sems.at[at, k],
            )
            for k in range(len(sizes))
        ]

    def store(at):
        return pltpu.make_async_copy(x.at[:, columns(at)], x_out.at[:, columns(at)], x_sems.at[at])

    @pl.when(step == 0)
    def _():
        for at in range(min(2, picks)):
            for copy in loads(at):
                copy.start()
        rows = lax.broadcasted_iota(jnp.int32, place.shape, 0)
        place[...] = jnp.where(rows == slot_ref[...], 1.0, 0.0).astype(bf16)

    @pl.when(step + 2 < picks)
    def _():
        for copy in loads(step + 2):
            copy.start()

    @pl.when(step >= 1)
    def _():
        start_weights(step - 1)

    @pl.when(step < picks)
    def _():
        for copy in loads(step):
            copy.wait()
        x[:, columns(step)] = dot(place[...], held[step], ((1,), (0,))).astype(bf16)
        store(step).start()

    @pl.when(step == pl.num_programs(0) - 1)
    def _():
        for at in range(picks):
            store(at).wait()

    return x


def pick_scratch(rows, sizes, cols):
    block = tile(cols, 1024)
    picks = cols // block
    return picks, [
        pltpu.VMEM((picks, sum(sizes), block), bf16),
        pltpu.VMEM((rows, sum(sizes)), bf16),
        pltpu.VMEM((rows, cols), bf16),
        pltpu.SemaphoreType.DMA((picks, len(sizes))),
        pltpu.SemaphoreType.DMA((picks,)),
    ]


def pick_forward_kernel(sizes, picks, blocks, slot_ref, *refs):
    count = len(sizes)
    pieces, (gate_any, up_any, x_out, hidden_ref, turned_ref, active_ref, pull_ref) = refs[:count], refs[count : count + 7]
    *scratch, gates, ups, sems = refs[count + 7 :]
    step = pl.program_id(0)
    width = gates.shape[2]

    def weights(at):
        source = pl.ds(pl.multiple_of(at * width, LANES), width)
        return [
            pltpu.make_async_copy(gate_any.at[:, source], gates.at[at], sems.at[0, at]),
            pltpu.make_async_copy(up_any.at[:, source], ups.at[at], sems.at[1, at]),
        ]

    def start_weights(at):
        @pl.when(at < blocks)
        def _():
            for copy in weights(at):
                copy.start()

    x = pick_phase(sizes, picks, slot_ref, pieces, x_out, scratch, start_weights)

    @pl.when(step >= picks)
    def _():
        at = step - picks
        for copy in weights(at):
            copy.wait()
        forward_kernel(x, gates.at[at], ups.at[at], hidden_ref, turned_ref, active_ref, pull_ref)


def pick_forward(slot, pieces, rows, w_gate, w_up, units):
    sizes = [piece.shape[0] for piece in pieces]
    cols = w_gate.shape[0]
    picks, scratch = pick_scratch(rows, sizes, cols)
    block = tile(units, 256)
    blocks = units // block
    unit = pl.BlockSpec((rows, block), lambda i: (0, jnp.maximum(i - picks, 0)))
    turned = pl.BlockSpec((block, rows), lambda i: (jnp.maximum(i - picks, 0), 0))
    shape = jax.ShapeDtypeStruct((rows, units), bf16)
    x, *ahead = call(
        functools.partial(pick_forward_kernel, sizes, picks, blocks),
        4 * rows * cols * units + 2 * rows * sum(sizes) * cols,
        4 * cols * units + 2 * (rows + sum(sizes)) * cols,
        grid=(picks + blocks,),
        in_specs=[whole(1, sum(sizes))] + [ANY] * (len(sizes) + 2),
        out_specs=[ANY, unit, turned, unit, unit],
        out_shape=[
            jax.ShapeDtypeStruct((rows, cols), bf16),
            shape,
            jax.ShapeDtypeStruct((units, rows), bf16),
            shape,
            shape,
        ],
        scratch_shapes=scratch
        + [pltpu.VMEM((blocks, cols, block), bf16)] * 2
        + [pltpu.SemaphoreType.DMA((2, blocks))],
    )(slot.reshape(1, sum(sizes)), *pieces, w_gate, w_up)
    return x, ahead


def pick_back_kernel(sizes, picks, blocks, ranges, tokens, half, slot_ref, slot_col, gain_ref, expert_ref, *refs):
    count = len(sizes)
    pieces, (down_any, gate_any, up_any), refs = refs[:count], refs[count : count + 3], refs[count + 3 :]
    *refs, held, place, rows_ref, piece_sems, x_sems, downs, gates, ups, d_gate, d_up, sems, token_sems = refs
    *parts, g_out, route_ref, own_0, other_0, own_1, other_1 = refs
    step = pl.program_id(0)
    width, token_width = downs.shape[1], gates.shape[1]
    slots = gates.shape[0]
    base = picks + blocks

    def weights(at):
        source = down_any.at[pl.ds(pl.multiple_of(at * width, LANES), width), :]
        return [pltpu.make_async_copy(source, downs.at[at], sems.at[at])]

    def token_weights(at):
        source = pl.ds(pl.multiple_of(at * token_width, LANES), token_width)
        to = lax.rem(at, slots)
        return [
            pltpu.make_async_copy(gate_any.at[source, :], gates.at[to], token_sems.at[0, to]),
            pltpu.make_async_copy(up_any.at[source, :], ups.at[to], token_sems.at[1, to]),
        ]

    def start_weights(at):
        @pl.when(at < blocks)
        def _():
            for copy in weights(at):
                copy.start()

        @pl.when((at >= blocks) & (at < blocks + tokens))
        def _():
            for copy in token_weights(at - blocks):
                copy.start()

    scratch = (held, place, rows_ref, piece_sems, x_sems)
    g = pick_phase(sizes, picks, slot_ref, pieces, g_out, scratch, start_weights)

    @pl.when(step == 0)
    def _():
        route_ref[...] = jnp.zeros_like(route_ref)

    for k, (low, high) in enumerate(ranges):
        hidden_ref, active_ref, pull_ref = parts[3 * k : 3 * k + 3]

        @pl.when((step >= picks + low) & (step < picks + high))
        def _(hidden_ref=hidden_ref, active_ref=active_ref, pull_ref=pull_ref):
            at = step - picks
            for copy in weights(at):
                copy.wait()
            back = dot(g[...], downs[at], ((1,), (1,)))
            d_hidden = gain_ref[...] * back
            units = pl.ds(pl.multiple_of(at * width, LANES), width)
            d_gate[:, units] = (d_hidden * pull_ref[...].astype(f32)).astype(bf16)
            d_up[:, units] = (d_hidden * active_ref[...].astype(f32)).astype(bf16)
            route_ref[...] += jnp.sum(hidden_ref[...].astype(f32) * back, axis=1, keepdims=True)

    @pl.when((step >= base) & (step < base + tokens))
    def _():
        at = step - base
        for copy in token_weights(at):
            copy.wait()
        to = lax.rem(at, slots)
        part = dot(d_gate[...], gates[to], ((1,), (1,)))
        part = (part + dot(d_up[...], ups[to], ((1,), (1,)))).astype(bf16)

        @pl.when(at < half)
        def _():
            spread_rows(slot_col, part, (own_0, other_0))

        @pl.when(at >= half)
        def _():
            spread_rows(slot_col, part, (own_1, other_1))

    @pl.when(step == base + tokens)
    def _():
        route = route_ref[...].astype(bf16).astype(f32)
        lanes = lax.broadcasted_iota(jnp.int32, (route.shape[0], LANES), 1)
        columns = jnp.where(lanes == expert_ref[...], route, 0.0).astype(bf16)
        spread_rows(slot_col, columns, (own_1, other_1))


def pick_back(slot, pieces, gain, expert, w_down, w_gate, w_up, parts):
    sizes = [piece.shape[0] for piece in pieces]
    total = sum(sizes)
    rows = gain.shape[0]
    units, cols = w_down.shape
    picks, scratch = pick_scratch(rows, sizes, cols)
    block = min(tile(part[0].shape[1], 256) for part in parts)
    blocks = units // block
    ends = [sum(part[0].shape[1] for part in parts[: k + 1]) // block for k in range(len(parts))]
    ranges = list(zip([0] + ends[:-1], ends))
    token_block = tile(cols, 512)
    tokens = cols // token_block
    half = tokens * 5 // 8
    base = picks + blocks
    dense_0 = pl.BlockSpec((total // 2, token_block), lambda i: (0, jnp.clip(i - base, 0, half - 1)))
    dense_1 = pl.BlockSpec((total // 2, token_block), lambda i: (0, jnp.maximum(i - base - half, 0)))

    def unit_of(part):
        return pl.BlockSpec((rows, block), lambda i: (0, jnp.clip(i - picks - part[0], 0, part[1] - part[0] - 1)))

    return call(
        functools.partial(pick_back_kernel, sizes, picks, blocks, ranges, tokens, half),
        2 * rows * (3 * cols * units + 2 * total * cols),
        6 * cols * units + 2 * (rows + 2 * total) * cols,
        grid=(base + tokens + 1,),
        in_specs=[whole(1, total), whole(total, 1), whole(rows, 1), whole(1, 1)]
        + [ANY] * (len(sizes) + 3)
        + [unit_of(part) for part in ranges for _ in range(3)],
        out_specs=[ANY, whole(rows, 1), dense_0, dense_0, dense_1, dense_1],
        out_shape=[jax.ShapeDtypeStruct((rows, cols), bf16), jax.ShapeDtypeStruct((rows, 1), f32)]
        + [jax.ShapeDtypeStruct((total // 2, half * token_block), bf16)] * 2
        + [jax.ShapeDtypeStruct((total // 2, cols - half * token_block + LANES), bf16)] * 2,
        scratch_shapes=scratch
        + [pltpu.VMEM((blocks, block, cols), bf16)]
        + [pltpu.VMEM((picks, token_block, units), bf16)] * 2
        + [pltpu.VMEM((rows, units), bf16)] * 2
        + [pltpu.SemaphoreType.DMA((blocks,)), pltpu.SemaphoreType.DMA((2, picks))],
    )(
        slot.reshape(1, total),
        slot.reshape(total, 1),
        gain,
        expert.reshape(1, 1),
        *pieces,
        w_down,
        w_gate,
        w_up,
        *[array for part in parts for array in part],
    )


def spread_rows(slot_ref, part, outs):
    half = slot_ref.shape[0] // 2
    rows, width = part.shape
    for k in range(2):
        slot = slot_ref[k * half : (k + 1) * half, :]
        lanes = lax.broadcasted_iota(jnp.int32, (half, rows), 1)
        place = jnp.where(lanes == slot, 1.0, 0.0).astype(bf16)
        outs[k][:, :width] = dot(place, part, ((1,), (0,))).astype(bf16)


def token_kernel(steps, spread, d_gate_ref, d_up_ref, slot_ref, route_ref, gate_ref, up_ref, *outs):
    step = pl.program_id(0)

    def store(part):
        if spread:
            spread_rows(slot_ref, part, outs)
        else:
            outs[0][...] = part

    @pl.when(step < steps)
    def _():
        part = dot(d_gate_ref[...], gate_ref[...], ((1,), (1,)))
        store((part + dot(d_up_ref[...], up_ref[...], ((1,), (1,)))).astype(bf16))

    if spread:

        @pl.when(step >= steps)
        def _():
            store(route_ref[...])


def token_grad(d_gate, d_up, slot, route, w_gate, w_up, chunk, chunks, spread):
    rows, units = d_gate.shape
    width = w_gate.shape[0] // chunks
    total = slot.shape[0]
    block = tile(width, 512)
    steps = width // block
    first = chunk * steps
    extra = route.shape[1] if spread and chunk == chunks - 1 else 0
    weight = pl.BlockSpec((block, units), lambda i: (first + jnp.minimum(i, steps - 1), 0))
    out_rows = [total // 2] * 2 if spread else [rows]
    return call(
        functools.partial(token_kernel, steps, spread),
        4 * rows * width * units + 2 * rows * width * total * spread,
        4 * width * units + 2 * total * width,
        grid=(steps + (extra > 0),),
        in_specs=[whole(rows, units), whole(rows, units), whole(total, 1), whole(*route.shape), weight, weight],
        out_specs=[pl.BlockSpec((n, block), lambda i: (0, i)) for n in out_rows],
        out_shape=[jax.ShapeDtypeStruct((n, width + extra), bf16) for n in out_rows],
    )(d_gate, d_up, slot.reshape(total, 1), route, w_gate, w_up)


def down_kernel(count, g_ref, gain_ref, *refs):
    turned, out_ref = refs[:count], refs[-1]
    scaled = (gain_ref[...] * g_ref[...].astype(f32)).astype(bf16)
    at = 0
    for ref in turned:
        out_ref[at : at + ref.shape[0], :] = dot(ref[...], scaled, ((1,), (0,))).astype(bf16)
        at += ref.shape[0]


def down_grad(turned, g, gain, chunk, chunks, into):
    rows, width = g.shape
    units = sum(part.shape[0] for part in turned)
    block = tile(width // chunks, 512)
    steps = width // chunks // block
    first = chunk * steps
    kept = [] if into is None else [into]
    return call(
        functools.partial(down_kernel, len(turned)),
        2 * rows * width * units // chunks,
        2 * width * units // chunks,
        grid=(steps,),
        in_specs=[pl.BlockSpec((rows, block), lambda i: (0, first + i)), whole(rows, 1)]
        + [whole(*part.shape) for part in turned]
        + [pl.BlockSpec(memory_space=pl.ANY)] * len(kept),
        out_specs=pl.BlockSpec((units, block), lambda i: (0, first + i)),
        out_shape=jax.ShapeDtypeStruct((units, width), bf16),
        input_output_aliases={2 + len(turned): 0} if kept else {},
    )(g, gain, *turned, *kept)


def body(tokens, grad_out, expert_ids, route_weights, w_gate, w_up, w_down):
    wide_count = lax.axis_size("wide")
    narrow_count = lax.axis_size("narrow")
    local_experts = w_gate.shape[0]
    experts_all = local_experts * wide_count
    tok_count, top_count = expert_ids.shape
    capacity = min(tok_count, 2 * tok_count * top_count // experts_all)
    rows = wide_count * capacity
    total = wide_count * tok_count
    cols = tokens.shape[1]
    me = lax.axis_index("wide")
    pad = -2 * top_count % LANES
    meta = jnp.concatenate(
        [expert_ids.astype(bf16), route_weights, jnp.zeros((tok_count, pad), bf16)], axis=1
    )
    first_t = gather_z(jnp.concatenate([tokens, meta], axis=1))
    x_t, y_t = gather_sides(first_t)
    first_g = gather_z(after(grad_out, first_t))
    far_t = gather_far(x_t, y_t)
    x_g, y_g = gather_sides(after(first_g, *far_t))
    pieces_t = gather_core([first_t, x_t, y_t] + far_t)
    all_meta = gather_meta(pieces_t, cols)
    all_ids = all_meta[:, :top_count].astype(jnp.int32)
    all_weights = all_meta[:, top_count : 2 * top_count].astype(f32)
    first = me * local_experts
    fused = narrow_count == 1 and local_experts == 1 and experts_all <= LANES
    chunks = CHUNKS if fused else 1
    units = w_gate.shape[2]
    ahead_units = units * 2 // 3 if fused and units % (6 * LANES) == 0 else units
    picked = []
    for j in range(local_experts):
        match = all_ids == first + j
        chosen = jnp.any(match, axis=1)
        gain = jnp.sum(jnp.where(match, all_weights, 0.0), axis=1)
        rank = jnp.cumsum(chosen.astype(jnp.int32)) - 1
        slot = jnp.where(chosen, rank, -1)
        place = slot[None, :] == jnp.arange(rows, dtype=jnp.int32)[:, None]
        row_gain = jnp.sum(jnp.where(place, gain[None, :], 0.0), axis=1, keepdims=True)
        if fused:
            x, first_part = pick_forward(slot, pieces_t, rows, w_gate[j], w_up[j], ahead_units)
        else:
            x = pick_rows(slot, pieces_t, rows, cols)
            x = lax.all_gather(x, "narrow", axis=1, tiled=True)
            first_part = forward(x, w_gate[j], w_up[j], 0, ahead_units)
        ahead = [first_part]
        picked.append((slot, place, row_gain, x, ahead))
    x_g, y_g, *_ = lax.optimization_barrier((x_g, y_g, *[ahead[0][0] for *_, ahead in picked]))
    far_g = gather_far(x_g, y_g)
    for j in range(local_experts):
        slot, place, row_gain, x, ahead = picked[j]
        if ahead_units < units:
            ahead.append(forward(after(x, x_g, y_g), w_gate[j], w_up[j], ahead_units, units))
    far_g = lax.optimization_barrier((*far_g, *[ahead[-1][0] for *_, ahead in picked]))[: len(far_g)]
    pieces_g = gather_core([first_g, x_g, y_g, *far_g])
    expert_cols = experts_all + -experts_all % LANES
    dense = [0, 0]
    route_all = 0
    ends = []
    for j in range(local_experts):
        slot, place, row_gain, x, ahead = picked[j]
        straight = [(hidden, active, pull) for hidden, _, active, pull in ahead]
        if fused:
            g, _, *dense = pick_back(
                slot, pieces_g, row_gain, first + j, w_down[j], w_gate[j], w_up[j], straight
            )
            ends.append(([part[1] for part in ahead], g, row_gain))
            continue
        g = pick_rows(slot, pieces_g, rows, cols)
        g = lax.all_gather(g, "narrow", axis=1, tiled=True)
        d_gate, d_up, route = back_project(g, row_gain, w_down[j], straight)
        route = lax.psum(route.astype(bf16).astype(f32), "narrow")
        at = jnp.arange(expert_cols, dtype=jnp.int32) == first + j
        route = jnp.where(at[None, :], route, 0.0).astype(bf16)
        ends.append(([part[1] for part in ahead], g, row_gain))
        (part,) = token_grad(d_gate, d_up, slot, route, w_gate[j], w_up[j], 0, 1, False)
        part = lax.psum_scatter(part, "narrow", scatter_dimension=1, tiled=True)
        part = jnp.concatenate([part, route], axis=1)
        part = dot(place.astype(bf16), part, ((0,), (0,)))
        dense = [dense[0] + part[: total // 2], dense[1] + part[total // 2 :]]
    grad_downs = []
    if fused:
        (turned, g, row_gain), = ends
        out = down_grad(turned, g, row_gain, 0, 4, None)
        dense[0], out = lax.optimization_barrier((dense[0], out))
        mine = [add(dense[0], flip(dense[1], CORE))]
        mine.append(add(after(dense[2], mine[0]), flip(dense[3], CORE)))
        out = down_grad(turned, after(g, mine[1]), row_gain, 1, 4, out)
        sides = [scatter_far(rows_) for rows_ in mine]
        sides[1] = lax.optimization_barrier((*sides[1], sides[0][1], sides[0][2]))[:3]
        sent = [send_sides(*side) for side in sides]
        out = down_grad(turned, after(g, sides[1][1]), row_gain, 2, 4, out)
        *sent[0], out = lax.optimization_barrier((*sent[0], out))
        firsts = [add(*sent[0])]
        shares = [send_z(firsts[0])]
        sent[1] = lax.optimization_barrier((*sent[1], shares[0][1]))[:3]
        firsts.append(add(*sent[1]))
        shares.append(send_z(firsts[1]))
        out = down_grad(turned, after(g, firsts[1]), row_gain, 3, 4, out)
        *shares[0], out = lax.optimization_barrier((*shares[0], out))
        shares = [add(*share) for share in shares]
        grad_downs.append(out)
    else:
        mine = add(dense[0].astype(bf16), flip(dense[1].astype(bf16), CORE))
        shares = [add(*send_z(add(*send_sides(*scatter_far(mine)))))]
        grad_downs += [down_grad(*end, 0, 1, None) for end in ends]
    joined = jnp.concatenate(shares, axis=1)
    width = tokens.shape[1]
    by_expert = joined[:, width : width + experts_all].astype(f32)
    pick = expert_ids[:, :, None] == jnp.arange(experts_all, dtype=jnp.int32)[None, None, :]
    grad_route = jnp.sum(jnp.where(pick, by_expert[:, None, :], 0.0), axis=2)
    return (joined[:, :width], grad_route.astype(bf16), jnp.stack(grad_downs))


def solution(mesh):
    in_specs = (
        P("wide", "narrow"),
        P("wide", "narrow"),
        P("wide", None),
        P("wide", None),
        P("wide", None, "narrow"),
        P("wide", None, "narrow"),
        P("wide", "narrow", None),
    )
    out_specs = (P("wide", "narrow"), P("wide", None), P("wide", "narrow", None))
    return jax.shard_map(body, mesh=mesh, in_specs=in_specs, out_specs=out_specs, check_vma=False)
```
